256 devices in a mesh: tm: 16 (over z_hi, x, core), sx: 4 (over y), sy: 4 (over z_lo).
Axes of the slice: x: 4, y: 4, z: 8 (z_hi: 2, z_lo: 4; z = z_hi * 4 + z_lo), core: 2. Of those that a mesh axis runs over, the one named last changes fastest.
Arguments:
- depth_start: float32 [16, 256, 4096], P('tm', 'sx', 'sy'), may hold values from 0 to 0.3
- flux_start: float32 [16, 2, 256, 4096], P('tm', None, 'sx', 'sy'), may hold values from -0.45 to 0.45
- elevation: float32 [256, 4096], P('sx', 'sy'), may hold values from 0 to 0.3
- roughness_class: int32 [256, 4096], P('sx', 'sy'), may hold values from 0 to 7
- building: int32 [256, 4096], P('sx', 'sy'), may hold values 0 or 1
- manning: float32 [8], replicated, may hold values from 0.03 to 0.3
- radar_rates: float32 [64], replicated, may hold values from 1e-05 to 0.0005
- tile_index: int32 [16, 8, 4, 64], P('tm'), may hold values from 0 to 63
Outputs:
- depth_end: float32 [16, 256, 4096], P('tm', 'sx', 'sy')
- flux_end: float32 [16, 2, 256, 4096], P('tm', None, 'sx', 'sy')
The draws below stay inside these ranges and needn't reach their ends.
All inputs are finite; a program needn't handle non-finite values. No bound on the sum of `building` on one device may be relied on, other than what follows from the above.
Results may differ from the reference program's by a relative error of at most 0.00002.
Values sent between devices are 32-bit elements; how exact they have to be, the bound alone decides.
No kernel may reach another device: no remote copies, remote signals or barrier semaphores. Data moves between devices by JAX's collectives and lax.ppermute only.
A program may use at most 128 MiB of HBM per device.

```python
import math
import jax
import jax.numpy as jnp
from jax import lax

FINE_STEPS = 8
COARSE_STEPS = 2
COARSENING = 4
RAIN_BLOCK = 64
RADAR_TILES = 64
ROUGH_CLASSES = 8
SLICES = 16
GRID_X = 256
GRID_Y = 4096
BLOCKS_X = 4
BLOCKS_Y = 64


def water_depths(key, exponent):
    wet = jax.random.bernoulli(jax.random.fold_in(key, 11), 2.0 / 3.0, (SLICES, GRID_X, GRID_Y))
    level = jax.random.uniform(jax.random.fold_in(key, 12), (SLICES, GRID_X, GRID_Y), jnp.float32)
    return 0.3 * jnp.power(level, exponent) * wet.astype(jnp.float32)


def draw_depth_start(key, part):
    depth = water_depths(key, 1.0)
    return depth


def draw_flux_start(key, part):
    depth = water_depths(key, 1.0)
    key = jax.random.fold_in(key, 3)
    velocity = jnp.clip(0.5 * jax.random.normal(key, (SLICES, 2, GRID_X, GRID_Y), jnp.float32), -1.5, 1.5)
    east_depth = jnp.minimum(depth, jnp.pad(depth, ((0, 0), (0, 1), (0, 0)))[:, 1:, :])
    north_depth = jnp.minimum(depth, jnp.pad(depth, ((0, 0), (0, 0), (0, 1)))[:, :, 1:])
    return velocity * jnp.stack([east_depth, north_depth], axis=1)


def with_ends(values, stream_key, smallest, top_value):
    longest = values.shape.index(max(values.shape))
    spots = []
    for shift in (0, 1):
        where = [jax.random.randint(jax.random.fold_in(stream_key, axis), (), 0, length) for axis, length in enumerate(values.shape)]
        where[longest] = (where[longest] + shift) % values.shape[longest]
        spots.append(tuple(where))
    return values.at[spots[0]].set(smallest).at[spots[1]].set(top_value)


def block_scale(own_key, extent, shards, smallest, high):
    def one(dim, shards_of):
        steps = jax.random.uniform(jax.random.fold_in(jax.random.fold_in(own_key, 6), dim), (shards_of,), jnp.float32, smallest / len(shards), high / len(shards))
        return jnp.repeat(jnp.exp(steps), extent[dim] // shards_of).reshape((-1,) + (1,) * (len(extent) - dim - 1))

    gain = one(*shards[0])
    for cut in shards[1:]:
        gain = gain * one(*cut)
    return gain


def setup_inputs(seed: int = 0) -> dict:
    splits = jax.random.split(jax.random.key(seed), 9)
    return {
        "depth_start": draw_depth_start(jax.random.fold_in(splits[8], 71), 0),
        "flux_start": draw_flux_start(jax.random.fold_in(splits[8], 71), 0),
        "elevation": jnp.clip(0.3 * jax.random.uniform(splits[2], (GRID_X, GRID_Y), jnp.float32) ** block_scale(splits[2], (GRID_X, GRID_Y), ((0, 4), (1, 4)), -0.2, 0.2), 0.0, 0.3),
        "roughness_class": with_ends(jax.random.randint(splits[3], (GRID_X, GRID_Y), 0, ROUGH_CLASSES), jax.random.fold_in(splits[3], 1), 0, ROUGH_CLASSES - 1).astype(jnp.int32),
        "building": with_ends((jax.random.randint(splits[4], (GRID_X, GRID_Y), 0, 8) < 1).astype(jnp.int32), jax.random.fold_in(splits[4], 1), 0, 1),
        "manning": jnp.clip(jnp.exp(jax.random.uniform(splits[5], (ROUGH_CLASSES,), jnp.float32, math.log(0.03), math.log(0.3))), 0.03, 0.3),
        "radar_rates": jnp.clip(jnp.exp(jax.random.uniform(splits[6], (RADAR_TILES,), jnp.float32, math.log(9.999999747378752e-06), math.log(0.0005))), 9.999999747378752e-06, 0.0005),
        "tile_index": with_ends(jax.random.randint(splits[7], (SLICES, FINE_STEPS, BLOCKS_X, BLOCKS_Y), 0, RADAR_TILES), jax.random.fold_in(splits[7], 1), 0, RADAR_TILES - 1).astype(jnp.int32),
    }


GRAVITY = 9.81
DEPTH_FLOOR = 0.05
CELL_SIDE = 2.0
TIME_STEP = 0.25
SEVEN_THIRDS = 7.0 / 3.0


def face_flux(flux_in, level_a, level_b, ground_a, ground_b, rough_a, rough_b, open_a, open_b, spacing, seconds):
    flow_depth = jnp.maximum(jnp.maximum(level_a, level_b) - jnp.maximum(ground_a, ground_b), 0.0)
    surface_slope = (level_b - level_a) / spacing
    face_rough = 0.5 * (rough_a + rough_b)
    depth_power = jnp.exp(SEVEN_THIRDS * jnp.log(jnp.maximum(flow_depth, DEPTH_FLOOR)))
    return open_a * open_b * (flux_in - GRAVITY * seconds * flow_depth * surface_slope) / (1.0 + GRAVITY * seconds * face_rough * face_rough * jnp.abs(flux_in) / depth_power)


def advance(fields, ground, rainfall, spacing, seconds):
    surface = ground[0] + fields[0]
    heights, frictions, openness = ground[0], ground[1], ground[2]
    east_flux = face_flux(fields[1][:-1, :], surface[:-1, :], surface[1:, :], heights[:-1, :], heights[1:, :], frictions[:-1, :], frictions[1:, :], openness[:-1, :], openness[1:, :], spacing, seconds)
    north_flux = face_flux(fields[2][:, :-1], surface[:, :-1], surface[:, 1:], heights[:, :-1], heights[:, 1:], frictions[:, :-1], frictions[:, 1:], openness[:, :-1], openness[:, 1:], spacing, seconds)
    inflow = (east_flux[:-1, 1:-1] - east_flux[1:, 1:-1]) + (north_flux[1:-1, :-1] - north_flux[1:-1, 1:])
    new_depth = fields[0][1:-1, 1:-1] + seconds * (inflow / spacing + rainfall)
    return jnp.stack([new_depth, east_flux[1:, 1:-1], north_flux[1:-1, 1:]])


def restrict(fields):
    return fields.reshape(fields.shape[0], fields.shape[1] // COARSENING, COARSENING, fields.shape[2] // COARSENING, COARSENING).mean(axis=(2, 4))


def spread(blocks, factor):
    return jnp.repeat(jnp.repeat(blocks, factor, axis=-2), factor, axis=-1)


def pad_cells(fields):
    return jnp.pad(fields, ((0, 0), (1, 1), (1, 1)))


def reference(depth_start, flux_start, elevation, roughness_class, building, manning, radar_rates, tile_index):
    open_cells = 1.0 - building.astype(jnp.float32)
    friction = manning[roughness_class]
    ground = jnp.stack([elevation, friction, open_cells])
    ground_pad = pad_cells(ground)
    coarse_pad = pad_cells(restrict(ground))
    coarse_seconds = TIME_STEP * FINE_STEPS / COARSE_STEPS
    tile_rates = radar_rates[tile_index]
    coarse_rates = tile_rates.reshape(tile_rates.shape[0], COARSE_STEPS, FINE_STEPS // COARSE_STEPS, tile_rates.shape[2], tile_rates.shape[3]).mean(axis=2)

    def fine_slice(inputs):
        depth_one, flux_one, rate_one = inputs
        fields = jnp.concatenate([depth_one[None], flux_one], axis=0)
        for moment in range(FINE_STEPS):
            fields = advance(pad_cells(fields), ground_pad, spread(rate_one[moment], RAIN_BLOCK), CELL_SIDE, TIME_STEP)
        return fields

    fine_all = lax.map(fine_slice, (depth_start, flux_start, tile_rates))

    def coarse_run(fields, rain_now):
        for moment in range(COARSE_STEPS):
            fields = advance(pad_cells(fields), coarse_pad, rain_now[moment], CELL_SIDE * COARSENING, coarse_seconds)
        return fields

    def coarse_slice(inputs):
        depth_one, flux_one, rate_one = inputs
        start_coarse = restrict(jnp.concatenate([depth_one[None], flux_one], axis=0))
        rain_coarse = spread(rate_one, RAIN_BLOCK // COARSENING)
        return start_coarse, coarse_run(start_coarse, rain_coarse), rain_coarse

    start_all, old_all, rain_all = lax.map(coarse_slice, (depth_start, flux_start, coarse_rates))
    corrections_all = lax.map(restrict, fine_all) - old_all

    def link_step(current, inputs):
        correction, rain_now = inputs
        advanced = coarse_run(current, rain_now)
        return advanced + correction, advanced

    _, newest = lax.scan(link_step, start_all[0], (corrections_all, rain_all))
    result = fine_all + spread(newest - old_all, COARSENING)
    return result[:, 0], result[:, 1:]
```

```python
import math

import jax
import jax.numpy as jnp
from jax import lax
from jax.experimental import pallas as pl
from jax.experimental.pallas import tpu as pltpu
from jax.sharding import PartitionSpec as P

FINE_STEPS = 8
COARSE_STEPS = 2
COARSENING = 4
RAIN_BLOCK = 64
RADAR_TILES = 64
ROUGH_CLASSES = 8
SLICES = 16

GRAVITY = 9.81
DEPTH_FLOOR = 0.05
CELL_SIDE = 2.0
TIME_STEP = 0.25
COARSE_SECONDS = TIME_STEP * FINE_STEPS / COARSE_STEPS
COARSE_SIDE = CELL_SIDE * COARSENING
POWER = -7.0 / 3.0 / math.log(2.0)

ROWS, COLS = 64, 1024
EDGE = 128
HALO = 8
HIGH, WIDE = ROWS + 2 * HALO, COLS + 2 * EDGE
C_ROWS, C_COLS = ROWS // COARSENING, COLS // COARSENING
C_HIGH, C_WIDE = 32, 384
BLOCK = 3 * C_ROWS + 8
F32 = jnp.float32
BF16 = jnp.bfloat16
VMEM_LIMIT = 40 * 1024 * 1024


def face(level, level_next, flux, sill, drag, gate, pull):
    depth = jnp.maximum(jnp.maximum(level, level_next) - sill, 0.0)
    power = jnp.exp2(POWER * jnp.log(jnp.maximum(depth, DEPTH_FLOOR)))
    below = 1.0 + drag * jnp.abs(flux) * power
    inverse = pl.reciprocal(below, approx=True)
    inverse = inverse * (2.0 - below * inverse)
    return gate * inverse * (flux - pull * (level_next - level) * depth)


def split_dot(values, weights):
    first = values.astype(BF16)
    rest = values - first.astype(F32)
    second = rest.astype(BF16)
    third = (rest - second.astype(F32)).astype(BF16)
    dot = lambda part: jnp.dot(part, weights, preferred_element_type=F32)
    return dot(third) + dot(second) + dot(first)


def turn(values, shift, axis):
    return pltpu.roll(values, shift % values.shape[axis], axis)


def static_faces(elev, friction, opened, axis, seconds):
    sill = jnp.maximum(elev, turn(elev, -1, axis))
    rough = 0.5 * (friction + turn(friction, -1, axis))
    gate = opened * turn(opened, -1, axis)
    return sill, GRAVITY * seconds * rough * rough, gate


def whole_step(level, flux_x, flux_y, faces_x, faces_y, rain, side, seconds):
    pull = GRAVITY * seconds / side
    flux_x = face(level, turn(level, -1, 0), flux_x, *faces_x, pull)
    flux_y = face(level, turn(level, -1, 1), flux_y, *faces_y, pull)
    gain = (turn(flux_x, 1, 0) - flux_x) + (turn(flux_y, 1, 1) - flux_y)
    return level + (seconds / side) * gain + seconds * rain, flux_x, flux_y


def columns_kernel(*refs):
    ins, outs = refs[:10], refs[10:]
    even = lax.axis_index("sy") % 2 == 0

    def put(index, left, right):
        outs[0][pl.ds(index * ROWS, ROWS), :] = jnp.where(even, right, left)
        outs[1][pl.ds(index * ROWS, ROWS), :] = jnp.where(even, left, right)

    dl, dr, fl, fr, el, er, rl, rr, bl, br = ins
    put(0, dl[0], dr[0])
    put(1, fl[0, 0], fr[0, 0])
    put(2, fl[0, 1], fr[0, 1])
    put(3, el[...], er[...])
    put(4, rl[...].astype(F32), rr[...].astype(F32))
    put(5, bl[...].astype(F32), br[...].astype(F32))


def pack_columns(depth, flux, elevation, roughness, building):
    last = COLS // EDGE - 1
    specs, args = [], []
    for array, shape in (
        (depth, (1, ROWS, EDGE)),
        (flux, (1, 2, ROWS, EDGE)),
        (elevation, (ROWS, EDGE)),
        (roughness, (ROWS, EDGE)),
        (building, (ROWS, EDGE)),
    ):
        for place in (0, last):
            zeros = (0,) * (len(shape) - 1)
            specs.append(pl.BlockSpec(shape, lambda i, zeros=zeros, place=place: zeros + (place,)))
            args.append(array)
    out = jax.ShapeDtypeStruct((6 * ROWS, EDGE), F32)
    whole = pl.BlockSpec((6 * ROWS, EDGE), lambda i: (0, 0))
    return pl.pallas_call(
        columns_kernel, grid=(1,), in_specs=specs, out_specs=(whole, whole), out_shape=(out, out)
    )(*args)


def rows_kernel(*refs):
    ins, first, second, outs = refs[:10], refs[10], refs[11], refs[12:]
    even = lax.axis_index("sy") % 2 == 0
    dt, db, ft, fb, et, eb, rt, rb, bt, bb = ins
    fields = (
        (dt[0], db[0]),
        (ft[0, 0], fb[0, 0]),
        (ft[0, 1], fb[0, 1]),
        (et[...], eb[...]),
        (rt[...].astype(F32), rb[...].astype(F32)),
        (bt[...].astype(F32), bb[...].astype(F32)),
    )
    for index, pair in enumerate(fields):
        for side, values in enumerate(pair):
            row = index * ROWS + side * (ROWS - HALO)
            a = first[pl.ds(row, HALO), :]
            b = second[pl.ds(row, HALO), :]
            here = pl.ds(index * HALO, HALO)
            outs[side][here, 0:EDGE] = jnp.where(even, b, a)
            outs[side][here, EDGE : EDGE + COLS] = values
            outs[side][here, EDGE + COLS : WIDE] = jnp.where(even, a, b)


def pack_rows(depth, flux, elevation, roughness, building, first, second):
    last = ROWS // HALO - 1
    specs, args = [], []
    for array, shape in (
        (depth, (1, HALO, COLS)),
        (flux, (1, 2, HALO, COLS)),
        (elevation, (HALO, COLS)),
        (roughness, (HALO, COLS)),
        (building, (HALO, COLS)),
    ):
        for place in (0, last):
            zeros = (0,) * (len(shape) - 2)
            specs.append(pl.BlockSpec(shape, lambda i, zeros=zeros, place=place: zeros + (place, 0)))
            args.append(array)
    for array in (first, second):
        specs.append(pl.BlockSpec((6 * ROWS, EDGE), lambda i: (0, 0)))
        args.append(array)
    out = jax.ShapeDtypeStruct((6 * HALO, WIDE), F32)
    whole = pl.BlockSpec((6 * HALO, WIDE), lambda i: (0, 0))
    return pl.pallas_call(
        rows_kernel, grid=(1,), in_specs=specs, out_specs=(whole, whole), out_shape=(out, out)
    )(*args)


def fine_kernel(
    manning, radar, depth, flux, elevation, roughness, building, tiles, first, second, above, below,
    depth_out, flux_out, old_out, to0, to1, to2, to3, ground_out,
    level, flow_x, flow_y, elev, friction, opened,
    sill_x, drag_x, gate_x, sill_y, drag_y, gate_y,
    index_s, rain_s, pooled, coarse,
):
    row_place = lax.axis_index("sx")
    col_place = lax.axis_index("sy")
    time_place = lax.axis_index("tm")
    x_place = (time_place // 2) % 4
    even = col_place % 2 == 0

    def fill(target, index, own):
        target[0:8, :] = jnp.zeros((8, WIDE), F32)
        target[88:96, :] = jnp.zeros((8, WIDE), F32)
        a = first[pl.ds(index * ROWS, ROWS), :]
        b = second[pl.ds(index * ROWS, ROWS), :]
        target[16:80, 0:EDGE] = jnp.where(even, b, a)
        target[16:80, EDGE : EDGE + COLS] = own
        target[16:80, EDGE + COLS : WIDE] = jnp.where(even, a, b)
        target[8:16, :] = above[pl.ds(index * HALO, HALO), :]
        target[80:88, :] = below[pl.ds(index * HALO, HALO), :]

    fill(level, 0, depth[0])
    fill(flow_x, 1, flux[0, 0])
    fill(flow_y, 2, flux[0, 1])
    fill(elev, 3, elevation[...])
    fill(friction, 4, roughness[...].astype(F32))
    fill(opened, 5, building[...].astype(F32))

    lane = lax.broadcasted_iota(jnp.int32, (8, WIDE), 1)
    inside = jnp.where(
        ((col_place == 0) & (lane < EDGE)) | ((col_place == 3) & (lane >= EDGE + COLS)), 0.0, 1.0
    )
    for k in range(12):
        here = pl.ds(8 * k, 8)
        classes = friction[here, :]
        value = jnp.full((8, WIDE), manning[0], F32)
        for entry in range(1, ROUGH_CLASSES):
            value = jnp.where(classes == float(entry), manning[entry], value)
        friction[here, :] = value
        if k in (0, 11):
            opened[here, :] = jnp.zeros((8, WIDE), F32)
            continue
        free = (1.0 - opened[here, :]) * inside
        if k == 1:
            free = free * jnp.where(row_place == 0, 0.0, 1.0)
        if k == 10:
            free = free * jnp.where(row_place == 3, 0.0, 1.0)
        opened[here, :] = free

    for k in range(10):
        rows, after, out = pl.ds(8 + 8 * k, 8), pl.ds(9 + 8 * k, 8), pl.ds(8 * k, 8)
        e, f, o = elev[rows, :], friction[rows, :], opened[rows, :]
        sill_x[out, :] = jnp.maximum(e, elev[after, :])
        rough = 0.5 * (f + friction[after, :])
        drag_x[out, :] = GRAVITY * TIME_STEP * rough * rough
        gate_x[out, :] = o * opened[after, :]
        s, d, g = static_faces(e, f, o, 1, TIME_STEP)
        sill_y[out, :], drag_y[out, :], gate_y[out, :] = s, d, g

    index_s[...] = jnp.full((32, 128), -1, jnp.int32)
    for step in range(FINE_STEPS):
        index_s[4 * step : 4 * step + 4, 0:64] = tiles[0, step]
    index = index_s[...]
    rates = jnp.zeros((32, 128), F32)
    for entry in range(RADAR_TILES):
        rates = jnp.where(index == entry, radar[entry], rates)
    block = lax.broadcasted_iota(jnp.int32, (128, WIDE), 0)
    column = lax.broadcasted_iota(jnp.int32, (128, WIDE), 1) + (COLS * col_place - EDGE)
    rain_s[0:32, :] = TIME_STEP * split_dot(rates, jnp.where((column >> 6) == block, 1.0, 0.0).astype(BF16))
    means = []
    for half in range(COARSE_STEPS):
        part = rates[16 * half : 16 * half + 16, :]
        means.append(0.25 * (part[0:4] + part[4:8] + part[8:12] + part[12:16]))
    coarse_rates = jnp.concatenate(means, axis=0)
    block = lax.broadcasted_iota(jnp.int32, (128, C_WIDE), 0)
    column = lax.broadcasted_iota(jnp.int32, (128, C_WIDE), 1) + (C_COLS * col_place - EDGE // COARSENING)
    padded = jnp.concatenate([coarse_rates, jnp.zeros((8, 128), F32)], axis=0)
    rain_s[32:40, 0:C_WIDE] = split_dot(
        padded, jnp.where((column >> 4) == block, 1.0, 0.0).astype(BF16)
    )[0:8]
    row_above = jnp.maximum(row_place - 1, 0)
    row_below = jnp.minimum(row_place + 1, 3)

    pool = jnp.where(
        lax.broadcasted_iota(jnp.int32, (512, 128), 0) // COARSENING
        == lax.broadcasted_iota(jnp.int32, (512, 128), 1),
        1.0 / 16.0,
        0.0,
    ).astype(BF16)

    def restrict(source, slot):
        values = source if isinstance(source, jax.Array) else source[8:88, :]
        for part in range(3):
            take = values[:, 512 * part : min(512 * part + 512, WIDE)]
            pooled[part, :, :] = split_dot(take, pool[0 : take.shape[1], :])
        for part in range(3):
            cols = slice(128 * part, 128 * part + 128)
            for target, start, count in ((6, 0, 2), (8, 8, 16), (24, 72, 2)):
                total = pooled[part, pl.ds(start, count, stride=4), :]
                for q in range(1, 4):
                    total = total + pooled[part, pl.ds(start + q, count, stride=4), :]
                coarse[slot, target : target + count, cols] = total

    coarse[...] = jnp.zeros(coarse.shape, F32)
    for slot, source in enumerate((level, flow_x, flow_y, elev, friction, opened)):
        restrict(source, slot)

    for k in range(12):
        here = pl.ds(8 * k, 8)
        level[here, :] = level[here, :] + elev[here, :]
    sub = lax.broadcasted_iota(jnp.int32, (8, WIDE), 0)
    pull = GRAVITY * TIME_STEP / CELL_SIDE

    def fine_step(step, carry):
        rains = [rain_s[pl.ds(4 * step + place, 1), :] for place in (row_above, row_place, row_below)]
        now = level[8:16, :]
        up = turn(now, -1, 0)
        west = jnp.zeros((8, WIDE), F32)
        for k in range(10):
            rows, out = pl.ds(8 + 8 * k, 8), pl.ds(8 * k, 8)
            after = level[pl.ds(16 + 8 * k, 8), :]
            up_after = turn(after, -1, 0)
            north = jnp.where(sub == 7, up_after, up)
            qx = face(now, north, flow_x[rows, :], sill_x[out, :], drag_x[out, :], gate_x[out, :], pull)
            qy = face(
                now, turn(now, -1, 1), flow_y[rows, :], sill_y[out, :], drag_y[out, :], gate_y[out, :], pull
            )
            flow_x[rows, :] = qx
            flow_y[rows, :] = qy
            down = turn(qx, 1, 0)
            gain = (jnp.where(sub == 0, west, down) - qx) + (turn(qy, 1, 1) - qy)
            rain = rains[0 if k == 0 else 2 if k == 9 else 1]
            level[rows, :] = now + ((TIME_STEP / CELL_SIDE) * gain + rain)
            now, up, west = after, up_after, down
        return carry

    lax.fori_loop(0, FINE_STEPS, fine_step, 0)

    c_elev, c_friction, c_open = coarse[3], coarse[4], coarse[5]
    faces_x = static_faces(c_elev, c_friction, c_open, 0, COARSE_SECONDS)
    faces_y = static_faces(c_elev, c_friction, c_open, 1, COARSE_SECONDS)
    state = (coarse[0] + c_elev, coarse[1], coarse[2])
    row = lax.broadcasted_iota(jnp.int32, (C_HIGH, C_WIDE), 0)
    for step in range(COARSE_STEPS):
        parts = [rain_s[pl.ds(32 + 4 * step + place, 1), 0:C_WIDE] for place in (row_above, row_place, row_below)]
        rain = jnp.where(row < 8, parts[0], jnp.where(row < 24, parts[1], parts[2]))
        state = whole_step(*state, faces_x, faces_y, rain, COARSE_SIDE, COARSE_SECONDS)
    old = (state[0] - c_elev, state[1], state[2])

    for k in range(10):
        rows = pl.ds(8 + 8 * k, 8)
        level[rows, :] = level[rows, :] - elev[rows, :]
    depth_out[0] = level[16:80, EDGE : EDGE + COLS]
    flux_out[0, 0] = flow_x[16:80, EDGE : EDGE + COLS]
    flux_out[0, 1] = flow_y[16:80, EDGE : EDGE + COLS]
    for slot, source in enumerate((level, flow_x, flow_y)):
        restrict(source, slot)
    factor = jnp.where(time_place == 0, 0.0, 1.0)
    side = EDGE // COARSENING
    outs = (to0, to1, to2, to3)
    for slot in range(3):
        mine = old[slot][8:24, :]
        old_out[C_ROWS * slot : C_ROWS * slot + C_ROWS, :] = turn(mine, -side, 1)[:, 0:C_COLS]
        value = coarse[slot, 8:24, :] - factor * mine
        for d, out in enumerate(outs):
            window = (x_place + d) % 4
            moved = pltpu.roll(value, (C_WIDE - 64 * window) % C_WIDE, 1)
            out[C_ROWS * slot : C_ROWS * slot + C_ROWS, :] = moved[:, 0:128]
        fixed = pltpu.roll(coarse[3 + slot, 8:24, :], (C_WIDE - 64 * x_place) % C_WIDE, 1)
        ground_out[C_ROWS * slot : C_ROWS * slot + C_ROWS, :] = fixed[:, 0:128]
    for out in outs:
        out[3 * C_ROWS : BLOCK, :] = coarse_rates


def fine(manning, radar, depth, flux, elevation, roughness, building, tiles, first, second, above, below):
    smem = pl.BlockSpec(memory_space=pltpu.SMEM)
    vmem = pl.BlockSpec(memory_space=pltpu.VMEM)
    message = jax.ShapeDtypeStruct((BLOCK, 128), F32)
    padded = pltpu.VMEM((HIGH + 16, WIDE), F32)
    faces = pltpu.VMEM((HIGH, WIDE), F32)
    return pl.pallas_call(
        fine_kernel,
        in_specs=[smem, smem] + [vmem] * 10,
        out_specs=[vmem] * 8,
        out_shape=(
            jax.ShapeDtypeStruct(depth.shape, F32),
            jax.ShapeDtypeStruct(flux.shape, F32),
            jax.ShapeDtypeStruct((3 * C_ROWS, C_COLS), F32),
            message,
            message,
            message,
            message,
            jax.ShapeDtypeStruct((3 * C_ROWS, 128), F32),
        ),
        scratch_shapes=[padded] * 6
        + [faces] * 6
        + [
            pltpu.VMEM((32, 128), jnp.int32),
            pltpu.VMEM((40, WIDE), F32),
            pltpu.VMEM((3, HIGH, 128), F32),
            pltpu.VMEM((6, C_HIGH, C_WIDE), F32),
        ],
        compiler_params=pltpu.CompilerParams(vmem_limit_bytes=VMEM_LIMIT),
    )(manning, radar, depth, flux, elevation, roughness, building, tiles, first, second, above, below)


def sweep_kernel(*refs):
    ins, outs = refs[:8], refs[8:12]
    change, rates, rain, ground, newest = refs[12:]
    row_place = lax.axis_index("sx")
    col_place = lax.axis_index("sy")
    time_place = lax.axis_index("tm")
    z_place, x_place, core = time_place // 8, (time_place // 2) % 4, time_place % 2

    for other in range(2):
        for e in range(4):
            ref = ins[4 * other + e]
            start = pl.multiple_of(C_ROWS * ((row_place + 4 - e) % 4), C_ROWS)
            rows = pl.ds(start, C_ROWS)
            for z_rel in range(2):
                for d in range(4):
                    base = (4 * z_rel + d) * BLOCK
                    slice_of = ((z_place + z_rel) % 2) * 8 + ((x_place + 4 - d) % 4) * 2 + (core + other) % 2
                    for field in range(3):
                        change[3 * slice_of + field, rows, :] = ref[
                            base + C_ROWS * field : base + C_ROWS * field + C_ROWS, :
                        ]
                    if e == 0:
                        rates[pl.ds(pl.multiple_of(8 * slice_of, 8), 8), :] = ref[
                            base + 3 * C_ROWS : base + BLOCK, :
                        ]
            if other == 0:
                for field in range(3):
                    base = 8 * BLOCK + C_ROWS * field
                    ground[field, rows, :] = ref[base : base + C_ROWS, :]

    block = lax.broadcasted_iota(jnp.int32, (128, 128), 0)
    column = lax.broadcasted_iota(jnp.int32, (128, 128), 1)
    column = column + (C_COLS * col_place + 64 * x_place - EDGE // COARSENING)
    rain[...] = split_dot(rates[...], jnp.where((column >> 4) == block, 1.0, 0.0).astype(BF16))

    tall = 4 * C_ROWS
    elev = ground[0]
    edge = jnp.where(lax.broadcasted_iota(jnp.int32, (tall, 128), 0) == tall - 1, 0.0, 1.0)
    sill, drag, gate = static_faces(elev, ground[1], ground[2], 0, COARSE_SECONDS)
    faces_x = (sill, drag, gate * edge)
    faces_y = static_faces(elev, ground[1], ground[2], 1, COARSE_SECONDS)
    mine = pl.ds(pl.multiple_of(C_ROWS * row_place, C_ROWS), C_ROWS)

    def one_slice(moment, state):
        for step in range(COARSE_STEPS):
            wet = jnp.concatenate(
                [
                    jnp.broadcast_to(rain[pl.ds(8 * moment + 4 * step + b, 1), :], (C_ROWS, 128))
                    for b in range(4)
                ],
                axis=0,
            )
            state = whole_step(*state, faces_x, faces_y, wet, COARSE_SIDE, COARSE_SECONDS)
        for field in range(3):
            newest[3 * moment + field] = state[field]
        return tuple(state[field] + change[3 * moment + field] for field in range(3))

    lax.fori_loop(1, SLICES, one_slice, (change[0] + elev, change[1], change[2]))
    for d, out in enumerate(outs):
        slice_of = z_place * 8 + ((x_place + d) % 4) * 2 + core
        out[0:C_ROWS, :] = newest[3 * slice_of, mine, :] - ground[0, mine, :]
        out[C_ROWS : 2 * C_ROWS, :] = newest[3 * slice_of + 1, mine, :]
        out[2 * C_ROWS : 3 * C_ROWS, :] = newest[3 * slice_of + 2, mine, :]


def sweep(arrays):
    vmem = pl.BlockSpec(memory_space=pltpu.VMEM)
    out = jax.ShapeDtypeStruct((3 * C_ROWS, 128), F32)
    return pl.pallas_call(
        sweep_kernel,
        in_specs=[vmem] * 8,
        out_specs=[vmem] * 4,
        out_shape=(out,) * 4,
        scratch_shapes=[
            pltpu.VMEM((3 * SLICES, 4 * C_ROWS, 128), F32),
            pltpu.VMEM((8 * SLICES, 128), F32),
            pltpu.VMEM((8 * SLICES, 128), F32),
            pltpu.VMEM((3, 4 * C_ROWS, 128), F32),
            pltpu.VMEM((3 * SLICES, 4 * C_ROWS, 128), F32),
        ],
        compiler_params=pltpu.CompilerParams(vmem_limit_bytes=VMEM_LIMIT),
    )(*arrays)


def finish_kernel(depth, flux, old, new0, new1, new2, new3, depth_out, flux_out, parts, spread):
    time_place = lax.axis_index("tm")
    x_place = (time_place // 2) % 4
    for d, ref in enumerate((new0, new1, new2, new3)):
        parts[(x_place + 4 - d) % 4] = ref[...]
    lane = lax.broadcasted_iota(jnp.int32, (3 * C_ROWS, 128), 1)
    halves = [jnp.where(lane < 64, turn(parts[b], -32, 1), turn(parts[b + 1], 32, 1)) for b in (0, 2)]
    delta = jnp.concatenate(halves, axis=1) - old[...]
    delta = jnp.where(time_place == 0, 0.0, delta)
    copies = jnp.where(
        lax.broadcasted_iota(jnp.int32, (C_COLS, COLS), 0)
        == lax.broadcasted_iota(jnp.int32, (C_COLS, COLS), 1) // COARSENING,
        1.0,
        0.0,
    ).astype(BF16)
    spread[...] = split_dot(delta, copies)
    low = lax.broadcasted_iota(jnp.int32, (8, COLS), 0) < 4
    for field in range(3):
        for k in range(ROWS // 8):
            row = C_ROWS * field + 2 * k
            add = jnp.where(low, spread[row : row + 1, :], spread[row + 1 : row + 2, :])
            rows = slice(8 * k, 8 * k + 8)
            if field == 0:
                depth_out[0, rows, :] = depth[0, rows, :] + add
            else:
                flux_out[0, field - 1, rows, :] = flux[0, field - 1, rows, :] + add


def finish(depth, flux, old, news):
    vmem = pl.BlockSpec(memory_space=pltpu.VMEM)
    return pl.pallas_call(
        finish_kernel,
        in_specs=[vmem] * 7,
        out_specs=[vmem] * 2,
        out_shape=(jax.ShapeDtypeStruct(depth.shape, F32), jax.ShapeDtypeStruct(flux.shape, F32)),
        scratch_shapes=[pltpu.VMEM((4, 3 * C_ROWS, 128), F32), pltpu.VMEM((3 * C_ROWS, COLS), F32)],
        compiler_params=pltpu.CompilerParams(vmem_limit_bytes=VMEM_LIMIT),
    )(depth, flux, old, *news)


def time_route(move):
    route = []
    for source in range(SLICES):
        z, x, core = move(source // 8, (source // 2) % 4, source % 2)
        route.append((source, (z % 2) * 8 + (x % 4) * 2 + core % 2))
    return route


def ring(values, distance):
    return lax.ppermute(values, "sx", [(i, (i + distance) % 4) for i in range(4)])


def over_x(values, distance):
    return lax.ppermute(values, "tm", time_route(lambda z, x, core: (z, x + distance, core)))


def on_device(
    depth_start, flux_start, elevation, roughness_class, building, manning, radar_rates, tile_index
):
    fields = (depth_start, flux_start, elevation, roughness_class, building)
    first, second = pack_columns(*fields)
    first = lax.ppermute(first, "sy", [(0, 1), (1, 0), (2, 3), (3, 2)])
    second = lax.ppermute(second, "sy", [(1, 2), (2, 1)])
    top, bottom = pack_rows(*fields, first, second)
    above = ring(bottom, 1)
    below = ring(top, 3)
    depth, flux, old, own, *away, ground = fine(
        manning, radar_rates, *fields, tile_index, first, second, above, below
    )
    half = jnp.concatenate([own] + [over_x(away[d - 1], d) for d in (1, 2, 3)], axis=0)
    across = lax.ppermute(half, "tm", time_route(lambda z, x, core: (z + 1, x, core)))
    mine = jnp.concatenate([half, across, ground], axis=0)
    column = [mine] + [ring(mine, distance) for distance in (1, 2, 3)]
    sibling = time_route(lambda z, x, core: (z, x, core + 1))
    twins = [lax.ppermute(part, "tm", sibling) for part in column]
    news = sweep(column + twins)
    news = [news[0]] + [over_x(news[d], d) for d in (1, 2, 3)]
    return finish(depth, flux, old, news)


def solution(mesh):
    placed = (
        P("tm", "sx", "sy"),
        P("tm", None, "sx", "sy"),
        P("sx", "sy"),
        P("sx", "sy"),
        P("sx", "sy"),
        P(),
        P(),
        P("tm", None, None, None),
    )
    return jax.shard_map(
        on_device,
        mesh=mesh,
        in_specs=placed,
        out_specs=(P("tm", "sx", "sy"), P("tm", None, "sx", "sy")),
        check_vma=False,
    )
```

```python
import math

import jax
import jax.numpy as jnp
from jax import lax
from jax.experimental import pallas as pl
from jax.experimental.pallas import tpu as pltpu
from jax.sharding import PartitionSpec as P

FINE_STEPS = 8
COARSE_STEPS = 2
COARSENING = 4
RAIN_BLOCK = 64
RADAR_TILES = 64
ROUGH_CLASSES = 8
SLICES = 16

GRAVITY = 9.81
DEPTH_FLOOR = 0.05
CELL_SIDE = 2.0
TIME_STEP = 0.25
COARSE_SECONDS = TIME_STEP * FINE_STEPS / COARSE_STEPS
COARSE_SIDE = CELL_SIDE * COARSENING
POWER = -7.0 / 3.0 / math.log(2.0)

COURANT = TIME_STEP / CELL_SIDE
SCALE = COURANT * GRAVITY * TIME_STEP / CELL_SIDE
FLOW_SCALE = SCALE * COURANT
FLOOR = SCALE * DEPTH_FLOOR
FINE_DRAG = GRAVITY * TIME_STEP * SCALE ** (7.0 / 3.0) / FLOW_SCALE
COARSE_DRAG = GRAVITY * COARSE_SECONDS * SCALE ** (7.0 / 3.0) / FLOW_SCALE
CLOSED = 1e30
GROUP = 40

ROWS, COLS = 64, 1024
EDGE = 128
HALO = 8
HIGH, WIDE = ROWS + 2 * HALO, COLS + 2 * EDGE
C_ROWS, C_COLS = ROWS // COARSENING, COLS // COARSENING
C_HIGH, C_WIDE = 32, 384
PART = 3 * C_ROWS // 2
BLOCK = 3 * C_ROWS + 8
F32 = jnp.float32
BF16 = jnp.bfloat16
VMEM_LIMIT = 40 * 1024 * 1024


def face(level, level_next, flux, sill, drag, gate=None):
    raw = jnp.maximum(level, level_next) - sill
    power = jnp.exp2(POWER * jnp.log(jnp.maximum(raw, FLOOR)))
    below = 1.0 + drag * jnp.abs(flux) * power
    inverse = pl.reciprocal(below, approx=True)
    if gate is not None:
        inverse = gate * inverse
    return inverse * (flux - (level_next - level) * jnp.maximum(raw, 0.0))


def split_dot(values, weights, parts=3):
    total = None
    for part in range(parts):
        piece = values.astype(BF16)
        product = jnp.dot(piece, weights, preferred_element_type=F32)
        total = product if total is None else total + product
        if part + 1 < parts:
            values = values - piece.astype(F32)
    return total


def turn(values, shift, axis):
    return pltpu.roll(values, shift % values.shape[axis], axis)


def static_faces(elev, friction, opened, axis, drag):
    sill = jnp.maximum(elev, turn(elev, -1, axis))
    rough = 0.5 * (friction + turn(friction, -1, axis))
    gate = opened * turn(opened, -1, axis)
    return sill, drag * rough * rough, gate


def whole_step(level, flux_x, flux_y, faces_x, faces_y, rain):
    flux_x = face(level, turn(level, -1, 0), flux_x, *faces_x)
    flux_y = face(level, turn(level, -1, 1), flux_y, *faces_y)
    gain = (turn(flux_x, 1, 0) - flux_x) + (turn(flux_y, 1, 1) - flux_y)
    return level + (gain + rain), flux_x, flux_y


def edge_parts(index):
    return (
        (0, HALO, HALO * index),
        (ROWS - HALO, HALO, 6 * HALO + HALO * index),
        (HALO, ROWS - 2 * HALO, 12 * HALO + (ROWS - 2 * HALO) * index),
    )


def pack_kernel(*refs):
    ins, (first, second, row_a, row_b) = refs[:20], refs[20:]
    even = lax.axis_index("sy") % 2 == 0
    even_row = lax.axis_index("sx") % 2 == 0
    index = 0
    for array in range(5):
        left, right, top, bottom = ins[4 * array : 4 * array + 4]
        for lead in (((0,),), ((0, 0), (0, 1)), ((),), ((),), ((),))[array]:
            for row, count, place in edge_parts(index):
                where = lead + (slice(row, row + count), slice(None))
                a, b = left[where].astype(F32), right[where].astype(F32)
                first[place : place + count, :] = jnp.where(even, b, a)
                second[place : place + count, :] = jnp.where(even, a, b)
            here = slice(HALO * index, HALO * index + HALO)
            where = lead + (slice(None), slice(None))
            a, b = top[where].astype(F32), bottom[where].astype(F32)
            row_a[here, :] = jnp.where(even_row, b, a)
            row_b[here, :] = jnp.where(even_row, a, b)
            index += 1


def pack(*fields):
    specs, args = [], []
    for array in fields:
        lead = array.shape[:-2]
        zeros = (0,) * len(lead)
        for shape, place in (
            ((ROWS, EDGE), (0, 0)),
            ((ROWS, EDGE), (0, COLS // EDGE - 1)),
            ((HALO, COLS), (0, 0)),
            ((HALO, COLS), (ROWS // HALO - 1, 0)),
        ):
            specs.append(pl.BlockSpec(lead + shape, lambda i, at=zeros + place: at))
            args.append(array)
    column = jax.ShapeDtypeStruct((6 * ROWS, EDGE), F32)
    row = jax.ShapeDtypeStruct((6 * HALO, COLS), F32)
    return pl.pallas_call(
        pack_kernel,
        grid=(1,),
        in_specs=specs,
        out_specs=[pl.BlockSpec(memory_space=pltpu.VMEM)] * 4,
        out_shape=(column, column, row, row),
    )(*args)


def fine_kernel(
    manning, radar, depth, flux, elevation, roughness, building, tiles, first, second, row_a, row_b, corner_a, corner_b,
    depth_out, flux_out, old_out, to0, to1, to2, to3, ground_out,
    level, flow_x, flow_y, elev, friction, opened,
    sill_x, drag_x, sill_y, drag_y,
    index_s, rain_s, pooled, coarse, ground_s,
):
    row_place = lax.axis_index("sx")
    col_place = lax.axis_index("sy")
    time_place = lax.axis_index("tm")
    x_place, core = (time_place // 2) % 4, time_place % 2
    even = col_place % 2 == 0
    odd_row = row_place % 2 == 1

    def fill(target, index, own, scale=1.0):
        target[0:8, :] = jnp.zeros((8, WIDE), F32)
        target[88:96, :] = jnp.zeros((8, WIDE), F32)
        target[16:80, EDGE : EDGE + COLS] = scale * own
        for row, count, place in edge_parts(index):
            rows, a, b = slice(16 + row, 16 + row + count), first[place : place + count], second[place : place + count]
            target[rows, 0:EDGE] = scale * jnp.where(even, b, a)
            target[rows, EDGE + COLS : WIDE] = scale * jnp.where(even, a, b)
        here = slice(index * HALO, index * HALO + HALO)
        there = slice((6 + index) * HALO, (6 + index) * HALO + HALO)
        for rows, is_first in ((slice(8, 16), odd_row), (slice(80, 88), ~odd_row)):
            target[rows, EDGE : EDGE + COLS] = scale * jnp.where(is_first, row_a[here, :], row_b[here, :])
            a = jnp.where(is_first, corner_a[here, :], corner_b[here, :])
            b = jnp.where(is_first, corner_a[there, :], corner_b[there, :])
            target[rows, 0:EDGE] = scale * jnp.where(even, b, a)
            target[rows, EDGE + COLS : WIDE] = scale * jnp.where(even, a, b)

    fill(level, 0, depth[0], SCALE)
    fill(flow_x, 1, flux[0, 0], FLOW_SCALE)
    fill(flow_y, 2, flux[0, 1], FLOW_SCALE)
    fill(elev, 3, elevation[...], SCALE)
    fill(friction, 4, roughness[...].astype(F32))
    fill(opened, 5, building[...].astype(F32))

    lane = lax.broadcasted_iota(jnp.int32, (8, WIDE), 1)
    inside = jnp.where(
        ((col_place == 0) & (lane < EDGE)) | ((col_place == 3) & (lane >= EDGE + COLS)), 0.0, 1.0
    )
    for k in range(12):
        here = pl.ds(8 * k, 8)
        classes = friction[here, :]
        value = jnp.full((8, WIDE), manning[0], F32)
        for entry in range(1, ROUGH_CLASSES):
            value = jnp.where(classes == float(entry), manning[entry], value)
        friction[here, :] = value
        if k in (0, 11):
            opened[here, :] = jnp.zeros((8, WIDE), F32)
            continue
        free = (1.0 - opened[here, :]) * inside
        if k == 1:
            free = free * jnp.where(row_place == 0, 0.0, 1.0)
        if k == 10:
            free = free * jnp.where(row_place == 3, 0.0, 1.0)
        opened[here, :] = free

    index_s[...] = jnp.full((32, 128), -1, jnp.int32)
    for step in range(FINE_STEPS):
        index_s[4 * step : 4 * step + 4, 0:64] = tiles[0, step]
    index = index_s[...]
    rates = jnp.zeros((32, 128), F32)
    for entry in range(RADAR_TILES):
        rates = jnp.where(index == entry, radar[entry], rates)
    block = lax.broadcasted_iota(jnp.int32, (128, WIDE), 0)
    column = lax.broadcasted_iota(jnp.int32, (128, WIDE), 1) + (COLS * col_place - EDGE)
    rain_s[0:32, :] = (SCALE * TIME_STEP) * split_dot(rates, jnp.where((column >> 6) == block, 1.0, 0.0).astype(BF16))
    means = []
    for half in range(COARSE_STEPS):
        part = rates[16 * half : 16 * half + 16, :]
        means.append((0.25 * SCALE * COARSE_SECONDS) * (part[0:4] + part[4:8] + part[8:12] + part[12:16]))
    coarse_rates = jnp.concatenate(means, axis=0)
    block = lax.broadcasted_iota(jnp.int32, (128, C_WIDE), 0)
    column = lax.broadcasted_iota(jnp.int32, (128, C_WIDE), 1) + (C_COLS * col_place - EDGE // COARSENING)
    padded = jnp.concatenate([coarse_rates, jnp.zeros((8, 128), F32)], axis=0)
    rain_s[32:40, 0:C_WIDE] = split_dot(
        padded, jnp.where((column >> 4) == block, 1.0, 0.0).astype(BF16)
    )[0:8]
    row_above = jnp.maximum(row_place - 1, 0)
    row_below = jnp.minimum(row_place + 1, 3)

    pool = jnp.where(
        lax.broadcasted_iota(jnp.int32, (512, 128), 0) // COARSENING
        == lax.broadcasted_iota(jnp.int32, (512, 128), 1),
        1.0 / 16.0,
        0.0,
    ).astype(BF16)

    def restrict(source, slot):
        for part in range(3):
            take = source[8:88, 512 * part : min(512 * part + 512, WIDE)]
            pooled[part, :, :] = split_dot(take, pool[0 : take.shape[1], :], 1 if slot == 5 else 2)
        for part in range(3):
            cols = slice(128 * part, 128 * part + 128)
            for target, start, count in ((6, 0, 2), (8, 8, 16), (24, 72, 2)):
                total = pooled[part, pl.ds(start, count, stride=4), :]
                for q in range(1, 4):
                    total = total + pooled[part, pl.ds(start + q, count, stride=4), :]
                coarse[slot, target : target + count, cols] = total

    coarse[...] = jnp.zeros(coarse.shape, F32)
    for slot, source in enumerate((level, flow_x, flow_y, elev, friction, opened)):
        restrict(source, slot)

    for k in range(10):
        rows, after, out = pl.ds(8 + 8 * k, 8), pl.ds(9 + 8 * k, 8), pl.ds(8 * k, 8)
        e, f, o = elev[rows, :], friction[rows, :], opened[rows, :]
        gate = o * opened[after, :]
        sill_x[out, :] = jnp.where(gate > 0.0, jnp.maximum(e, elev[after, :]), CLOSED)
        flow_x[rows, :] = gate * flow_x[rows, :]
        rough = 0.5 * (f + friction[after, :])
        drag_x[out, :] = FINE_DRAG * rough * rough
        sill, drag_y[out, :], gate = static_faces(e, f, o, 1, FINE_DRAG)
        sill_y[out, :] = jnp.where(gate > 0.0, sill, CLOSED)
        flow_y[rows, :] = gate * flow_y[rows, :]

    for k in range(12):
        here = pl.ds(8 * k, 8)
        level[here, :] = level[here, :] + elev[here, :]
    sub = lax.broadcasted_iota(jnp.int32, (GROUP, WIDE), 0)

    def fine_step(step, carry):
        rains = [rain_s[pl.ds(4 * step + place, 1), :] for place in (row_above, row_place, row_below)]
        now = level[8 : 8 + GROUP, :]
        up = turn(now, -1, 0)
        west = now
        for k in range(HIGH // GROUP):
            out = slice(GROUP * k, GROUP * k + GROUP)
            rows = slice(8 + GROUP * k, 8 + GROUP * k + GROUP)
            if k + 1 < HIGH // GROUP:
                after = level[8 + GROUP * k + GROUP : 8 + 2 * GROUP + GROUP * k, :]
                up_after = turn(after, -1, 0)
            north = jnp.where(sub == GROUP - 1, up_after, up)
            qx = face(now, north, flow_x[rows, :], sill_x[out, :], drag_x[out, :])
            qy = face(now, turn(now, -1, 1), flow_y[rows, :], sill_y[out, :], drag_y[out, :])
            flow_x[rows, :] = qx
            flow_y[rows, :] = qy
            down = turn(qx, 1, 0)
            gain = (jnp.where(sub == 0, west, down) - qx) + (turn(qy, 1, 1) - qy)
            rain = rains[1]
            if k == 0:
                rain = jnp.where(sub < HALO, rains[0], rain)
            if k + 1 == HIGH // GROUP:
                rain = jnp.where(sub >= GROUP - HALO, rains[2], rain)
            level[rows, :] = now + (gain + rain)
            now, up, west = after, up_after, down
        return carry

    lax.fori_loop(0, FINE_STEPS, fine_step, 0)

    c_elev, c_friction, c_open = coarse[3], coarse[4], coarse[5]
    faces_x = static_faces(c_elev, c_friction, c_open, 0, COARSE_DRAG)
    faces_y = static_faces(c_elev, c_friction, c_open, 1, COARSE_DRAG)
    state = (coarse[0] + c_elev, coarse[1], coarse[2])
    row = lax.broadcasted_iota(jnp.int32, (C_HIGH, C_WIDE), 0)
    for step in range(COARSE_STEPS):
        parts = [rain_s[pl.ds(32 + 4 * step + place, 1), 0:C_WIDE] for place in (row_above, row_place, row_below)]
        rain = jnp.where(row < 8, parts[0], jnp.where(row < 24, parts[1], parts[2]))
        state = whole_step(*state, faces_x, faces_y, rain)
    old = (state[0] - c_elev, state[1], state[2])

    for k in range(10):
        rows = pl.ds(8 + 8 * k, 8)
        level[rows, :] = level[rows, :] - elev[rows, :]
    own = (slice(16, 80), slice(EDGE, EDGE + COLS))
    depth_out[0] = (1.0 / SCALE) * level[own]
    flux_out[0, 0] = (1.0 / FLOW_SCALE) * flow_x[own]
    flux_out[0, 1] = (1.0 / FLOW_SCALE) * flow_y[own]
    for slot, source in enumerate((level, flow_x, flow_y)):
        restrict(source, slot)
    factor = jnp.where(time_place == 0, 0.0, 1.0)
    side = EDGE // COARSENING
    outs = (to0, to1, to2, to3)
    for slot in range(3):
        mine = old[slot][8:24, :]
        old_out[C_ROWS * slot : C_ROWS * slot + C_ROWS, :] = turn(mine, -side, 1)[:, 0:C_COLS]
        value = coarse[slot, 8:24, :] - factor * mine
        for d, out in enumerate(outs):
            window = (x_place + d) % 4
            moved = pltpu.roll(value, (C_WIDE - 64 * window) % C_WIDE, 1)
            out[C_ROWS * slot : C_ROWS * slot + C_ROWS, :] = moved[:, 0:128]
        fixed = pltpu.roll(coarse[3 + slot, 8:24, :], (C_WIDE - 64 * x_place) % C_WIDE, 1)
        ground_s[C_ROWS * slot : C_ROWS * slot + C_ROWS, :] = fixed[:, 0:128]
    ground_out[...] = ground_s[pl.ds(pl.multiple_of(core * PART, PART), PART), :]
    for out in outs:
        out[3 * C_ROWS : BLOCK, :] = coarse_rates


def fine(manning, radar, depth, flux, *rest):
    smem = pl.BlockSpec(memory_space=pltpu.SMEM)
    vmem = pl.BlockSpec(memory_space=pltpu.VMEM)
    message = jax.ShapeDtypeStruct((BLOCK, 128), F32)
    padded = pltpu.VMEM((HIGH + 16, WIDE), F32)
    faces = pltpu.VMEM((HIGH, WIDE), F32)
    return pl.pallas_call(
        fine_kernel,
        in_specs=[smem, smem] + [vmem] * 12,
        out_specs=[vmem] * 8,
        out_shape=(
            jax.ShapeDtypeStruct(depth.shape, F32),
            jax.ShapeDtypeStruct(flux.shape, F32),
            jax.ShapeDtypeStruct((3 * C_ROWS, C_COLS), F32),
            message,
            message,
            message,
            message,
            jax.ShapeDtypeStruct((PART, 128), F32),
        ),
        scratch_shapes=[padded] * 6
        + [faces] * 4
        + [
            pltpu.VMEM((32, 128), jnp.int32),
            pltpu.VMEM((40, WIDE), F32),
            pltpu.VMEM((3, HIGH, 128), F32),
            pltpu.VMEM((6, C_HIGH, C_WIDE), F32),
            pltpu.VMEM((3 * C_ROWS, 128), F32),
        ],
        compiler_params=pltpu.CompilerParams(vmem_limit_bytes=VMEM_LIMIT),
    )(manning, radar, depth, flux, *rest)


HALF = SLICES // 2
TALL = 4 * C_ROWS
NEAR = 3 * C_ROWS
FIELDS = 3 * C_ROWS


def sweep_faces(ground):
    sill, drag, gate = static_faces(*ground, 0, COARSE_DRAG)
    last = lax.broadcasted_iota(jnp.int32, gate.shape, 0) == gate.shape[0] - 1
    gate = jnp.where(last, 0.0, gate)
    return (sill, drag, gate), static_faces(*ground, 1, COARSE_DRAG)


def near_start(row_place):
    return pl.multiple_of(C_ROWS * jnp.clip(row_place - 1, 0, 1), C_ROWS)


def sweep_slices(start, state, change, rain, ground, newest, top, high):
    faces_x, faces_y = sweep_faces(ground)
    rows = pl.ds(top, high)

    def one_slice(moment, state):
        for step in range(COARSE_STEPS):
            wet = jnp.concatenate(
                [
                    jnp.broadcast_to(
                        rain[pl.ds(8 * moment + 4 * step + top // C_ROWS + b, 1), :], (C_ROWS, 128)
                    )
                    for b in range(high // C_ROWS)
                ],
                axis=0,
            )
            state = whole_step(*state, faces_x, faces_y, wet)
        for field in range(3):
            newest[3 * moment + field, 0:high, :] = state[field]
        return tuple(state[field] + change[3 * moment + field, rows, :] for field in range(3))

    return lax.fori_loop(start, HALF, one_slice, state)


def first_kernel(*refs):
    ins, (change, rain, ground, newest, halfway), (rates, state_s, all_s, parts_s) = refs[:8], refs[8:13], refs[13:]
    row_place = lax.axis_index("sx")
    col_place = lax.axis_index("sy")
    time_place = lax.axis_index("tm")
    z_place, x_place, core = time_place // 8, (time_place // 2) % 4, time_place % 2

    for other in range(2):
        for e in range(4):
            ref = ins[4 * other + e]
            source = (row_place, row_place + 1 - 2 * (row_place % 2), 3 - row_place, (row_place + 2) % 4)[e]
            start = pl.multiple_of(C_ROWS * source, C_ROWS)
            rows = pl.ds(start, C_ROWS)
            for d in range(4):
                slice_of = ((x_place + 4 - d) % 4) * 2 + (core + other) % 2
                for field in range(3):
                    base = FIELDS * d + C_ROWS * field
                    change[3 * slice_of + field, rows, :] = ref[base : base + C_ROWS, :]
                if e == 0:
                    base = 4 * FIELDS + PART + 8 * d
                    rates[pl.ds(pl.multiple_of(8 * slice_of, 8), 8), :] = ref[base : base + 8, :]
            half = (core + other) % 2
            base = 4 * FIELDS
            parts_s[pl.ds(pl.multiple_of(half * PART, PART), PART), :] = ref[base : base + PART, :]
            if other == 1:
                twin = ins[e]
                parts_s[pl.ds(pl.multiple_of(core * PART, PART), PART), :] = twin[base : base + PART, :]
                for field in range(3):
                    ground[field, rows, :] = parts_s[C_ROWS * field : C_ROWS * field + C_ROWS, :]

    block = lax.broadcasted_iota(jnp.int32, (128, 128), 0)
    column = lax.broadcasted_iota(jnp.int32, (128, 128), 1)
    column = column + (C_COLS * col_place + 64 * x_place - EDGE // COARSENING)
    rain[...] = split_dot(rates[...], jnp.where((column >> 4) == block, 1.0, 0.0).astype(BF16))

    start = jnp.where(z_place == 0, 1, HALF)
    fixed = (ground[0], ground[1], ground[2])
    state = (change[0] + ground[0], change[1], change[2])
    state = sweep_slices(start, state, change, rain, fixed, newest, 0, TALL)
    near = pl.ds(near_start(row_place), NEAR)
    for field in range(3):
        all_s[field] = state[field]
        state_s[NEAR * field : NEAR * field + NEAR, :] = all_s[field, near, :]
    count = 3 * NEAR // 2
    halfway[...] = state_s[pl.ds(pl.multiple_of(core * count, count), count), :]


def first_sweep(arrays):
    vmem = pl.BlockSpec(memory_space=pltpu.VMEM)
    field = jax.ShapeDtypeStruct((3 * HALF, TALL, 128), F32)
    return pl.pallas_call(
        first_kernel,
        in_specs=[vmem] * 8,
        out_specs=[vmem] * 5,
        out_shape=(
            field,
            jax.ShapeDtypeStruct((8 * HALF, 128), F32),
            jax.ShapeDtypeStruct((3, TALL, 128), F32),
            field,
            jax.ShapeDtypeStruct((3 * NEAR // 2, 128), F32),
        ),
        scratch_shapes=[
            pltpu.VMEM((8 * HALF, 128), F32),
            pltpu.VMEM((3 * NEAR, 128), F32),
            pltpu.VMEM((3, TALL, 128), F32),
            pltpu.VMEM((3 * C_ROWS, 128), F32),
        ],
        compiler_params=pltpu.CompilerParams(vmem_limit_bytes=VMEM_LIMIT),
    )(*arrays)


def second_kernel(change, rain, ground, early, mine, twin, out0, out1, out2, out3, late, state_s):
    row_place = lax.axis_index("sx")
    time_place = lax.axis_index("tm")
    z_place, x_place, core = time_place // 8, (time_place // 2) % 4, time_place % 2
    count = 3 * NEAR // 2
    state_s[pl.ds(pl.multiple_of(core * count, count), count), :] = mine[...]
    state_s[pl.ds(pl.multiple_of((1 - core) * count, count), count), :] = twin[...]
    state = tuple(state_s[NEAR * field : NEAR * field + NEAR, :] for field in range(3))
    start = jnp.where(z_place == 0, HALF, 0)
    top = near_start(row_place)
    fixed = tuple(ground[field, pl.ds(top, NEAR), :] for field in range(3))
    sweep_slices(start, state, change, rain, fixed, late, top, NEAR)
    rows = pl.ds(pl.multiple_of(C_ROWS * row_place, C_ROWS), C_ROWS)
    late_rows = pl.ds(pl.multiple_of(C_ROWS * row_place - top, C_ROWS), C_ROWS)
    for d, out in enumerate((out0, out1, out2, out3)):
        slice_of = ((x_place + d) % 4) * 2 + core
        for field in range(3):
            here = 3 * slice_of + field
            value = jnp.where(z_place == 0, early[here, rows, :], late[here, late_rows, :])
            if field == 0:
                value = value - ground[0, rows, :]
            out[C_ROWS * field : C_ROWS * field + C_ROWS, :] = value


def second_sweep(change, rain, ground, early, mine, twin):
    vmem = pl.BlockSpec(memory_space=pltpu.VMEM)
    out = jax.ShapeDtypeStruct((FIELDS, 128), F32)
    return pl.pallas_call(
        second_kernel,
        in_specs=[vmem] * 6,
        out_specs=[vmem] * 4,
        out_shape=(out,) * 4,
        scratch_shapes=[pltpu.VMEM((3 * HALF, NEAR, 128), F32), pltpu.VMEM((3 * NEAR, 128), F32)],
        compiler_params=pltpu.CompilerParams(vmem_limit_bytes=VMEM_LIMIT),
    )(change, rain, ground, early, mine, twin)


def finish_kernel(depth, flux, old, new0, new1, new2, new3, depth_out, flux_out, parts, spread):
    time_place = lax.axis_index("tm")
    x_place = (time_place // 2) % 4
    for d, ref in enumerate((new0, new1, new2, new3)):
        parts[(x_place + 4 - d) % 4] = ref[...]
    lane = lax.broadcasted_iota(jnp.int32, (3 * C_ROWS, 128), 1)
    halves = [jnp.where(lane < 64, turn(parts[b], -32, 1), turn(parts[b + 1], 32, 1)) for b in (0, 2)]
    delta = jnp.concatenate(halves, axis=1) - old[...]
    delta = jnp.where(time_place == 0, 0.0, delta)
    copies = jnp.where(
        lax.broadcasted_iota(jnp.int32, (C_COLS, COLS), 0)
        == lax.broadcasted_iota(jnp.int32, (C_COLS, COLS), 1) // COARSENING,
        1.0,
        0.0,
    ).astype(BF16)
    scale = jnp.where(
        lax.broadcasted_iota(jnp.int32, (3 * C_ROWS, C_COLS), 0) < C_ROWS, 1.0 / SCALE, 1.0 / FLOW_SCALE
    )
    spread[...] = split_dot(scale * delta, copies)
    low = lax.broadcasted_iota(jnp.int32, (8, COLS), 0) < 4
    for field in range(3):
        for k in range(ROWS // 8):
            row = C_ROWS * field + 2 * k
            add = jnp.where(low, spread[row : row + 1, :], spread[row + 1 : row + 2, :])
            rows = slice(8 * k, 8 * k + 8)
            if field == 0:
                depth_out[0, rows, :] = depth[0, rows, :] + add
            else:
                flux_out[0, field - 1, rows, :] = flux[0, field - 1, rows, :] + add


def finish(depth, flux, old, news):
    vmem = pl.BlockSpec(memory_space=pltpu.VMEM)
    return pl.pallas_call(
        finish_kernel,
        in_specs=[vmem] * 7,
        out_specs=[vmem] * 2,
        out_shape=(jax.ShapeDtypeStruct(depth.shape, F32), jax.ShapeDtypeStruct(flux.shape, F32)),
        scratch_shapes=[pltpu.VMEM((4, 3 * C_ROWS, 128), F32), pltpu.VMEM((3 * C_ROWS, COLS), F32)],
        compiler_params=pltpu.CompilerParams(vmem_limit_bytes=VMEM_LIMIT),
    )(depth, flux, old, *news)


def time_route(move):
    route = []
    for source in range(SLICES):
        z, x, core = move(source // 8, (source // 2) % 4, source % 2)
        route.append((source, (z % 2) * 8 + (x % 4) * 2 + core % 2))
    return route


def with_row(values, flip):
    return lax.ppermute(values, "sx", [(i, i ^ flip) for i in range(4)])


def over_x(values, distance):
    return lax.ppermute(values, "tm", time_route(lambda z, x, core: (z, x + distance, core)))


def on_device(
    depth_start, flux_start, elevation, roughness_class, building, manning, radar_rates, tile_index
):
    fields = (depth_start, flux_start, elevation, roughness_class, building)
    first, second, row_a, row_b = pack(*fields)
    first = lax.ppermute(first, "sy", [(0, 1), (1, 0), (2, 3), (3, 2)])
    second = lax.ppermute(second, "sy", [(1, 2), (2, 1)])
    row_a, row_b = with_row(row_a, 1), with_row(row_b, 3)
    size = 6 * HALO
    tops = jnp.concatenate([first[:size], second[:size]], axis=0)
    bottoms = jnp.concatenate([first[size : 2 * size], second[size : 2 * size]], axis=0)
    even_row = lax.axis_index("sx") % 2 == 0
    corner_a = with_row(jnp.where(even_row, bottoms, tops), 1)
    corner_b = with_row(jnp.where(even_row, tops, bottoms), 3)
    depth, flux, old, own, *away, ground = fine(
        manning, radar_rates, *fields, tile_index, first, second, row_a, row_b, corner_a, corner_b
    )
    parts = [own] + [over_x(away[d - 1], d) for d in (1, 2, 3)]
    column = jnp.concatenate([part[:FIELDS] for part in parts] + [ground], axis=0)
    mine = jnp.concatenate([column] + [part[FIELDS:] for part in parts], axis=0)
    sibling = time_route(lambda z, x, core: (z, x, core + 1))
    arrays = [mine] + [with_row(column, flip) for flip in (1, 3, 2)]
    arrays = arrays + [lax.ppermute(part, "tm", sibling) for part in arrays]
    change, rain, ground, early, halfway = first_sweep(arrays)
    halfway = lax.ppermute(halfway, "tm", time_route(lambda z, x, core: (z + 1, x, core)))
    twin = lax.ppermute(halfway, "tm", sibling)
    news = second_sweep(change, rain, ground, early, halfway, twin)
    news = [news[0]] + [over_x(news[d], d) for d in (1, 2, 3)]
    return finish(depth, flux, old, news)


def solution(mesh):
    placed = (
        P("tm", "sx", "sy"),
        P("tm", None, "sx", "sy"),
        P("sx", "sy"),
        P("sx", "sy"),
        P("sx", "sy"),
        P(),
        P(),
        P("tm", None, None, None),
    )
    return jax.shard_map(
        on_device,
        mesh=mesh,
        in_specs=placed,
        out_specs=(P("tm", "sx", "sy"), P("tm", None, "sx", "sy")),
        check_vma=False,
    )
```

```python
import math

import jax
import jax.numpy as jnp
from jax import lax
from jax.experimental import pallas as pl
from jax.experimental.pallas import tpu as pltpu
from jax.sharding import PartitionSpec as P

FINE_STEPS = 8
COARSE_STEPS = 2
COARSENING = 4
RAIN_BLOCK = 64
RADAR_TILES = 64
ROUGH_CLASSES = 8
SLICES = 16

GRAVITY = 9.81
DEPTH_FLOOR = 0.05
CELL_SIDE = 2.0
TIME_STEP = 0.25
COARSE_SECONDS = TIME_STEP * FINE_STEPS / COARSE_STEPS
COARSE_SIDE = CELL_SIDE * COARSENING
POWER = -7.0 / 3.0 / math.log(2.0)

COURANT = TIME_STEP / CELL_SIDE
SCALE = COURANT * GRAVITY * TIME_STEP / CELL_SIDE
FLOW_SCALE = SCALE * COURANT
FLOOR = SCALE * DEPTH_FLOOR
FINE_DRAG = GRAVITY * TIME_STEP * SCALE ** (7.0 / 3.0) / FLOW_SCALE
COARSE_DRAG = GRAVITY * COARSE_SECONDS * SCALE ** (7.0 / 3.0) / FLOW_SCALE
CLOSED = 1e30
GROUP = 40

ROWS, COLS = 64, 1024
EDGE = 128
HALO = 8
HIGH, WIDE = ROWS + 2 * HALO, COLS + 2 * EDGE
C_ROWS, C_COLS = ROWS // COARSENING, COLS // COARSENING
C_HIGH, C_WIDE = 32, 384
PART = 3 * C_ROWS // 2
BLOCK = 3 * C_ROWS + 8
F32 = jnp.float32
BF16 = jnp.bfloat16
VMEM_LIMIT = 24 * 1024 * 1024


def face(level, level_next, flux, sill, drag, gate=None):
    raw = jnp.maximum(level, level_next) - sill
    power = jnp.exp2(POWER * jnp.log(jnp.maximum(raw, FLOOR)))
    below = 1.0 + drag * jnp.abs(flux) * power
    inverse = pl.reciprocal(below, approx=True)
    if gate is not None:
        inverse = gate * inverse
    return inverse * (flux - (level_next - level) * jnp.maximum(raw, 0.0))


def split_dot(values, weights, parts=3):
    total = None
    for part in range(parts):
        piece = values.astype(BF16)
        product = jnp.dot(piece, weights, preferred_element_type=F32)
        total = product if total is None else total + product
        if part + 1 < parts:
            values = values - piece.astype(F32)
    return total


def turn(values, shift, axis):
    return pltpu.roll(values, shift % values.shape[axis], axis)


def static_faces(elev, friction, opened, axis, drag):
    sill = jnp.maximum(elev, turn(elev, -1, axis))
    rough = 0.5 * (friction + turn(friction, -1, axis))
    gate = opened * turn(opened, -1, axis)
    return sill, drag * rough * rough, gate


def whole_step(level, flux_x, flux_y, faces_x, faces_y, rain):
    flux_x = face(level, turn(level, -1, 0), flux_x, *faces_x)
    flux_y = face(level, turn(level, -1, 1), flux_y, *faces_y)
    gain = (turn(flux_x, 1, 0) - flux_x) + (turn(flux_y, 1, 1) - flux_y)
    return level + (gain + rain), flux_x, flux_y


def both_sides_step(level, fluxes, faces, rain):
    last_x, next_x, last_y, next_y = fluxes
    fluxes = (
        face(turn(level, 1, 0), level, last_x, *faces[0]),
        face(level, turn(level, -1, 0), next_x, *faces[1]),
        face(turn(level, 1, 1), level, last_y, *faces[2]),
        face(level, turn(level, -1, 1), next_y, *faces[3]),
    )
    gain = (fluxes[0] - fluxes[1]) + (fluxes[2] - fluxes[3])
    return level + (gain + rain), fluxes


def edge_parts(index):
    return (
        (0, HALO, HALO * index),
        (ROWS - HALO, HALO, 6 * HALO + HALO * index),
        (HALO, ROWS - 2 * HALO, 12 * HALO + (ROWS - 2 * HALO) * index),
    )


def pack_kernel(*refs):
    ins, (first, second, row_a, row_b) = refs[:20], refs[20:]
    even = lax.axis_index("sy") % 2 == 0
    even_row = lax.axis_index("sx") % 2 == 0
    index = 0
    for array in range(5):
        left, right, top, bottom = ins[4 * array : 4 * array + 4]
        for lead in (((0,),), ((0, 0), (0, 1)), ((),), ((),), ((),))[array]:
            for row, count, place in edge_parts(index):
                where = lead + (slice(row, row + count), slice(None))
                a, b = left[where].astype(F32), right[where].astype(F32)
                first[place : place + count, :] = jnp.where(even, b, a)
                second[place : place + count, :] = jnp.where(even, a, b)
            here = slice(HALO * index, HALO * index + HALO)
            where = lead + (slice(None), slice(None))
            a, b = top[where].astype(F32), bottom[where].astype(F32)
            row_a[here, :] = jnp.where(even_row, b, a)
            row_b[here, :] = jnp.where(even_row, a, b)
            index += 1


def pack(*fields):
    specs, args = [], []
    for array in fields:
        lead = array.shape[:-2]
        zeros = (0,) * len(lead)
        for shape, place in (
            ((ROWS, EDGE), (0, 0)),
            ((ROWS, EDGE), (0, COLS // EDGE - 1)),
            ((HALO, COLS), (0, 0)),
            ((HALO, COLS), (ROWS // HALO - 1, 0)),
        ):
            specs.append(pl.BlockSpec(lead + shape, lambda i, at=zeros + place: at))
            args.append(array)
    column = jax.ShapeDtypeStruct((6 * ROWS, EDGE), F32)
    row = jax.ShapeDtypeStruct((6 * HALO, COLS), F32)
    return pl.pallas_call(
        pack_kernel,
        grid=(1,),
        in_specs=specs,
        out_specs=[pl.BlockSpec(memory_space=pltpu.VMEM)] * 4,
        out_shape=(column, column, row, row),
    )(*args)


def roughness_of(classes, manning):
    value = jnp.full(classes.shape, manning[0], F32)
    for entry in range(1, ROUGH_CLASSES):
        value = jnp.where(classes == float(entry), manning[entry], value)
    return value


def pool_matrix():
    return jnp.where(
        lax.broadcasted_iota(jnp.int32, (512, 128), 0) // COARSENING
        == lax.broadcasted_iota(jnp.int32, (512, 128), 1),
        1.0 / 16.0,
        0.0,
    ).astype(BF16)


def restrict(sources, take, spans, pooled, coarse):
    pool = pool_matrix()
    high = None
    for part in range(3):
        cols = slice(512 * part, min(512 * part + 512, WIDE))
        values = [take(source, cols) for source in sources]
        high = values[0].shape[0]
        values = jnp.concatenate(values, axis=0)
        pooled[part, 0 : values.shape[0], :] = split_dot(values, pool[0 : values.shape[1], :], 2)
    for slot in range(len(sources)):
        for part in range(3):
            cols = slice(128 * part, 128 * part + 128)
            for target, start, count in spans:
                first = high * slot + start
                total = pooled[part, pl.ds(first, count, stride=4), :]
                for q in range(1, 4):
                    total = total + pooled[part, pl.ds(first + q, count, stride=4), :]
                coarse[slot, target : target + count, cols] = total


def set_faces(k, elev, friction, opened, sill_x, drag_x, sill_y, drag_y):
    rows, after, out = pl.ds(8 + 8 * k, 8), pl.ds(9 + 8 * k, 8), pl.ds(8 * k, 8)
    e, f, o = elev[rows, :], friction[rows, :], opened[rows, :]
    gate = o * opened[after, :]
    sill_x[out, :] = jnp.where(gate > 0.0, jnp.maximum(e, elev[after, :]), CLOSED)
    rough = 0.5 * (f + friction[after, :])
    drag_x[out, :] = FINE_DRAG * rough * rough
    sill, drag_y[out, :], gate = static_faces(e, f, o, 1, FINE_DRAG)
    sill_y[out, :] = jnp.where(gate > 0.0, sill, CLOSED)


def places():
    time_place = lax.axis_index("tm")
    return lax.axis_index("sx"), lax.axis_index("sy"), time_place, (time_place // 2) % 4, time_place % 2


def ready_kernel(
    manning, radar, depth, flux, elevation, roughness, building, tiles, first, second, row_a, row_b,
    level, flow_x, flow_y, elev, friction, opened, sill_x, drag_x, sill_y, drag_y, coarse, rain_s, rates_out,
    index_s, pooled,
):
    row_place, col_place, time_place, x_place, core = places()
    even = col_place % 2 == 0
    odd_row = row_place % 2 == 1
    none = jnp.zeros((HALO, EDGE), F32)

    def fill(target, index, own, scale=1.0):
        target[0:8, :] = jnp.zeros((8, WIDE), F32)
        target[88:96, :] = jnp.zeros((8, WIDE), F32)
        target[16:80, EDGE : EDGE + COLS] = scale * own
        for row, count, place in edge_parts(index):
            rows, a, b = slice(16 + row, 16 + row + count), first[place : place + count], second[place : place + count]
            target[rows, 0:EDGE] = scale * jnp.where(even, b, a)
            target[rows, EDGE + COLS : WIDE] = scale * jnp.where(even, a, b)
        here = slice(index * HALO, index * HALO + HALO)
        for rows, is_first in ((slice(8, 16), odd_row), (slice(80, 88), ~odd_row)):
            target[rows, EDGE : EDGE + COLS] = scale * jnp.where(is_first, row_a[here, :], row_b[here, :])
            target[rows, 0:EDGE] = none
            target[rows, EDGE + COLS : WIDE] = none

    fill(level, 0, depth[0], SCALE)
    fill(flow_x, 1, flux[0, 0], FLOW_SCALE)
    fill(flow_y, 2, flux[0, 1], FLOW_SCALE)
    fill(elev, 3, elevation[...], SCALE)
    fill(friction, 4, roughness[...].astype(F32))
    fill(opened, 5, building[...].astype(F32))

    lane = lax.broadcasted_iota(jnp.int32, (8, WIDE), 1)
    inside = jnp.where(
        ((col_place == 0) & (lane < EDGE)) | ((col_place == 3) & (lane >= EDGE + COLS)), 0.0, 1.0
    )
    for k in range(12):
        here = pl.ds(8 * k, 8)
        friction[here, :] = roughness_of(friction[here, :], manning)
        if k in (0, 11):
            opened[here, :] = jnp.zeros((8, WIDE), F32)
            continue
        free = (1.0 - opened[here, :]) * inside
        if k == 1:
            free = free * jnp.where(row_place == 0, 0.0, 1.0)
        if k == 10:
            free = free * jnp.where(row_place == 3, 0.0, 1.0)
        opened[here, :] = free

    index_s[...] = jnp.full((32, 128), -1, jnp.int32)
    for step in range(FINE_STEPS):
        index_s[4 * step : 4 * step + 4, 0:64] = tiles[0, step]
    index = index_s[...]
    rates = jnp.zeros((32, 128), F32)
    for entry in range(RADAR_TILES):
        rates = jnp.where(index == entry, radar[entry], rates)
    block = lax.broadcasted_iota(jnp.int32, (128, WIDE), 0)
    column = lax.broadcasted_iota(jnp.int32, (128, WIDE), 1) + (COLS * col_place - EDGE)
    rain_s[0:32, :] = (SCALE * TIME_STEP) * split_dot(
        rates, jnp.where((column >> 6) == block, 1.0, 0.0).astype(BF16)
    )
    means = []
    for half in range(COARSE_STEPS):
        part = rates[16 * half : 16 * half + 16, :]
        means.append((0.25 * SCALE * COARSE_SECONDS) * (part[0:4] + part[4:8] + part[8:12] + part[12:16]))
    coarse_rates = jnp.concatenate(means, axis=0)
    rates_out[...] = coarse_rates
    block = lax.broadcasted_iota(jnp.int32, (128, C_WIDE), 0)
    column = lax.broadcasted_iota(jnp.int32, (128, C_WIDE), 1) + (C_COLS * col_place - EDGE // COARSENING)
    padded = jnp.concatenate([coarse_rates, jnp.zeros((8, 128), F32)], axis=0)
    rain_s[32:40, :] = jnp.zeros((8, WIDE), F32)
    rain_s[32:40, 0:C_WIDE] = split_dot(
        padded, jnp.where((column >> 4) == block, 1.0, 0.0).astype(BF16)
    )[0:8]

    coarse[...] = jnp.zeros(coarse.shape, F32)
    sources = (level, flow_x, flow_y, elev, friction, opened)
    restrict(sources, lambda source, cols: source[16:80, cols], ((8, 0, 16),), pooled, coarse)
    for k in range(1, 8):
        set_faces(k, elev, friction, opened, sill_x, drag_x, sill_y, drag_y)


def fine_kernel(*refs):
    manning, corner_a, corner_b, rain_s, rates = refs[:5]
    level, flow_x, flow_y, elev, friction, opened, sill_x, drag_x, sill_y, drag_y, coarse = refs[16:27]
    depth_out, flux_out, old_out, to0, to1, to2, to3, ground_out = refs[27:35]
    pooled, ground_s, windows = refs[35:]
    row_place, col_place, time_place, x_place, core = places()
    even = col_place % 2 == 0
    odd_row = row_place % 2 == 1

    left, right = slice(0, EDGE), slice(EDGE + COLS, WIDE)
    grid_row = (jnp.where(row_place == 0, 0.0, 1.0), jnp.where(row_place == 3, 0.0, 1.0))
    grid_col = (jnp.where(col_place == 0, 0.0, 1.0), jnp.where(col_place == 3, 0.0, 1.0))
    scales = (SCALE, FLOW_SCALE, FLOW_SCALE, SCALE)
    for index, target in enumerate((level, flow_x, flow_y, elev, friction, opened)):
        here = slice(index * HALO, index * HALO + HALO)
        there = slice((6 + index) * HALO, (6 + index) * HALO + HALO)
        for r, (rows, is_first) in enumerate(((slice(8, 16), odd_row), (slice(80, 88), ~odd_row))):
            a = jnp.where(is_first, corner_a[here, :], corner_b[here, :])
            b = jnp.where(is_first, corner_a[there, :], corner_b[there, :])
            for c, (cols, value) in enumerate(((left, jnp.where(even, b, a)), (right, jnp.where(even, a, b)))):
                if index < 4:
                    value = scales[index] * value
                elif index == 4:
                    value = roughness_of(value, manning)
                else:
                    value = (1.0 - value) * (grid_row[r] * grid_col[c])
                target[rows, cols] = value

    sources = (level, flow_x, flow_y, elev, friction, opened)
    take = lambda source, cols: jnp.concatenate([source[8:16, cols], source[80:88, cols]], axis=0)
    restrict(sources, take, ((6, 0, 2), (24, 8, 2)), pooled, coarse)
    for k in (0, 8, 9):
        set_faces(k, elev, friction, opened, sill_x, drag_x, sill_y, drag_y)
    for k in range(10):
        rows, out = pl.ds(8 + 8 * k, 8), pl.ds(8 * k, 8)
        level[rows, :] = level[rows, :] + elev[rows, :]
        flow_x[rows, :] = jnp.where(sill_x[out, :] < CLOSED, flow_x[rows, :], 0.0)
        flow_y[rows, :] = jnp.where(sill_y[out, :] < CLOSED, flow_y[rows, :], 0.0)
    row_above = jnp.maximum(row_place - 1, 0)
    row_below = jnp.minimum(row_place + 1, 3)

    sub = lax.broadcasted_iota(jnp.int32, (GROUP, WIDE), 0)

    def fine_step(step, carry):
        rains = [rain_s[pl.ds(4 * step + place, 1), :] for place in (row_above, row_place, row_below)]
        now = level[8 : 8 + GROUP, :]
        up = turn(now, -1, 0)
        after, up_after, west = now, up, now
        for k in range(HIGH // GROUP):
            out = slice(GROUP * k, GROUP * k + GROUP)
            rows = slice(8 + GROUP * k, 8 + GROUP * k + GROUP)
            if k + 1 < HIGH // GROUP:
                after = level[8 + GROUP * k + GROUP : 8 + 2 * GROUP + GROUP * k, :]
                up_after = turn(after, -1, 0)
            north = jnp.where(sub == GROUP - 1, up_after, up)
            qx = face(now, north, flow_x[rows, :], sill_x[out, :], drag_x[out, :])
            qy = face(now, turn(now, -1, 1), flow_y[rows, :], sill_y[out, :], drag_y[out, :])
            flow_x[rows, :] = qx
            flow_y[rows, :] = qy
            down = turn(qx, 1, 0)
            gain = (jnp.where(sub == 0, west, down) - qx) + (turn(qy, 1, 1) - qy)
            rain = rains[1]
            if k == 0:
                rain = jnp.where(sub < HALO, rains[0], rain)
            if k + 1 == HIGH // GROUP:
                rain = jnp.where(sub >= GROUP - HALO, rains[2], rain)
            level[rows, :] = now + (gain + rain)
            now, up, west = after, up_after, down
        return carry

    lax.fori_loop(0, FINE_STEPS, fine_step, 0, unroll=True)

    c_elev, c_friction, c_open = coarse[3], coarse[4], coarse[5]
    faces_x = static_faces(c_elev, c_friction, c_open, 0, COARSE_DRAG)
    faces_y = static_faces(c_elev, c_friction, c_open, 1, COARSE_DRAG)
    state = (coarse[0] + c_elev, coarse[1], coarse[2])
    row = lax.broadcasted_iota(jnp.int32, (C_HIGH, C_WIDE), 0)
    for step in range(COARSE_STEPS):
        parts = [rain_s[pl.ds(32 + 4 * step + place, 1), 0:C_WIDE] for place in (row_above, row_place, row_below)]
        rain = jnp.where(row < 8, parts[0], jnp.where(row < 24, parts[1], parts[2]))
        state = whole_step(*state, faces_x, faces_y, rain)
    old = (state[0] - c_elev, state[1], state[2])

    for k in range(10):
        rows = pl.ds(8 + 8 * k, 8)
        level[rows, :] = level[rows, :] - elev[rows, :]
    own = (slice(16, 80), slice(EDGE, EDGE + COLS))
    depth_out[0] = (1.0 / SCALE) * level[own]
    flux_out[0, 0] = (1.0 / FLOW_SCALE) * flow_x[own]
    flux_out[0, 1] = (1.0 / FLOW_SCALE) * flow_y[own]
    sources = (level, flow_x, flow_y)
    restrict(sources, lambda source, cols: source[16:80, cols], ((8, 0, 16),), pooled, coarse)
    factor = jnp.where(time_place == 0, 0.0, 1.0)
    side = EDGE // COARSENING
    outs = (to0, to1, to2, to3)
    for slot in range(3):
        mine = old[slot][8:24, :]
        old_out[C_ROWS * slot : C_ROWS * slot + C_ROWS, :] = turn(mine, -side, 1)[:, 0:C_COLS]
        value = coarse[slot, 8:24, :] - factor * mine
        fixed = coarse[3 + slot, 8:24, :]
        here = slice(C_ROWS * slot, C_ROWS * slot + C_ROWS)
        for odd, (now, ground_now) in enumerate(((value, fixed), (turn(value, -64, 1), turn(fixed, -64, 1)))):
            for half in range(2):
                cols = slice(128 * half, 128 * half + 128)
                windows[2 * half + odd, here, :] = now[:, cols]
                ground_s[2 * half + odd, here, :] = ground_now[:, cols]
    ground_out[...] = ground_s[x_place, pl.ds(pl.multiple_of(core * PART, PART), PART), :]
    for d, out in enumerate(outs):
        out[0 : 3 * C_ROWS, :] = windows[(x_place + d) % 4]
        out[3 * C_ROWS : BLOCK, :] = rates[...]


def ready(manning, radar, *rest):
    smem = pl.BlockSpec(memory_space=pltpu.SMEM)
    vmem = pl.BlockSpec(memory_space=pltpu.VMEM)
    padded = jax.ShapeDtypeStruct((HIGH + 16, WIDE), F32)
    faces = jax.ShapeDtypeStruct((HIGH, WIDE), F32)
    coarse = jax.ShapeDtypeStruct((6, C_HIGH, C_WIDE), F32)
    rain = jax.ShapeDtypeStruct((40, WIDE), F32)
    rates = jax.ShapeDtypeStruct((8, 128), F32)
    return pl.pallas_call(
        ready_kernel,
        in_specs=[smem, smem] + [vmem] * 10,
        out_specs=[vmem] * 13,
        out_shape=[padded] * 6 + [faces] * 4 + [coarse, rain, rates],
        scratch_shapes=[pltpu.VMEM((32, 128), jnp.int32), pltpu.VMEM((3, 6 * ROWS, 128), F32)],
        cost_estimate=pl.CostEstimate(flops=40_000_000, bytes_accessed=10_000_000, transcendentals=0),
        compiler_params=pltpu.CompilerParams(vmem_limit_bytes=VMEM_LIMIT),
    )(manning, radar, *rest)


def fine(manning, corner_a, corner_b, rain, rates, arrays):
    smem = pl.BlockSpec(memory_space=pltpu.SMEM)
    vmem = pl.BlockSpec(memory_space=pltpu.VMEM)
    message = jax.ShapeDtypeStruct((BLOCK, 128), F32)
    shapes = [jax.ShapeDtypeStruct(array.shape, F32) for array in arrays]
    return pl.pallas_call(
        fine_kernel,
        in_specs=[smem] + [vmem] * 15,
        out_specs=[vmem] * 19,
        out_shape=shapes
        + [
            jax.ShapeDtypeStruct((1, ROWS, COLS), F32),
            jax.ShapeDtypeStruct((1, 2, ROWS, COLS), F32),
            jax.ShapeDtypeStruct((3 * C_ROWS, C_COLS), F32),
            message,
            message,
            message,
            message,
            jax.ShapeDtypeStruct((PART, 128), F32),
        ],
        input_output_aliases={5 + place: place for place in range(11)},
        scratch_shapes=[
            pltpu.VMEM((3, 3 * ROWS, 128), F32),
            pltpu.VMEM((4, 3 * C_ROWS, 128), F32),
            pltpu.VMEM((4, 3 * C_ROWS, 128), F32),
        ],
        compiler_params=pltpu.CompilerParams(vmem_limit_bytes=VMEM_LIMIT),
    )(manning, corner_a, corner_b, rain, rates, *arrays)[11:]


HALF = SLICES // 2
TALL = 4 * C_ROWS
NEAR = 3 * C_ROWS
FIELDS = 3 * C_ROWS


def sweep_faces(ground):
    sill, drag, gate = static_faces(*ground, 0, COARSE_DRAG)
    last = lax.broadcasted_iota(jnp.int32, gate.shape, 0) == gate.shape[0] - 1
    gate = jnp.where(last, 0.0, gate)
    faces_x, faces_y = (sill, drag, gate), static_faces(*ground, 1, COARSE_DRAG)
    moved_x = tuple(turn(part, 1, 0) for part in faces_x)
    moved_y = tuple(turn(part, 1, 1) for part in faces_y)
    return moved_x, faces_x, moved_y, faces_y


def near_start(row_place):
    return pl.multiple_of(C_ROWS * jnp.clip(row_place - 1, 0, 1), C_ROWS)


def sweep_slices(first, state, change, rain, ground, newest, top, high):
    faces = sweep_faces(ground)
    rows = pl.ds(top, high)
    level, flux_x, flux_y = state
    fluxes = (turn(flux_x, 1, 0), flux_x, turn(flux_y, 1, 1), flux_y)

    for moment in range(first, HALF):
        for step in range(COARSE_STEPS):
            wet = jnp.concatenate(
                [
                    jnp.broadcast_to(
                        rain[pl.ds(8 * moment + 4 * step + top // C_ROWS + b, 1), :], (C_ROWS, 128)
                    )
                    for b in range(high // C_ROWS)
                ],
                axis=0,
            )
            level, fluxes = both_sides_step(level, fluxes, faces, wet)
        for field, value in enumerate((level, fluxes[1], fluxes[3])):
            newest[3 * moment + field, 0:high, :] = value
        add, add_x, add_y = (change[3 * moment + field, rows, :] for field in range(3))
        level = level + add
        fluxes = (
            fluxes[0] + turn(add_x, 1, 0), fluxes[1] + add_x, fluxes[2] + turn(add_y, 1, 1), fluxes[3] + add_y
        )
    return level, fluxes[1], fluxes[3]


def first_kernel(*refs):
    ins, (change, rain, ground, newest, halfway), (rates, state_s, all_s, parts_s) = refs[:8], refs[8:13], refs[13:]
    row_place = lax.axis_index("sx")
    col_place = lax.axis_index("sy")
    time_place = lax.axis_index("tm")
    z_place, x_place, core = time_place // 8, (time_place // 2) % 4, time_place % 2

    for other in range(2):
        for e in range(4):
            ref = ins[4 * other + e]
            source = (row_place, row_place + 1 - 2 * (row_place % 2), 3 - row_place, (row_place + 2) % 4)[e]
            start = pl.multiple_of(C_ROWS * source, C_ROWS)
            rows = pl.ds(start, C_ROWS)
            for d in range(4):
                slice_of = ((x_place + 4 - d) % 4) * 2 + (core + other) % 2
                for field in range(3):
                    base = FIELDS * d + C_ROWS * field
                    change[3 * slice_of + field, rows, :] = ref[base : base + C_ROWS, :]
                if e == 0:
                    base = 4 * FIELDS + PART + 8 * d
                    rates[pl.ds(pl.multiple_of(8 * slice_of, 8), 8), :] = ref[base : base + 8, :]
            half = (core + other) % 2
            base = 4 * FIELDS
            parts_s[pl.ds(pl.multiple_of(half * PART, PART), PART), :] = ref[base : base + PART, :]
            if other == 1:
                twin = ins[e]
                parts_s[pl.ds(pl.multiple_of(core * PART, PART), PART), :] = twin[base : base + PART, :]
                for field in range(3):
                    ground[field, rows, :] = parts_s[C_ROWS * field : C_ROWS * field + C_ROWS, :]

    block = lax.broadcasted_iota(jnp.int32, (128, 128), 0)
    column = lax.broadcasted_iota(jnp.int32, (128, 128), 1)
    column = column + (C_COLS * col_place + 64 * x_place - EDGE // COARSENING)
    rain[...] = split_dot(rates[...], jnp.where((column >> 4) == block, 1.0, 0.0).astype(BF16))

    all_s[...] = jnp.zeros(all_s.shape, F32)

    @pl.when(z_place == 0)
    def _():
        fixed = (ground[0], ground[1], ground[2])
        state = (change[0] + ground[0], change[1], change[2])
        state = sweep_slices(1, state, change, rain, fixed, newest, 0, TALL)
        for field in range(3):
            all_s[field] = state[field]

    near = pl.ds(near_start(row_place), NEAR)
    for field in range(3):
        state_s[NEAR * field : NEAR * field + NEAR, :] = all_s[field, near, :]
    count = 3 * NEAR // 2
    halfway[...] = state_s[pl.ds(pl.multiple_of(core * count, count), count), :]


def first_sweep(arrays):
    vmem = pl.BlockSpec(memory_space=pltpu.VMEM)
    field = jax.ShapeDtypeStruct((3 * HALF, TALL, 128), F32)
    return pl.pallas_call(
        first_kernel,
        in_specs=[vmem] * 8,
        out_specs=[vmem] * 5,
        out_shape=(
            field,
            jax.ShapeDtypeStruct((8 * HALF, 128), F32),
            jax.ShapeDtypeStruct((3, TALL, 128), F32),
            field,
            jax.ShapeDtypeStruct((3 * NEAR // 2, 128), F32),
        ),
        scratch_shapes=[
            pltpu.VMEM((8 * HALF, 128), F32),
            pltpu.VMEM((3 * NEAR, 128), F32),
            pltpu.VMEM((3, TALL, 128), F32),
            pltpu.VMEM((3 * C_ROWS, 128), F32),
        ],
        compiler_params=pltpu.CompilerParams(vmem_limit_bytes=VMEM_LIMIT),
    )(*arrays)


def second_kernel(change, rain, ground, early, mine, twin, out0, out1, out2, out3, late, state_s):
    row_place = lax.axis_index("sx")
    time_place = lax.axis_index("tm")
    z_place, x_place, core = time_place // 8, (time_place // 2) % 4, time_place % 2
    top = near_start(row_place)

    @pl.when(z_place == 1)
    def _():
        count = 3 * NEAR // 2
        state_s[pl.ds(pl.multiple_of(core * count, count), count), :] = mine[...]
        state_s[pl.ds(pl.multiple_of((1 - core) * count, count), count), :] = twin[...]
        state = tuple(state_s[NEAR * field : NEAR * field + NEAR, :] for field in range(3))
        fixed = tuple(ground[field, pl.ds(top, NEAR), :] for field in range(3))
        sweep_slices(0, state, change, rain, fixed, late, top, NEAR)

    rows = pl.ds(pl.multiple_of(C_ROWS * row_place, C_ROWS), C_ROWS)
    late_rows = pl.ds(pl.multiple_of(C_ROWS * row_place - top, C_ROWS), C_ROWS)
    for d, out in enumerate((out0, out1, out2, out3)):
        slice_of = ((x_place + d) % 4) * 2 + core
        for field in range(3):
            here = 3 * slice_of + field
            value = jnp.where(z_place == 0, early[here, rows, :], late[here, late_rows, :])
            if field == 0:
                value = value - ground[0, rows, :]
            out[C_ROWS * field : C_ROWS * field + C_ROWS, :] = value


def second_sweep(change, rain, ground, early, mine, twin):
    vmem = pl.BlockSpec(memory_space=pltpu.VMEM)
    out = jax.ShapeDtypeStruct((FIELDS, 128), F32)
    return pl.pallas_call(
        second_kernel,
        in_specs=[vmem] * 6,
        out_specs=[vmem] * 4,
        out_shape=(out,) * 4,
        scratch_shapes=[pltpu.VMEM((3 * HALF, NEAR, 128), F32), pltpu.VMEM((3 * NEAR, 128), F32)],
        compiler_params=pltpu.CompilerParams(vmem_limit_bytes=VMEM_LIMIT),
    )(change, rain, ground, early, mine, twin)


def finish_kernel(depth, flux, old, new0, new1, new2, new3, depth_out, flux_out, parts, spread):
    time_place = lax.axis_index("tm")
    x_place = (time_place // 2) % 4
    for d, ref in enumerate((new0, new1, new2, new3)):
        parts[(x_place + 4 - d) % 4] = ref[...]
    lane = lax.broadcasted_iota(jnp.int32, (3 * C_ROWS, 128), 1)
    halves = [jnp.where(lane < 64, turn(parts[b], -32, 1), turn(parts[b + 1], 32, 1)) for b in (0, 2)]
    delta = jnp.concatenate(halves, axis=1) - old[...]
    delta = jnp.where(time_place == 0, 0.0, delta)
    copies = jnp.where(
        lax.broadcasted_iota(jnp.int32, (C_COLS, COLS), 0)
        == lax.broadcasted_iota(jnp.int32, (C_COLS, COLS), 1) // COARSENING,
        1.0,
        0.0,
    ).astype(BF16)
    scale = jnp.where(
        lax.broadcasted_iota(jnp.int32, (3 * C_ROWS, C_COLS), 0) < C_ROWS, 1.0 / SCALE, 1.0 / FLOW_SCALE
    )
    spread[...] = split_dot(scale * delta, copies)
    low = lax.broadcasted_iota(jnp.int32, (8, COLS), 0) < 4
    for field in range(3):
        for k in range(ROWS // 8):
            row = C_ROWS * field + 2 * k
            add = jnp.where(low, spread[row : row + 1, :], spread[row + 1 : row + 2, :])
            rows = slice(8 * k, 8 * k + 8)
            if field == 0:
                depth_out[0, rows, :] = depth[0, rows, :] + add
            else:
                flux_out[0, field - 1, rows, :] = flux[0, field - 1, rows, :] + add


def finish(depth, flux, old, news):
    vmem = pl.BlockSpec(memory_space=pltpu.VMEM)
    return pl.pallas_call(
        finish_kernel,
        in_specs=[vmem] * 7,
        out_specs=[vmem] * 2,
        out_shape=(jax.ShapeDtypeStruct(depth.shape, F32), jax.ShapeDtypeStruct(flux.shape, F32)),
        scratch_shapes=[pltpu.VMEM((4, 3 * C_ROWS, 128), F32), pltpu.VMEM((3 * C_ROWS, COLS), F32)],
        compiler_params=pltpu.CompilerParams(vmem_limit_bytes=VMEM_LIMIT),
    )(depth, flux, old, *news)


def time_route(move):
    route = []
    for source in range(SLICES):
        z, x, core = move(source // 8, (source // 2) % 4, source % 2)
        route.append((source, (z % 2) * 8 + (x % 4) * 2 + core % 2))
    return route


def with_row(values, flip):
    return lax.ppermute(values, "sx", [(i, i ^ flip) for i in range(4)])


def over_x(values, distance):
    return lax.ppermute(values, "tm", time_route(lambda z, x, core: (z, x + distance, core)))


def on_device(
    depth_start, flux_start, elevation, roughness_class, building, manning, radar_rates, tile_index
):
    fields = (depth_start, flux_start, elevation, roughness_class, building)
    first, second, row_a, row_b = pack(*fields)
    first = lax.ppermute(first, "sy", [(0, 1), (1, 0), (2, 3), (3, 2)])
    second = lax.ppermute(second, "sy", [(1, 2), (2, 1)])
    row_a, row_b = with_row(row_a, 1), with_row(row_b, 3)
    size = 6 * HALO
    tops = jnp.concatenate([first[:size], second[:size]], axis=0)
    bottoms = jnp.concatenate([first[size : 2 * size], second[size : 2 * size]], axis=0)
    even_row = lax.axis_index("sx") % 2 == 0
    corner_a = with_row(jnp.where(even_row, bottoms, tops), 1)
    corner_b = with_row(jnp.where(even_row, tops, bottoms), 3)
    *arrays, rain, rates = ready(
        manning, radar_rates, *fields, tile_index, first, second, row_a, row_b
    )
    depth, flux, old, own, *away, ground = fine(manning, corner_a, corner_b, rain, rates, arrays)
    parts = [own] + [over_x(away[d - 1], d) for d in (1, 2, 3)]
    column = jnp.concatenate([part[:FIELDS] for part in parts] + [ground], axis=0)
    mine = jnp.concatenate([column] + [part[FIELDS:] for part in parts], axis=0)
    sibling = time_route(lambda z, x, core: (z, x, core + 1))
    arrays = [mine] + [with_row(column, flip) for flip in (1, 3, 2)]
    arrays = arrays + [lax.ppermute(part, "tm", sibling) for part in arrays]
    change, rain, ground, early, halfway = first_sweep(arrays)
    halfway = lax.ppermute(halfway, "tm", time_route(lambda z, x, core: (z + 1, x, core)))
    twin = lax.ppermute(halfway, "tm", sibling)
    news = second_sweep(change, rain, ground, early, halfway, twin)
    news = [news[0]] + [over_x(news[d], d) for d in (1, 2, 3)]
    return finish(depth, flux, old, news)


def solution(mesh):
    placed = (
        P("tm", "sx", "sy"),
        P("tm", None, "sx", "sy"),
        P("sx", "sy"),
        P("sx", "sy"),
        P("sx", "sy"),
        P(),
        P(),
        P("tm", None, None, None),
    )
    return jax.shard_map(
        on_device,
        mesh=mesh,
        in_specs=placed,
        out_specs=(P("tm", "sx", "sy"), P("tm", None, "sx", "sy")),
        check_vma=False,
    )
```

```python
import math

import jax
import jax.numpy as jnp
from jax import lax
from jax.experimental import pallas as pl
from jax.experimental.pallas import tpu as pltpu
from jax.sharding import PartitionSpec as P

FINE_STEPS = 8
COARSE_STEPS = 2
COARSENING = 4
RAIN_BLOCK = 64
RADAR_TILES = 64
ROUGH_CLASSES = 8
SLICES = 16

GRAVITY = 9.81
DEPTH_FLOOR = 0.05
CELL_SIDE = 2.0
TIME_STEP = 0.25
COARSE_SECONDS = TIME_STEP * FINE_STEPS / COARSE_STEPS
COARSE_SIDE = CELL_SIDE * COARSENING
POWER = -7.0 / 3.0 / math.log(2.0)

COURANT = TIME_STEP / CELL_SIDE
SCALE = COURANT * GRAVITY * TIME_STEP / CELL_SIDE
FLOW_SCALE = SCALE * COURANT
FLOOR = SCALE * DEPTH_FLOOR
FINE_DRAG = GRAVITY * TIME_STEP * SCALE ** (7.0 / 3.0) / FLOW_SCALE
COARSE_DRAG = GRAVITY * COARSE_SECONDS * SCALE ** (7.0 / 3.0) / FLOW_SCALE
CLOSED = 1e30
GROUP = 40

ROWS, COLS = 64, 1024
EDGE = 128
HALO = 8
HIGH, WIDE = ROWS + 2 * HALO, COLS + 2 * EDGE
C_ROWS, C_COLS = ROWS // COARSENING, COLS // COARSENING
C_HIGH, C_WIDE = 32, 384
PART = 3 * C_ROWS // 2
BLOCK = 3 * C_ROWS + 8
F32 = jnp.float32
BF16 = jnp.bfloat16
VMEM_LIMIT = 24 * 1024 * 1024


def face(level, level_next, flux, sill, drag, gate=None):
    raw = jnp.maximum(level, level_next) - sill
    power = jnp.exp2(POWER * jnp.log(jnp.maximum(raw, FLOOR)))
    below = 1.0 + drag * jnp.abs(flux) * power
    inverse = pl.reciprocal(below, approx=True)
    if gate is not None:
        inverse = gate * inverse
    return inverse * (flux - (level_next - level) * jnp.maximum(raw, 0.0))


def split_dot(values, weights, parts=3):
    total = None
    for part in range(parts):
        piece = values.astype(BF16)
        product = jnp.dot(piece, weights, preferred_element_type=F32)
        total = product if total is None else total + product
        if part + 1 < parts:
            values = values - piece.astype(F32)
    return total


def turn(values, shift, axis):
    return pltpu.roll(values, shift % values.shape[axis], axis)


def static_faces(elev, friction, opened, axis, drag):
    sill = jnp.maximum(elev, turn(elev, -1, axis))
    rough = 0.5 * (friction + turn(friction, -1, axis))
    gate = opened * turn(opened, -1, axis)
    return sill, drag * rough * rough, gate


def whole_step(level, flux_x, flux_y, faces_x, faces_y, rain):
    flux_x = face(level, turn(level, -1, 0), flux_x, *faces_x)
    flux_y = face(level, turn(level, -1, 1), flux_y, *faces_y)
    gain = (turn(flux_x, 1, 0) - flux_x) + (turn(flux_y, 1, 1) - flux_y)
    return level + (gain + rain), flux_x, flux_y


def both_sides_step(level, fluxes, faces, rain):
    last_x, next_x, last_y, next_y = fluxes
    fluxes = (
        face(turn(level, 1, 0), level, last_x, *faces[0]),
        face(level, turn(level, -1, 0), next_x, *faces[1]),
        face(turn(level, 1, 1), level, last_y, *faces[2]),
        face(level, turn(level, -1, 1), next_y, *faces[3]),
    )
    gain = (fluxes[0] - fluxes[1]) + (fluxes[2] - fluxes[3])
    return level + (gain + rain), fluxes


def edge_parts(index):
    return (
        (0, HALO, HALO * index),
        (ROWS - HALO, HALO, 6 * HALO + HALO * index),
        (HALO, ROWS - 2 * HALO, 12 * HALO + (ROWS - 2 * HALO) * index),
    )


def pack_kernel(*refs):
    ins, (first, second, row_a, row_b) = refs[:20], refs[20:]
    even = lax.axis_index("sy") % 2 == 0
    even_row = lax.axis_index("sx") % 2 == 0
    index = 0
    for array in range(5):
        left, right, top, bottom = ins[4 * array : 4 * array + 4]
        for lead in (((0,),), ((0, 0), (0, 1)), ((),), ((),), ((),))[array]:
            for row, count, place in edge_parts(index):
                where = lead + (slice(row, row + count), slice(None))
                a, b = left[where].astype(F32), right[where].astype(F32)
                first[place : place + count, :] = jnp.where(even, b, a)
                second[place : place + count, :] = jnp.where(even, a, b)
            here = slice(HALO * index, HALO * index + HALO)
            where = lead + (slice(None), slice(None))
            a, b = top[where].astype(F32), bottom[where].astype(F32)
            row_a[here, :] = jnp.where(even_row, b, a)
            row_b[here, :] = jnp.where(even_row, a, b)
            index += 1


def pack(*fields):
    specs, args = [], []
    for array in fields:
        lead = array.shape[:-2]
        zeros = (0,) * len(lead)
        for shape, place in (
            ((ROWS, EDGE), (0, 0)),
            ((ROWS, EDGE), (0, COLS // EDGE - 1)),
            ((HALO, COLS), (0, 0)),
            ((HALO, COLS), (ROWS // HALO - 1, 0)),
        ):
            specs.append(pl.BlockSpec(lead + shape, lambda i, at=zeros + place: at))
            args.append(array)
    column = jax.ShapeDtypeStruct((6 * ROWS, EDGE), F32)
    row = jax.ShapeDtypeStruct((6 * HALO, COLS), F32)
    return pl.pallas_call(
        pack_kernel,
        grid=(1,),
        in_specs=specs,
        out_specs=[pl.BlockSpec(memory_space=pltpu.VMEM)] * 4,
        out_shape=(column, column, row, row),
    )(*args)


def roughness_of(classes, manning):
    value = jnp.full(classes.shape, manning[0], F32)
    for entry in range(1, ROUGH_CLASSES):
        value = jnp.where(classes == float(entry), manning[entry], value)
    return value


def pool_matrix():
    return jnp.where(
        lax.broadcasted_iota(jnp.int32, (512, 128), 0) // COARSENING
        == lax.broadcasted_iota(jnp.int32, (512, 128), 1),
        1.0 / 16.0,
        0.0,
    ).astype(BF16)


def restrict(sources, take, spans, pooled, coarse):
    pool = pool_matrix()
    high = None
    for part in range(3):
        cols = slice(512 * part, min(512 * part + 512, WIDE))
        values = [take(source, cols) for source in sources]
        high = values[0].shape[0]
        values = jnp.concatenate(values, axis=0)
        pooled[part, 0 : values.shape[0], :] = split_dot(values, pool[0 : values.shape[1], :], 2)
    for slot in range(len(sources)):
        for part in range(3):
            cols = slice(128 * part, 128 * part + 128)
            for target, start, count in spans:
                first = high * slot + start
                total = pooled[part, pl.ds(first, count, stride=4), :]
                for q in range(1, 4):
                    total = total + pooled[part, pl.ds(first + q, count, stride=4), :]
                coarse[slot, target : target + count, cols] = total


def set_faces(k, elev, friction, opened, sill_x, drag_x, sill_y, drag_y):
    rows, after, out = pl.ds(8 + 8 * k, 8), pl.ds(9 + 8 * k, 8), pl.ds(8 * k, 8)
    e, f, o = elev[rows, :], friction[rows, :], opened[rows, :]
    gate = o * opened[after, :]
    sill_x[out, :] = jnp.where(gate > 0.0, jnp.maximum(e, elev[after, :]), CLOSED)
    rough = 0.5 * (f + friction[after, :])
    drag_x[out, :] = FINE_DRAG * rough * rough
    sill, drag_y[out, :], gate = static_faces(e, f, o, 1, FINE_DRAG)
    sill_y[out, :] = jnp.where(gate > 0.0, sill, CLOSED)


def places():
    time_place = lax.axis_index("tm")
    return lax.axis_index("sx"), lax.axis_index("sy"), time_place, (time_place // 2) % 4, time_place % 2


def ready_kernel(
    manning, radar, depth, flux, elevation, roughness, building, tiles, first, second, row_a, row_b,
    level, flow_x, flow_y, elev, friction, opened, sill_x, drag_x, sill_y, drag_y, coarse, rain_s, rates_out,
    index_s, pooled,
):
    row_place, col_place, time_place, x_place, core = places()
    even = col_place % 2 == 0
    odd_row = row_place % 2 == 1
    none = jnp.zeros((HALO, EDGE), F32)

    def fill(target, index, own, scale=1.0):
        target[0:8, :] = jnp.zeros((8, WIDE), F32)
        target[88:96, :] = jnp.zeros((8, WIDE), F32)
        target[16:80, EDGE : EDGE + COLS] = scale * own
        for row, count, place in edge_parts(index):
            rows, a, b = slice(16 + row, 16 + row + count), first[place : place + count], second[place : place + count]
            target[rows, 0:EDGE] = scale * jnp.where(even, b, a)
            target[rows, EDGE + COLS : WIDE] = scale * jnp.where(even, a, b)
        here = slice(index * HALO, index * HALO + HALO)
        for rows, is_first in ((slice(8, 16), odd_row), (slice(80, 88), ~odd_row)):
            target[rows, EDGE : EDGE + COLS] = scale * jnp.where(is_first, row_a[here, :], row_b[here, :])
            target[rows, 0:EDGE] = none
            target[rows, EDGE + COLS : WIDE] = none

    fill(level, 0, depth[0], SCALE)
    fill(flow_x, 1, flux[0, 0], FLOW_SCALE)
    fill(flow_y, 2, flux[0, 1], FLOW_SCALE)
    fill(elev, 3, elevation[...], SCALE)
    fill(friction, 4, roughness[...].astype(F32))
    fill(opened, 5, building[...].astype(F32))

    lane = lax.broadcasted_iota(jnp.int32, (8, WIDE), 1)
    inside = jnp.where(
        ((col_place == 0) & (lane < EDGE)) | ((col_place == 3) & (lane >= EDGE + COLS)), 0.0, 1.0
    )
    for k in range(12):
        here = pl.ds(8 * k, 8)
        friction[here, :] = roughness_of(friction[here, :], manning)
        if k in (0, 11):
            opened[here, :] = jnp.zeros((8, WIDE), F32)
            continue
        free = (1.0 - opened[here, :]) * inside
        if k == 1:
            free = free * jnp.where(row_place == 0, 0.0, 1.0)
        if k == 10:
            free = free * jnp.where(row_place == 3, 0.0, 1.0)
        opened[here, :] = free

    index_s[...] = jnp.full((32, 128), -1, jnp.int32)
    for step in range(FINE_STEPS):
        index_s[4 * step : 4 * step + 4, 0:64] = tiles[0, step]
    index = index_s[...]
    rates = jnp.zeros((32, 128), F32)
    for entry in range(RADAR_TILES):
        rates = jnp.where(index == entry, radar[entry], rates)
    block = lax.broadcasted_iota(jnp.int32, (128, WIDE), 0)
    column = lax.broadcasted_iota(jnp.int32, (128, WIDE), 1) + (COLS * col_place - EDGE)
    rain_s[0:32, :] = (SCALE * TIME_STEP) * split_dot(
        rates, jnp.where((column >> 6) == block, 1.0, 0.0).astype(BF16)
    )
    means = []
    for half in range(COARSE_STEPS):
        part = rates[16 * half : 16 * half + 16, :]
        means.append((0.25 * SCALE * COARSE_SECONDS) * (part[0:4] + part[4:8] + part[8:12] + part[12:16]))
    coarse_rates = jnp.concatenate(means, axis=0)
    rates_out[...] = coarse_rates
    block = lax.broadcasted_iota(jnp.int32, (128, C_WIDE), 0)
    column = lax.broadcasted_iota(jnp.int32, (128, C_WIDE), 1) + (C_COLS * col_place - EDGE // COARSENING)
    padded = jnp.concatenate([coarse_rates, jnp.zeros((8, 128), F32)], axis=0)
    rain_s[32:40, :] = jnp.zeros((8, WIDE), F32)
    rain_s[32:40, 0:C_WIDE] = split_dot(
        padded, jnp.where((column >> 4) == block, 1.0, 0.0).astype(BF16)
    )[0:8]

    coarse[...] = jnp.zeros(coarse.shape, F32)
    sources = (level, flow_x, flow_y, elev, friction, opened)
    restrict(sources, lambda source, cols: source[16:80, cols], ((8, 0, 16),), pooled, coarse)
    for k in range(1, 8):
        set_faces(k, elev, friction, opened, sill_x, drag_x, sill_y, drag_y)


def fine_kernel(*refs):
    manning, corner_a, corner_b, rain_s, rates = refs[:5]
    level, flow_x, flow_y, elev, friction, opened, sill_x, drag_x, sill_y, drag_y, coarse = refs[16:27]
    depth_out, flux_out, old_out, to0, to1, to2, to3, ground_out = refs[27:35]
    pooled, ground_s, windows = refs[35:]
    row_place, col_place, time_place, x_place, core = places()
    even = col_place % 2 == 0
    odd_row = row_place % 2 == 1

    left, right = slice(0, EDGE), slice(EDGE + COLS, WIDE)
    grid_row = (jnp.where(row_place == 0, 0.0, 1.0), jnp.where(row_place == 3, 0.0, 1.0))
    grid_col = (jnp.where(col_place == 0, 0.0, 1.0), jnp.where(col_place == 3, 0.0, 1.0))
    scales = (SCALE, FLOW_SCALE, FLOW_SCALE, SCALE)
    for index, target in enumerate((level, flow_x, flow_y, elev, friction, opened)):
        here = slice(index * HALO, index * HALO + HALO)
        there = slice((6 + index) * HALO, (6 + index) * HALO + HALO)
        for r, (rows, is_first) in enumerate(((slice(8, 16), odd_row), (slice(80, 88), ~odd_row))):
            a = jnp.where(is_first, corner_a[here, :], corner_b[here, :])
            b = jnp.where(is_first, corner_a[there, :], corner_b[there, :])
            for c, (cols, value) in enumerate(((left, jnp.where(even, b, a)), (right, jnp.where(even, a, b)))):
                if index < 4:
                    value = scales[index] * value
                elif index == 4:
                    value = roughness_of(value, manning)
                else:
                    value = (1.0 - value) * (grid_row[r] * grid_col[c])
                target[rows, cols] = value

    sources = (level, flow_x, flow_y, elev, friction, opened)
    take = lambda source, cols: jnp.concatenate([source[8:16, cols], source[80:88, cols]], axis=0)
    restrict(sources, take, ((6, 0, 2), (24, 8, 2)), pooled, coarse)
    for k in (0, 8, 9):
        set_faces(k, elev, friction, opened, sill_x, drag_x, sill_y, drag_y)
    for k in range(10):
        rows, out = pl.ds(8 + 8 * k, 8), pl.ds(8 * k, 8)
        level[rows, :] = level[rows, :] + elev[rows, :]
        flow_x[rows, :] = jnp.where(sill_x[out, :] < CLOSED, flow_x[rows, :], 0.0)
        flow_y[rows, :] = jnp.where(sill_y[out, :] < CLOSED, flow_y[rows, :], 0.0)
    row_above = jnp.maximum(row_place - 1, 0)
    row_below = jnp.minimum(row_place + 1, 3)

    sub = lax.broadcasted_iota(jnp.int32, (GROUP, WIDE), 0)

    def fine_step(step, carry):
        rains = [rain_s[pl.ds(4 * step + place, 1), :] for place in (row_above, row_place, row_below)]
        now = level[8 : 8 + GROUP, :]
        up = turn(now, -1, 0)
        after, up_after, west = now, up, now
        for k in range(HIGH // GROUP):
            out = slice(GROUP * k, GROUP * k + GROUP)
            rows = slice(8 + GROUP * k, 8 + GROUP * k + GROUP)
            if k + 1 < HIGH // GROUP:
                after = level[8 + GROUP * k + GROUP : 8 + 2 * GROUP + GROUP * k, :]
                up_after = turn(after, -1, 0)
            north = jnp.where(sub == GROUP - 1, up_after, up)
            qx = face(now, north, flow_x[rows, :], sill_x[out, :], drag_x[out, :])
            qy = face(now, turn(now, -1, 1), flow_y[rows, :], sill_y[out, :], drag_y[out, :])
            flow_x[rows, :] = qx
            flow_y[rows, :] = qy
            down = turn(qx, 1, 0)
            gain = (jnp.where(sub == 0, west, down) - qx) + (turn(qy, 1, 1) - qy)
            rain = rains[1]
            if k == 0:
                rain = jnp.where(sub < HALO, rains[0], rain)
            if k + 1 == HIGH // GROUP:
                rain = jnp.where(sub >= GROUP - HALO, rains[2], rain)
            level[rows, :] = now + (gain + rain)
            now, up, west = after, up_after, down
        return carry

    lax.fori_loop(0, FINE_STEPS, fine_step, 0, unroll=True)

    c_elev, c_friction, c_open = coarse[3], coarse[4], coarse[5]
    faces_x = static_faces(c_elev, c_friction, c_open, 0, COARSE_DRAG)
    faces_y = static_faces(c_elev, c_friction, c_open, 1, COARSE_DRAG)
    state = (coarse[0] + c_elev, coarse[1], coarse[2])
    row = lax.broadcasted_iota(jnp.int32, (C_HIGH, C_WIDE), 0)
    for step in range(COARSE_STEPS):
        parts = [rain_s[pl.ds(32 + 4 * step + place, 1), 0:C_WIDE] for place in (row_above, row_place, row_below)]
        rain = jnp.where(row < 8, parts[0], jnp.where(row < 24, parts[1], parts[2]))
        state = whole_step(*state, faces_x, faces_y, rain)
    old = (state[0] - c_elev, state[1], state[2])

    for k in range(10):
        rows = pl.ds(8 + 8 * k, 8)
        level[rows, :] = level[rows, :] - elev[rows, :]
    own = (slice(16, 80), slice(EDGE, EDGE + COLS))
    depth_out[0] = (1.0 / SCALE) * level[own]
    flux_out[0, 0] = (1.0 / FLOW_SCALE) * flow_x[own]
    flux_out[0, 1] = (1.0 / FLOW_SCALE) * flow_y[own]
    sources = (level, flow_x, flow_y)
    restrict(sources, lambda source, cols: source[16:80, cols], ((8, 0, 16),), pooled, coarse)
    factor = jnp.where(time_place == 0, 0.0, 1.0)
    side = EDGE // COARSENING
    outs = (to0, to1, to2, to3)
    for slot in range(3):
        mine = old[slot][8:24, :]
        old_out[C_ROWS * slot : C_ROWS * slot + C_ROWS, :] = turn(mine, -side, 1)[:, 0:C_COLS]
        value = coarse[slot, 8:24, :] - factor * mine
        fixed = coarse[3 + slot, 8:24, :]
        here = slice(C_ROWS * slot, C_ROWS * slot + C_ROWS)
        for odd, (now, ground_now) in enumerate(((value, fixed), (turn(value, -64, 1), turn(fixed, -64, 1)))):
            for half in range(2):
                cols = slice(128 * half, 128 * half + 128)
                windows[2 * half + odd, here, :] = now[:, cols]
                ground_s[2 * half + odd, here, :] = ground_now[:, cols]
    ground_out[...] = ground_s[x_place, pl.ds(pl.multiple_of(core * PART, PART), PART), :]
    for d, out in enumerate(outs):
        out[0 : 3 * C_ROWS, :] = windows[(x_place + d) % 4]
        out[3 * C_ROWS : BLOCK, :] = rates[...]


def ready(manning, radar, *rest):
    smem = pl.BlockSpec(memory_space=pltpu.SMEM)
    vmem = pl.BlockSpec(memory_space=pltpu.VMEM)
    padded = jax.ShapeDtypeStruct((HIGH + 16, WIDE), F32)
    faces = jax.ShapeDtypeStruct((HIGH, WIDE), F32)
    coarse = jax.ShapeDtypeStruct((6, C_HIGH, C_WIDE), F32)
    rain = jax.ShapeDtypeStruct((40, WIDE), F32)
    rates = jax.ShapeDtypeStruct((8, 128), F32)
    return pl.pallas_call(
        ready_kernel,
        in_specs=[smem, smem] + [vmem] * 10,
        out_specs=[vmem] * 13,
        out_shape=[padded] * 6 + [faces] * 4 + [coarse, rain, rates],
        scratch_shapes=[pltpu.VMEM((32, 128), jnp.int32), pltpu.VMEM((3, 6 * ROWS, 128), F32)],
        cost_estimate=pl.CostEstimate(flops=40_000_000, bytes_accessed=10_000_000, transcendentals=0),
        compiler_params=pltpu.CompilerParams(vmem_limit_bytes=VMEM_LIMIT),
    )(manning, radar, *rest)


def fine(manning, corner_a, corner_b, rain, rates, arrays):
    smem = pl.BlockSpec(memory_space=pltpu.SMEM)
    vmem = pl.BlockSpec(memory_space=pltpu.VMEM)
    message = jax.ShapeDtypeStruct((BLOCK, 128), F32)
    shapes = [jax.ShapeDtypeStruct(array.shape, F32) for array in arrays]
    return pl.pallas_call(
        fine_kernel,
        in_specs=[smem] + [vmem] * 15,
        out_specs=[vmem] * 19,
        out_shape=shapes
        + [
            jax.ShapeDtypeStruct((1, ROWS, COLS), F32),
            jax.ShapeDtypeStruct((1, 2, ROWS, COLS), F32),
            jax.ShapeDtypeStruct((3 * C_ROWS, C_COLS), F32),
            message,
            message,
            message,
            message,
            jax.ShapeDtypeStruct((PART, 128), F32),
        ],
        input_output_aliases={5 + place: place for place in range(11)},
        scratch_shapes=[
            pltpu.VMEM((3, 3 * ROWS, 128), F32),
            pltpu.VMEM((4, 3 * C_ROWS, 128), F32),
            pltpu.VMEM((4, 3 * C_ROWS, 128), F32),
        ],
        compiler_params=pltpu.CompilerParams(vmem_limit_bytes=VMEM_LIMIT),
    )(manning, corner_a, corner_b, rain, rates, *arrays)[11:]


HALF = SLICES // 2
TALL = 4 * C_ROWS
NEAR = 3 * C_ROWS
FIELDS = 3 * C_ROWS


def sweep_faces(ground):
    sill, drag, gate = static_faces(*ground, 0, COARSE_DRAG)
    last = lax.broadcasted_iota(jnp.int32, gate.shape, 0) == gate.shape[0] - 1
    gate = jnp.where(last, 0.0, gate)
    faces_x, faces_y = (sill, drag, gate), static_faces(*ground, 1, COARSE_DRAG)
    moved_x = tuple(turn(part, 1, 0) for part in faces_x)
    moved_y = tuple(turn(part, 1, 1) for part in faces_y)
    return moved_x, faces_x, moved_y, faces_y


def near_start(row_place):
    return pl.multiple_of(C_ROWS * jnp.clip(row_place - 1, 0, 1), C_ROWS)


def sweep_slices(first, state, change, rain, ground, newest, top, high):
    faces = sweep_faces(ground)
    rows = pl.ds(top, high)
    level, flux_x, flux_y = state
    fluxes = (turn(flux_x, 1, 0), flux_x, turn(flux_y, 1, 1), flux_y)

    for moment in range(first, HALF):
        for step in range(COARSE_STEPS):
            wet = jnp.concatenate(
                [
                    jnp.broadcast_to(
                        rain[pl.ds(8 * moment + 4 * step + top // C_ROWS + b, 1), :], (C_ROWS, 128)
                    )
                    for b in range(high // C_ROWS)
                ],
                axis=0,
            )
            level, fluxes = both_sides_step(level, fluxes, faces, wet)
        for field, value in enumerate((level, fluxes[1], fluxes[3])):
            newest[3 * moment + field, 0:high, :] = value
        add, add_x, add_y = (change[3 * moment + field, rows, :] for field in range(3))
        level = level + add
        fluxes = (
            fluxes[0] + turn(add_x, 1, 0), fluxes[1] + add_x, fluxes[2] + turn(add_y, 1, 1), fluxes[3] + add_y
        )
    return level, fluxes[1], fluxes[3]


def first_kernel(*refs):
    ins, (change, rain, ground, newest, halfway), (rates, state_s, all_s, parts_s) = refs[:8], refs[8:13], refs[13:]
    row_place = lax.axis_index("sx")
    col_place = lax.axis_index("sy")
    time_place = lax.axis_index("tm")
    z_place, x_place, core = time_place // 8, (time_place // 2) % 4, time_place % 2

    for other in range(2):
        for e in range(4):
            ref = ins[4 * other + e]
            source = (row_place, row_place + 1 - 2 * (row_place % 2), 3 - row_place, (row_place + 2) % 4)[e]
            start = pl.multiple_of(C_ROWS * source, C_ROWS)
            rows = pl.ds(start, C_ROWS)
            for d in range(4):
                slice_of = ((x_place + 4 - d) % 4) * 2 + (core + other) % 2
                for field in range(3):
                    base = FIELDS * d + C_ROWS * field
                    change[3 * slice_of + field, rows, :] = ref[base : base + C_ROWS, :]
                if e == 0:
                    base = 4 * FIELDS + PART + 8 * d
                    rates[pl.ds(pl.multiple_of(8 * slice_of, 8), 8), :] = ref[base : base + 8, :]
            half = (core + other) % 2
            base = 4 * FIELDS
            parts_s[pl.ds(pl.multiple_of(half * PART, PART), PART), :] = ref[base : base + PART, :]
            if other == 1:
                twin = ins[e]
                parts_s[pl.ds(pl.multiple_of(core * PART, PART), PART), :] = twin[base : base + PART, :]
                for field in range(3):
                    ground[field, rows, :] = parts_s[C_ROWS * field : C_ROWS * field + C_ROWS, :]

    block = lax.broadcasted_iota(jnp.int32, (128, 128), 0)
    column = lax.broadcasted_iota(jnp.int32, (128, 128), 1)
    column = column + (C_COLS * col_place + 64 * x_place - EDGE // COARSENING)
    rain[...] = split_dot(rates[...], jnp.where((column >> 4) == block, 1.0, 0.0).astype(BF16))

    all_s[...] = jnp.zeros(all_s.shape, F32)

    @pl.when(z_place == 0)
    def _():
        fixed = (ground[0], ground[1], ground[2])
        state = (change[0] + ground[0], change[1], change[2])
        state = sweep_slices(1, state, change, rain, fixed, newest, 0, TALL)
        for field in range(3):
            all_s[field] = state[field]

    near = pl.ds(near_start(row_place), NEAR)
    for field in range(3):
        state_s[NEAR * field : NEAR * field + NEAR, :] = all_s[field, near, :]
    lane = lax.broadcasted_iota(jnp.int32, (C_ROWS, 128), 1)
    pieces = [state_s[C_ROWS * k : C_ROWS * k + C_ROWS, :] for k in range(9)]
    for k in range(6):
        guest = turn(pieces[6 + k // 3], 80 - 32 * (k % 3), 1)
        halfway[C_ROWS * k : C_ROWS * k + C_ROWS, :] = jnp.where(lane < 96, turn(pieces[k], -16, 1), guest)
    halfway[6 * C_ROWS : 7 * C_ROWS, :] = turn(pieces[8], -16, 1)


def first_sweep(arrays):
    vmem = pl.BlockSpec(memory_space=pltpu.VMEM)
    field = jax.ShapeDtypeStruct((3 * HALF, TALL, 128), F32)
    return pl.pallas_call(
        first_kernel,
        in_specs=[vmem] * 8,
        out_specs=[vmem] * 5,
        out_shape=(
            field,
            jax.ShapeDtypeStruct((8 * HALF, 128), F32),
            jax.ShapeDtypeStruct((3, TALL, 128), F32),
            field,
            jax.ShapeDtypeStruct((7 * C_ROWS, 128), F32),
        ),
        scratch_shapes=[
            pltpu.VMEM((8 * HALF, 128), F32),
            pltpu.VMEM((3 * NEAR, 128), F32),
            pltpu.VMEM((3, TALL, 128), F32),
            pltpu.VMEM((3 * C_ROWS, 128), F32),
        ],
        compiler_params=pltpu.CompilerParams(vmem_limit_bytes=VMEM_LIMIT),
    )(*arrays)


def second_kernel(change, rain, ground, early, halfway, out0, out1, out2, out3, late, state_s):
    row_place = lax.axis_index("sx")
    time_place = lax.axis_index("tm")
    z_place, x_place, core = time_place // 8, (time_place // 2) % 4, time_place % 2
    top = near_start(row_place)

    @pl.when(z_place == 1)
    def _():
        lane = lax.broadcasted_iota(jnp.int32, (C_ROWS, 128), 1)
        pieces = [halfway[C_ROWS * k : C_ROWS * k + C_ROWS, :] for k in range(7)]
        for k in range(6):
            state_s[C_ROWS * k : C_ROWS * k + C_ROWS, :] = turn(pieces[k], 16, 1)
        for k in range(2):
            a, b, c = (turn(pieces[3 * k + part], 32 * part - 80, 1) for part in range(3))
            value = jnp.where(lane < 48, a, jnp.where(lane < 80, b, c))
            state_s[C_ROWS * (6 + k) : C_ROWS * (7 + k), :] = value
        state_s[8 * C_ROWS : 9 * C_ROWS, :] = turn(pieces[6], 16, 1)
        state = tuple(state_s[NEAR * field : NEAR * field + NEAR, :] for field in range(3))
        fixed = tuple(ground[field, pl.ds(top, NEAR), :] for field in range(3))
        sweep_slices(0, state, change, rain, fixed, late, top, NEAR)

    rows = pl.ds(pl.multiple_of(C_ROWS * row_place, C_ROWS), C_ROWS)
    late_rows = pl.ds(pl.multiple_of(C_ROWS * row_place - top, C_ROWS), C_ROWS)
    for d, out in enumerate((out0, out1, out2, out3)):
        slice_of = ((x_place + d) % 4) * 2 + core
        for field in range(3):
            here = 3 * slice_of + field
            value = jnp.where(z_place == 0, early[here, rows, :], late[here, late_rows, :])
            if field == 0:
                value = value - ground[0, rows, :]
            out[C_ROWS * field : C_ROWS * field + C_ROWS, :] = value


def second_sweep(change, rain, ground, early, halfway):
    vmem = pl.BlockSpec(memory_space=pltpu.VMEM)
    out = jax.ShapeDtypeStruct((FIELDS, 128), F32)
    return pl.pallas_call(
        second_kernel,
        in_specs=[vmem] * 5,
        out_specs=[vmem] * 4,
        out_shape=(out,) * 4,
        scratch_shapes=[pltpu.VMEM((3 * HALF, NEAR, 128), F32), pltpu.VMEM((3 * NEAR, 128), F32)],
        compiler_params=pltpu.CompilerParams(vmem_limit_bytes=VMEM_LIMIT),
    )(change, rain, ground, early, halfway)


def finish_kernel(depth, flux, old, new0, new1, new2, new3, depth_out, flux_out, parts, spread):
    time_place = lax.axis_index("tm")
    x_place = (time_place // 2) % 4
    for d, ref in enumerate((new0, new1, new2, new3)):
        parts[(x_place + 4 - d) % 4] = ref[...]
    lane = lax.broadcasted_iota(jnp.int32, (3 * C_ROWS, 128), 1)
    halves = [jnp.where(lane < 64, turn(parts[b], -32, 1), turn(parts[b + 1], 32, 1)) for b in (0, 2)]
    delta = jnp.concatenate(halves, axis=1) - old[...]
    delta = jnp.where(time_place == 0, 0.0, delta)
    copies = jnp.where(
        lax.broadcasted_iota(jnp.int32, (C_COLS, COLS), 0)
        == lax.broadcasted_iota(jnp.int32, (C_COLS, COLS), 1) // COARSENING,
        1.0,
        0.0,
    ).astype(BF16)
    scale = jnp.where(
        lax.broadcasted_iota(jnp.int32, (3 * C_ROWS, C_COLS), 0) < C_ROWS, 1.0 / SCALE, 1.0 / FLOW_SCALE
    )
    spread[...] = split_dot(scale * delta, copies)
    low = lax.broadcasted_iota(jnp.int32, (8, COLS), 0) < 4
    for field in range(3):
        for k in range(ROWS // 8):
            row = C_ROWS * field + 2 * k
            add = jnp.where(low, spread[row : row + 1, :], spread[row + 1 : row + 2, :])
            rows = slice(8 * k, 8 * k + 8)
            if field == 0:
                depth_out[0, rows, :] = depth[0, rows, :] + add
            else:
                flux_out[0, field - 1, rows, :] = flux[0, field - 1, rows, :] + add


def finish(depth, flux, old, news):
    vmem = pl.BlockSpec(memory_space=pltpu.VMEM)
    return pl.pallas_call(
        finish_kernel,
        in_specs=[vmem] * 7,
        out_specs=[vmem] * 2,
        out_shape=(jax.ShapeDtypeStruct(depth.shape, F32), jax.ShapeDtypeStruct(flux.shape, F32)),
        scratch_shapes=[pltpu.VMEM((4, 3 * C_ROWS, 128), F32), pltpu.VMEM((3 * C_ROWS, COLS), F32)],
        compiler_params=pltpu.CompilerParams(vmem_limit_bytes=VMEM_LIMIT),
    )(depth, flux, old, *news)


def time_route(move):
    route = []
    for source in range(SLICES):
        z, x, core = move(source // 8, (source // 2) % 4, source % 2)
        route.append((source, (z % 2) * 8 + (x % 4) * 2 + core % 2))
    return route


def with_row(values, flip):
    return lax.ppermute(values, "sx", [(i, i ^ flip) for i in range(4)])


def over_x(values, distance):
    return lax.ppermute(values, "tm", time_route(lambda z, x, core: (z, x + distance, core)))


def on_device(
    depth_start, flux_start, elevation, roughness_class, building, manning, radar_rates, tile_index
):
    fields = (depth_start, flux_start, elevation, roughness_class, building)
    first, second, row_a, row_b = pack(*fields)
    first = lax.ppermute(first, "sy", [(0, 1), (1, 0), (2, 3), (3, 2)])
    second = lax.ppermute(second, "sy", [(1, 2), (2, 1)])
    row_a, row_b = with_row(row_a, 1), with_row(row_b, 3)
    size = 6 * HALO
    tops = jnp.concatenate([first[:size], second[:size]], axis=0)
    bottoms = jnp.concatenate([first[size : 2 * size], second[size : 2 * size]], axis=0)
    even_row = lax.axis_index("sx") % 2 == 0
    corner_a = with_row(jnp.where(even_row, bottoms, tops), 1)
    corner_b = with_row(jnp.where(even_row, tops, bottoms), 3)
    *arrays, rain, rates = ready(
        manning, radar_rates, *fields, tile_index, first, second, row_a, row_b
    )
    depth, flux, old, own, *away, ground = fine(manning, corner_a, corner_b, rain, rates, arrays)
    parts = [own] + [over_x(away[d - 1], d) for d in (1, 2, 3)]
    column = jnp.concatenate([part[:FIELDS] for part in parts] + [ground], axis=0)
    mine = jnp.concatenate([column] + [part[FIELDS:] for part in parts], axis=0)
    sibling = time_route(lambda z, x, core: (z, x, core + 1))
    arrays = [mine] + [with_row(column, flip) for flip in (1, 3, 2)]
    arrays = arrays + [lax.ppermute(part, "tm", sibling) for part in arrays]
    change, rain, ground, early, halfway = first_sweep(arrays)
    halfway = lax.ppermute(halfway, "tm", time_route(lambda z, x, core: (z + 1, x, core)))
    news = second_sweep(change, rain, ground, early, halfway)
    news = [news[0]] + [over_x(news[d], d) for d in (1, 2, 3)]
    return finish(depth, flux, old, news)


def solution(mesh):
    placed = (
        P("tm", "sx", "sy"),
        P("tm", None, "sx", "sy"),
        P("sx", "sy"),
        P("sx", "sy"),
        P("sx", "sy"),
        P(),
        P(),
        P("tm", None, None, None),
    )
    return jax.shard_map(
        on_device,
        mesh=mesh,
        in_specs=placed,
        out_specs=(P("tm", "sx", "sy"), P("tm", None, "sx", "sy")),
        check_vma=False,
    )
```

```python
import math

import jax
import jax.numpy as jnp
from jax import lax
from jax.experimental import pallas as pl
from jax.experimental.pallas import tpu as pltpu
from jax.sharding import PartitionSpec as P

FINE_STEPS = 8
COARSE_STEPS = 2
COARSENING = 4
RAIN_BLOCK = 64
RADAR_TILES = 64
ROUGH_CLASSES = 8
SLICES = 16

GRAVITY = 9.81
DEPTH_FLOOR = 0.05
CELL_SIDE = 2.0
TIME_STEP = 0.25
COARSE_SECONDS = TIME_STEP * FINE_STEPS / COARSE_STEPS
COARSE_SIDE = CELL_SIDE * COARSENING
POWER = -7.0 / 3.0 / math.log(2.0)

COURANT = TIME_STEP / CELL_SIDE
SCALE = COURANT * GRAVITY * TIME_STEP / CELL_SIDE
FLOW_SCALE = SCALE * COURANT
FLOOR = SCALE * DEPTH_FLOOR
FINE_DRAG = GRAVITY * TIME_STEP * SCALE ** (7.0 / 3.0) / FLOW_SCALE
COARSE_DRAG = GRAVITY * COARSE_SECONDS * SCALE ** (7.0 / 3.0) / FLOW_SCALE
CLOSED = 1e30
GROUP = 40

ROWS, COLS = 64, 1024
EDGE = 128
HALO = 8
HIGH, WIDE = ROWS + 2 * HALO, COLS + 2 * EDGE
C_ROWS, C_COLS = ROWS // COARSENING, COLS // COARSENING
C_HIGH, C_WIDE = 32, 384
PART = 3 * C_ROWS // 2
BLOCK = 3 * C_ROWS + 8
F32 = jnp.float32
BF16 = jnp.bfloat16
VMEM_LIMIT = 24 * 1024 * 1024


def face(level, level_next, flux, sill, drag, gate=None):
    raw = jnp.maximum(level, level_next) - sill
    power = jnp.exp2(POWER * jnp.log(jnp.maximum(raw, FLOOR)))
    below = 1.0 + drag * jnp.abs(flux) * power
    inverse = pl.reciprocal(below, approx=True)
    if gate is not None:
        inverse = gate * inverse
    return inverse * (flux - (level_next - level) * jnp.maximum(raw, 0.0))


def split_dot(values, weights, parts=3):
    total = None
    for part in range(parts):
        piece = values.astype(BF16)
        product = jnp.dot(piece, weights, preferred_element_type=F32)
        total = product if total is None else total + product
        if part + 1 < parts:
            values = values - piece.astype(F32)
    return total


def turn(values, shift, axis):
    return pltpu.roll(values, shift % values.shape[axis], axis)


def static_faces(elev, friction, opened, axis, drag):
    sill = jnp.maximum(elev, turn(elev, -1, axis))
    rough = 0.5 * (friction + turn(friction, -1, axis))
    gate = opened * turn(opened, -1, axis)
    return sill, drag * rough * rough, gate


def whole_step(level, flux_x, flux_y, faces_x, faces_y, rain):
    flux_x = face(level, turn(level, -1, 0), flux_x, *faces_x)
    flux_y = face(level, turn(level, -1, 1), flux_y, *faces_y)
    gain = (turn(flux_x, 1, 0) - flux_x) + (turn(flux_y, 1, 1) - flux_y)
    return level + (gain + rain), flux_x, flux_y


def both_sides_step(level, fluxes, faces, rain):
    last_x, next_x, last_y, next_y = fluxes
    fluxes = (
        face(turn(level, 1, 0), level, last_x, *faces[0]),
        face(level, turn(level, -1, 0), next_x, *faces[1]),
        face(turn(level, 1, 1), level, last_y, *faces[2]),
        face(level, turn(level, -1, 1), next_y, *faces[3]),
    )
    gain = (fluxes[0] - fluxes[1]) + (fluxes[2] - fluxes[3])
    return level + (gain + rain), fluxes


def edge_parts(index):
    return (
        (0, HALO, HALO * index),
        (ROWS - HALO, HALO, 6 * HALO + HALO * index),
        (HALO, ROWS - 2 * HALO, 12 * HALO + (ROWS - 2 * HALO) * index),
    )


def pack_kernel(*refs):
    ins, (first, second, row_a, row_b) = refs[:20], refs[20:]
    even = lax.axis_index("sy") % 2 == 0
    even_row = lax.axis_index("sx") % 2 == 0
    index = 0
    for array in range(5):
        left, right, top, bottom = ins[4 * array : 4 * array + 4]
        for lead in (((0,),), ((0, 0), (0, 1)), ((),), ((),), ((),))[array]:
            for row, count, place in edge_parts(index):
                where = lead + (slice(row, row + count), slice(None))
                a, b = left[where].astype(F32), right[where].astype(F32)
                first[place : place + count, :] = jnp.where(even, b, a)
                second[place : place + count, :] = jnp.where(even, a, b)
            here = slice(HALO * index, HALO * index + HALO)
            where = lead + (slice(None), slice(None))
            a, b = top[where].astype(F32), bottom[where].astype(F32)
            row_a[here, :] = jnp.where(even_row, b, a)
            row_b[here, :] = jnp.where(even_row, a, b)
            index += 1


def pack(*fields):
    specs, args = [], []
    for array in fields:
        lead = array.shape[:-2]
        zeros = (0,) * len(lead)
        for shape, place in (
            ((ROWS, EDGE), (0, 0)),
            ((ROWS, EDGE), (0, COLS // EDGE - 1)),
            ((HALO, COLS), (0, 0)),
            ((HALO, COLS), (ROWS // HALO - 1, 0)),
        ):
            specs.append(pl.BlockSpec(lead + shape, lambda i, at=zeros + place: at))
            args.append(array)
    column = jax.ShapeDtypeStruct((6 * ROWS, EDGE), F32)
    row = jax.ShapeDtypeStruct((6 * HALO, COLS), F32)
    return pl.pallas_call(
        pack_kernel,
        grid=(1,),
        in_specs=specs,
        out_specs=[pl.BlockSpec(memory_space=pltpu.VMEM)] * 4,
        out_shape=(column, column, row, row),
    )(*args)


def roughness_of(classes, manning):
    value = jnp.full(classes.shape, manning[0], F32)
    for entry in range(1, ROUGH_CLASSES):
        value = jnp.where(classes == float(entry), manning[entry], value)
    return value


def pool_matrix():
    return jnp.where(
        lax.broadcasted_iota(jnp.int32, (512, 128), 0) // COARSENING
        == lax.broadcasted_iota(jnp.int32, (512, 128), 1),
        1.0 / 16.0,
        0.0,
    ).astype(BF16)


def restrict(sources, take, spans, pooled, coarse):
    pool = pool_matrix()
    high = None
    for part in range(3):
        cols = slice(512 * part, min(512 * part + 512, WIDE))
        values = [take(source, cols) for source in sources]
        high = values[0].shape[0]
        values = jnp.concatenate(values, axis=0)
        pooled[part, 0 : values.shape[0], :] = split_dot(values, pool[0 : values.shape[1], :], 2)
    for slot in range(len(sources)):
        for part in range(3):
            cols = slice(128 * part, 128 * part + 128)
            for target, start, count in spans:
                first = high * slot + start
                total = pooled[part, pl.ds(first, count, stride=4), :]
                for q in range(1, 4):
                    total = total + pooled[part, pl.ds(first + q, count, stride=4), :]
                coarse[slot, target : target + count, cols] = total


def set_faces(k, elev, friction, opened, sill_x, drag_x, sill_y, drag_y):
    rows, after, out = pl.ds(8 + 8 * k, 8), pl.ds(9 + 8 * k, 8), pl.ds(8 * k, 8)
    e, f, o = elev[rows, :], friction[rows, :], opened[rows, :]
    gate = o * opened[after, :]
    sill_x[out, :] = jnp.where(gate > 0.0, jnp.maximum(e, elev[after, :]), CLOSED)
    rough = 0.5 * (f + friction[after, :])
    drag_x[out, :] = FINE_DRAG * rough * rough
    sill, drag_y[out, :], gate = static_faces(e, f, o, 1, FINE_DRAG)
    sill_y[out, :] = jnp.where(gate > 0.0, sill, CLOSED)


def places():
    time_place = lax.axis_index("tm")
    return lax.axis_index("sx"), lax.axis_index("sy"), time_place, (time_place // 2) % 4, time_place % 2


def ready_kernel(
    manning, radar, depth, flux, elevation, roughness, building, tiles, first, second, row_a, row_b,
    level, flow_x, flow_y, elev, friction, opened, sill_x, drag_x, sill_y, drag_y, coarse, rain_s, rates_out,
    index_s, pooled,
):
    row_place, col_place, time_place, x_place, core = places()
    even = col_place % 2 == 0
    odd_row = row_place % 2 == 1
    none = jnp.zeros((HALO, EDGE), F32)

    def fill(target, index, own, scale=1.0):
        target[0:8, :] = jnp.zeros((8, WIDE), F32)
        target[88:96, :] = jnp.zeros((8, WIDE), F32)
        target[16:80, EDGE : EDGE + COLS] = scale * own
        for row, count, place in edge_parts(index):
            rows, a, b = slice(16 + row, 16 + row + count), first[place : place + count], second[place : place + count]
            target[rows, 0:EDGE] = scale * jnp.where(even, b, a)
            target[rows, EDGE + COLS : WIDE] = scale * jnp.where(even, a, b)
        here = slice(index * HALO, index * HALO + HALO)
        for rows, is_first in ((slice(8, 16), odd_row), (slice(80, 88), ~odd_row)):
            target[rows, EDGE : EDGE + COLS] = scale * jnp.where(is_first, row_a[here, :], row_b[here, :])
            target[rows, 0:EDGE] = none
            target[rows, EDGE + COLS : WIDE] = none

    fill(level, 0, depth[0], SCALE)
    fill(flow_x, 1, flux[0, 0], FLOW_SCALE)
    fill(flow_y, 2, flux[0, 1], FLOW_SCALE)
    fill(elev, 3, elevation[...], SCALE)
    fill(friction, 4, roughness[...].astype(F32))
    fill(opened, 5, building[...].astype(F32))

    lane = lax.broadcasted_iota(jnp.int32, (8, WIDE), 1)
    inside = jnp.where(
        ((col_place == 0) & (lane < EDGE)) | ((col_place == 3) & (lane >= EDGE + COLS)), 0.0, 1.0
    )
    for k in range(12):
        here = pl.ds(8 * k, 8)
        friction[here, :] = roughness_of(friction[here, :], manning)
        if k in (0, 11):
            opened[here, :] = jnp.zeros((8, WIDE), F32)
            continue
        free = (1.0 - opened[here, :]) * inside
        if k == 1:
            free = free * jnp.where(row_place == 0, 0.0, 1.0)
        if k == 10:
            free = free * jnp.where(row_place == 3, 0.0, 1.0)
        opened[here, :] = free

    index_s[...] = jnp.full((32, 128), -1, jnp.int32)
    for step in range(FINE_STEPS):
        index_s[4 * step : 4 * step + 4, 0:64] = tiles[0, step]
    index = index_s[...]
    rates = jnp.zeros((32, 128), F32)
    for entry in range(RADAR_TILES):
        rates = jnp.where(index == entry, radar[entry], rates)
    block = lax.broadcasted_iota(jnp.int32, (128, WIDE), 0)
    column = lax.broadcasted_iota(jnp.int32, (128, WIDE), 1) + (COLS * col_place - EDGE)
    rain_s[0:32, :] = (SCALE * TIME_STEP) * split_dot(
        rates, jnp.where((column >> 6) == block, 1.0, 0.0).astype(BF16)
    )
    means = []
    for half in range(COARSE_STEPS):
        part = rates[16 * half : 16 * half + 16, :]
        means.append((0.25 * SCALE * COARSE_SECONDS) * (part[0:4] + part[4:8] + part[8:12] + part[12:16]))
    coarse_rates = jnp.concatenate(means, axis=0)
    rates_out[...] = coarse_rates
    block = lax.broadcasted_iota(jnp.int32, (128, C_WIDE), 0)
    column = lax.broadcasted_iota(jnp.int32, (128, C_WIDE), 1) + (C_COLS * col_place - EDGE // COARSENING)
    padded = jnp.concatenate([coarse_rates, jnp.zeros((8, 128), F32)], axis=0)
    rain_s[32:40, :] = jnp.zeros((8, WIDE), F32)
    rain_s[32:40, 0:C_WIDE] = split_dot(
        padded, jnp.where((column >> 4) == block, 1.0, 0.0).astype(BF16)
    )[0:8]

    coarse[...] = jnp.zeros(coarse.shape, F32)
    sources = (level, flow_x, flow_y, elev, friction, opened)
    restrict(sources, lambda source, cols: source[16:80, cols], ((8, 0, 16),), pooled, coarse)
    for k in range(1, 8):
        set_faces(k, elev, friction, opened, sill_x, drag_x, sill_y, drag_y)


def fine_kernel(*refs):
    manning, corner_a, corner_b, rain_s, rates = refs[:5]
    level, flow_x, flow_y, elev, friction, opened, sill_x, drag_x, sill_y, drag_y, coarse = refs[16:27]
    depth_out, flux_out, old_out, to0, to1, to2, to3, ground_out = refs[27:35]
    pooled, ground_s, windows = refs[35:]
    row_place, col_place, time_place, x_place, core = places()
    even = col_place % 2 == 0
    odd_row = row_place % 2 == 1

    left, right = slice(0, EDGE), slice(EDGE + COLS, WIDE)
    grid_row = (jnp.where(row_place == 0, 0.0, 1.0), jnp.where(row_place == 3, 0.0, 1.0))
    grid_col = (jnp.where(col_place == 0, 0.0, 1.0), jnp.where(col_place == 3, 0.0, 1.0))
    scales = (SCALE, FLOW_SCALE, FLOW_SCALE, SCALE)
    for index, target in enumerate((level, flow_x, flow_y, elev, friction, opened)):
        here = slice(index * HALO, index * HALO + HALO)
        there = slice((6 + index) * HALO, (6 + index) * HALO + HALO)
        for r, (rows, is_first) in enumerate(((slice(8, 16), odd_row), (slice(80, 88), ~odd_row))):
            a = jnp.where(is_first, corner_a[here, :], corner_b[here, :])
            b = jnp.where(is_first, corner_a[there, :], corner_b[there, :])
            for c, (cols, value) in enumerate(((left, jnp.where(even, b, a)), (right, jnp.where(even, a, b)))):
                if index < 4:
                    value = scales[index] * value
                elif index == 4:
                    value = roughness_of(value, manning)
                else:
                    value = (1.0 - value) * (grid_row[r] * grid_col[c])
                target[rows, cols] = value

    sources = (level, flow_x, flow_y, elev, friction, opened)
    take = lambda source, cols: jnp.concatenate([source[8:16, cols], source[80:88, cols]], axis=0)
    restrict(sources, take, ((6, 0, 2), (24, 8, 2)), pooled, coarse)
    for k in (0, 8, 9):
        set_faces(k, elev, friction, opened, sill_x, drag_x, sill_y, drag_y)
    for k in range(10):
        rows, out = pl.ds(8 + 8 * k, 8), pl.ds(8 * k, 8)
        level[rows, :] = level[rows, :] + elev[rows, :]
        flow_x[rows, :] = jnp.where(sill_x[out, :] < CLOSED, flow_x[rows, :], 0.0)
        flow_y[rows, :] = jnp.where(sill_y[out, :] < CLOSED, flow_y[rows, :], 0.0)
    row_above = jnp.maximum(row_place - 1, 0)
    row_below = jnp.minimum(row_place + 1, 3)

    sub = lax.broadcasted_iota(jnp.int32, (GROUP, WIDE), 0)

    def fine_step(step, carry):
        rains = [rain_s[pl.ds(4 * step + place, 1), :] for place in (row_above, row_place, row_below)]
        now = level[8 : 8 + GROUP, :]
        up = turn(now, -1, 0)
        after, up_after, west = now, up, now
        for k in range(HIGH // GROUP):
            out = slice(GROUP * k, GROUP * k + GROUP)
            rows = slice(8 + GROUP * k, 8 + GROUP * k + GROUP)
            if k + 1 < HIGH // GROUP:
                after = level[8 + GROUP * k + GROUP : 8 + 2 * GROUP + GROUP * k, :]
                up_after = turn(after, -1, 0)
            north = jnp.where(sub == GROUP - 1, up_after, up)
            qx = face(now, north, flow_x[rows, :], sill_x[out, :], drag_x[out, :])
            qy = face(now, turn(now, -1, 1), flow_y[rows, :], sill_y[out, :], drag_y[out, :])
            flow_x[rows, :] = qx
            flow_y[rows, :] = qy
            down = turn(qx, 1, 0)
            gain = (jnp.where(sub == 0, west, down) - qx) + (turn(qy, 1, 1) - qy)
            rain = rains[1]
            if k == 0:
                rain = jnp.where(sub < HALO, rains[0], rain)
            if k + 1 == HIGH // GROUP:
                rain = jnp.where(sub >= GROUP - HALO, rains[2], rain)
            level[rows, :] = now + (gain + rain)
            now, up, west = after, up_after, down
        return carry

    lax.fori_loop(0, FINE_STEPS, fine_step, 0, unroll=True)

    c_elev, c_friction, c_open = coarse[3], coarse[4], coarse[5]
    faces_x = static_faces(c_elev, c_friction, c_open, 0, COARSE_DRAG)
    faces_y = static_faces(c_elev, c_friction, c_open, 1, COARSE_DRAG)
    state = (coarse[0] + c_elev, coarse[1], coarse[2])
    row = lax.broadcasted_iota(jnp.int32, (C_HIGH, C_WIDE), 0)
    for step in range(COARSE_STEPS):
        parts = [rain_s[pl.ds(32 + 4 * step + place, 1), 0:C_WIDE] for place in (row_above, row_place, row_below)]
        rain = jnp.where(row < 8, parts[0], jnp.where(row < 24, parts[1], parts[2]))
        state = whole_step(*state, faces_x, faces_y, rain)
    old = (state[0] - c_elev, state[1], state[2])

    for k in range(10):
        rows = pl.ds(8 + 8 * k, 8)
        level[rows, :] = level[rows, :] - elev[rows, :]
    own = (slice(16, 80), slice(EDGE, EDGE + COLS))
    depth_out[0] = (1.0 / SCALE) * level[own]
    flux_out[0, 0] = (1.0 / FLOW_SCALE) * flow_x[own]
    flux_out[0, 1] = (1.0 / FLOW_SCALE) * flow_y[own]
    sources = (level, flow_x, flow_y)
    restrict(sources, lambda source, cols: source[16:80, cols], ((8, 0, 16),), pooled, coarse)
    factor = jnp.where(time_place == 0, 0.0, 1.0)
    side = EDGE // COARSENING
    outs = (to0, to1, to2, to3)
    for slot in range(3):
        mine = old[slot][8:24, :]
        old_out[C_ROWS * slot : C_ROWS * slot + C_ROWS, :] = turn(mine, -side, 1)[:, 0:C_COLS]
        value = coarse[slot, 8:24, :] - factor * mine
        fixed = coarse[3 + slot, 8:24, :]
        here = slice(C_ROWS * slot, C_ROWS * slot + C_ROWS)
        for odd, (now, ground_now) in enumerate(((value, fixed), (turn(value, -64, 1), turn(fixed, -64, 1)))):
            for half in range(2):
                cols = slice(128 * half, 128 * half + 128)
                windows[2 * half + odd, here, :] = now[:, cols]
                ground_s[2 * half + odd, here, :] = ground_now[:, cols]
    ground_out[...] = ground_s[x_place, pl.ds(pl.multiple_of(core * PART, PART), PART), :]
    for d, out in enumerate(outs):
        out[0 : 3 * C_ROWS, :] = windows[(x_place + d) % 4]
        out[3 * C_ROWS : BLOCK, :] = rates[...]


def ready(manning, radar, *rest):
    smem = pl.BlockSpec(memory_space=pltpu.SMEM)
    vmem = pl.BlockSpec(memory_space=pltpu.VMEM)
    padded = jax.ShapeDtypeStruct((HIGH + 16, WIDE), F32)
    faces = jax.ShapeDtypeStruct((HIGH, WIDE), F32)
    coarse = jax.ShapeDtypeStruct((6, C_HIGH, C_WIDE), F32)
    rain = jax.ShapeDtypeStruct((40, WIDE), F32)
    rates = jax.ShapeDtypeStruct((8, 128), F32)
    return pl.pallas_call(
        ready_kernel,
        in_specs=[smem, smem] + [vmem] * 10,
        out_specs=[vmem] * 13,
        out_shape=[padded] * 6 + [faces] * 4 + [coarse, rain, rates],
        scratch_shapes=[pltpu.VMEM((32, 128), jnp.int32), pltpu.VMEM((3, 6 * ROWS, 128), F32)],
        cost_estimate=pl.CostEstimate(flops=40_000_000, bytes_accessed=10_000_000, transcendentals=0),
        compiler_params=pltpu.CompilerParams(vmem_limit_bytes=VMEM_LIMIT),
    )(manning, radar, *rest)


def fine(manning, corner_a, corner_b, rain, rates, arrays):
    smem = pl.BlockSpec(memory_space=pltpu.SMEM)
    vmem = pl.BlockSpec(memory_space=pltpu.VMEM)
    message = jax.ShapeDtypeStruct((BLOCK, 128), F32)
    shapes = [jax.ShapeDtypeStruct(array.shape, F32) for array in arrays]
    return pl.pallas_call(
        fine_kernel,
        in_specs=[smem] + [vmem] * 15,
        out_specs=[vmem] * 19,
        out_shape=shapes
        + [
            jax.ShapeDtypeStruct((1, ROWS, COLS), F32),
            jax.ShapeDtypeStruct((1, 2, ROWS, COLS), F32),
            jax.ShapeDtypeStruct((3 * C_ROWS, C_COLS), F32),
            message,
            message,
            message,
            message,
            jax.ShapeDtypeStruct((PART, 128), F32),
        ],
        input_output_aliases={5 + place: place for place in range(11)},
        scratch_shapes=[
            pltpu.VMEM((3, 3 * ROWS, 128), F32),
            pltpu.VMEM((4, 3 * C_ROWS, 128), F32),
            pltpu.VMEM((4, 3 * C_ROWS, 128), F32),
        ],
        compiler_params=pltpu.CompilerParams(vmem_limit_bytes=VMEM_LIMIT),
    )(manning, corner_a, corner_b, rain, rates, *arrays)[11:]


HALF = SLICES // 2
TALL = 4 * C_ROWS
NEAR = 3 * C_ROWS
FIELDS = 3 * C_ROWS


def sweep_faces(ground):
    sill, drag, gate = static_faces(*ground, 0, COARSE_DRAG)
    last = lax.broadcasted_iota(jnp.int32, gate.shape, 0) == gate.shape[0] - 1
    gate = jnp.where(last, 0.0, gate)
    faces_x, faces_y = (sill, drag, gate), static_faces(*ground, 1, COARSE_DRAG)
    moved_x = tuple(turn(part, 1, 0) for part in faces_x)
    moved_y = tuple(turn(part, 1, 1) for part in faces_y)
    return moved_x, faces_x, moved_y, faces_y


def near_start(row_place):
    return pl.multiple_of(C_ROWS * jnp.clip(row_place - 1, 0, 1), C_ROWS)


def sweep_slices(first, state, change, rain, ground, newest, top, high):
    faces = sweep_faces(ground)
    rows = pl.ds(top, high)
    level, flux_x, flux_y = state
    fluxes = (turn(flux_x, 1, 0), flux_x, turn(flux_y, 1, 1), flux_y)

    for moment in range(first, HALF):
        for step in range(COARSE_STEPS):
            wet = jnp.concatenate(
                [
                    jnp.broadcast_to(
                        rain[pl.ds(8 * moment + 4 * step + top // C_ROWS + b, 1), :], (C_ROWS, 128)
                    )
                    for b in range(high // C_ROWS)
                ],
                axis=0,
            )
            level, fluxes = both_sides_step(level, fluxes, faces, wet)
        for field, value in enumerate((level, fluxes[1], fluxes[3])):
            newest[3 * moment + field, 0:high, :] = value
        add, add_x, add_y = (change[3 * moment + field, rows, :] for field in range(3))
        level = level + add
        fluxes = (
            fluxes[0] + turn(add_x, 1, 0), fluxes[1] + add_x, fluxes[2] + turn(add_y, 1, 1), fluxes[3] + add_y
        )
    return level, fluxes[1], fluxes[3]


def first_kernel(*refs):
    ins, (change, rain, ground, newest, halfway), (rates, state_s, all_s, parts_s) = refs[:8], refs[8:13], refs[13:]
    row_place = lax.axis_index("sx")
    col_place = lax.axis_index("sy")
    time_place = lax.axis_index("tm")
    z_place, x_place, core = time_place // 8, (time_place // 2) % 4, time_place % 2

    for other in range(2):
        for e in range(4):
            ref = ins[4 * other + e]
            source = (row_place, row_place + 1 - 2 * (row_place % 2), 3 - row_place, (row_place + 2) % 4)[e]
            start = pl.multiple_of(C_ROWS * source, C_ROWS)
            rows = pl.ds(start, C_ROWS)
            for d in range(4):
                slice_of = ((x_place + 4 - d) % 4) * 2 + (core + other) % 2
                for field in range(3):
                    base = FIELDS * d + C_ROWS * field
                    change[3 * slice_of + field, rows, :] = ref[base : base + C_ROWS, :]
                if e == 0:
                    base = 4 * FIELDS + PART + 8 * d
                    rates[pl.ds(pl.multiple_of(8 * slice_of, 8), 8), :] = ref[base : base + 8, :]
            half = (core + other) % 2
            base = 4 * FIELDS
            parts_s[pl.ds(pl.multiple_of(half * PART, PART), PART), :] = ref[base : base + PART, :]
            if other == 1:
                twin = ins[e]
                parts_s[pl.ds(pl.multiple_of(core * PART, PART), PART), :] = twin[base : base + PART, :]
                for field in range(3):
                    ground[field, rows, :] = parts_s[C_ROWS * field : C_ROWS * field + C_ROWS, :]

    block = lax.broadcasted_iota(jnp.int32, (128, 128), 0)
    column = lax.broadcasted_iota(jnp.int32, (128, 128), 1)
    column = column + (C_COLS * col_place + 64 * x_place - EDGE // COARSENING)
    rain[...] = split_dot(rates[...], jnp.where((column >> 4) == block, 1.0, 0.0).astype(BF16))

    all_s[...] = jnp.zeros(all_s.shape, F32)

    @pl.when(z_place == 0)
    def _():
        fixed = (ground[0], ground[1], ground[2])
        state = (change[0] + ground[0], change[1], change[2])
        state = sweep_slices(1, state, change, rain, fixed, newest, 0, TALL)
        for field in range(3):
            all_s[field] = state[field]

    near = pl.ds(near_start(row_place), NEAR)
    for field in range(3):
        state_s[NEAR * field : NEAR * field + NEAR, :] = all_s[field, near, :]
    lane = lax.broadcasted_iota(jnp.int32, (C_ROWS, 128), 1)
    pieces = [state_s[C_ROWS * k : C_ROWS * k + C_ROWS, :] for k in range(9)]
    for k in range(6):
        guest = turn(pieces[6 + k // 3], 80 - 32 * (k % 3), 1)
        halfway[C_ROWS * k : C_ROWS * k + C_ROWS, :] = jnp.where(lane < 96, turn(pieces[k], -16, 1), guest)
    halfway[6 * C_ROWS : 7 * C_ROWS, :] = turn(pieces[8], -16, 1)


def first_sweep(arrays):
    vmem = pl.BlockSpec(memory_space=pltpu.VMEM)
    field = jax.ShapeDtypeStruct((3 * HALF, TALL, 128), F32)
    return pl.pallas_call(
        first_kernel,
        in_specs=[vmem] * 8,
        out_specs=[vmem] * 5,
        out_shape=(
            field,
            jax.ShapeDtypeStruct((8 * HALF, 128), F32),
            jax.ShapeDtypeStruct((3, TALL, 128), F32),
            field,
            jax.ShapeDtypeStruct((7 * C_ROWS, 128), F32),
        ),
        scratch_shapes=[
            pltpu.VMEM((8 * HALF, 128), F32),
            pltpu.VMEM((3 * NEAR, 128), F32),
            pltpu.VMEM((3, TALL, 128), F32),
            pltpu.VMEM((3 * C_ROWS, 128), F32),
        ],
        compiler_params=pltpu.CompilerParams(vmem_limit_bytes=VMEM_LIMIT),
    )(*arrays)


def second_kernel(change, rain, ground, early, halfway, out0, out1, out2, out3, late, state_s):
    row_place = lax.axis_index("sx")
    time_place = lax.axis_index("tm")
    z_place, x_place, core = time_place // 8, (time_place // 2) % 4, time_place % 2
    top = near_start(row_place)

    @pl.when(z_place == 1)
    def _():
        lane = lax.broadcasted_iota(jnp.int32, (C_ROWS, 128), 1)
        pieces = [halfway[C_ROWS * k : C_ROWS * k + C_ROWS, :] for k in range(7)]
        for k in range(6):
            state_s[C_ROWS * k : C_ROWS * k + C_ROWS, :] = turn(pieces[k], 16, 1)
        for k in range(2):
            a, b, c = (turn(pieces[3 * k + part], 32 * part - 80, 1) for part in range(3))
            value = jnp.where(lane < 48, a, jnp.where(lane < 80, b, c))
            state_s[C_ROWS * (6 + k) : C_ROWS * (7 + k), :] = value
        state_s[8 * C_ROWS : 9 * C_ROWS, :] = turn(pieces[6], 16, 1)
        state = tuple(state_s[NEAR * field : NEAR * field + NEAR, :] for field in range(3))
        fixed = tuple(ground[field, pl.ds(top, NEAR), :] for field in range(3))
        sweep_slices(0, state, change, rain, fixed, late, top, NEAR)

    rows = pl.ds(pl.multiple_of(C_ROWS * row_place, C_ROWS), C_ROWS)
    late_rows = pl.ds(pl.multiple_of(C_ROWS * row_place - top, C_ROWS), C_ROWS)
    for d, out in enumerate((out0, out1, out2, out3)):
        slice_of = ((x_place + d) % 4) * 2 + core
        for field in range(3):
            here = 3 * slice_of + field
            value = jnp.where(z_place == 0, early[here, rows, :], late[here, late_rows, :])
            if field == 0:
                value = value - ground[0, rows, :]
            out[C_ROWS * field : C_ROWS * field + C_ROWS, :] = value


def second_sweep(change, rain, ground, early, halfway):
    vmem = pl.BlockSpec(memory_space=pltpu.VMEM)
    out = jax.ShapeDtypeStruct((FIELDS, 128), F32)
    return pl.pallas_call(
        second_kernel,
        in_specs=[vmem] * 5,
        out_specs=[vmem] * 4,
        out_shape=(out,) * 4,
        scratch_shapes=[pltpu.VMEM((3 * HALF, NEAR, 128), F32), pltpu.VMEM((3 * NEAR, 128), F32)],
        compiler_params=pltpu.CompilerParams(vmem_limit_bytes=VMEM_LIMIT),
    )(change, rain, ground, early, halfway)


def finish_kernel(depth, flux, old, new0, new1, new2, new3, depth_out, flux_out, parts, spread):
    time_place = lax.axis_index("tm")
    x_place = (time_place // 2) % 4
    for d, ref in enumerate((new0, new1, new2, new3)):
        parts[(x_place + 4 - d) % 4] = ref[...]
    lane = lax.broadcasted_iota(jnp.int32, (3 * C_ROWS, 128), 1)
    halves = [jnp.where(lane < 64, turn(parts[b], -32, 1), turn(parts[b + 1], 32, 1)) for b in (0, 2)]
    delta = jnp.concatenate(halves, axis=1) - old[...]
    delta = jnp.where(time_place == 0, 0.0, delta)
    copies = jnp.where(
        lax.broadcasted_iota(jnp.int32, (C_COLS, COLS), 0)
        == lax.broadcasted_iota(jnp.int32, (C_COLS, COLS), 1) // COARSENING,
        1.0,
        0.0,
    ).astype(BF16)
    scale = jnp.where(
        lax.broadcasted_iota(jnp.int32, (3 * C_ROWS, C_COLS), 0) < C_ROWS, 1.0 / SCALE, 1.0 / FLOW_SCALE
    )
    spread[...] = split_dot(scale * delta, copies)
    low = lax.broadcasted_iota(jnp.int32, (8, COLS), 0) < 4
    for field in range(3):
        for k in range(ROWS // 8):
            row = C_ROWS * field + 2 * k
            add = jnp.where(low, spread[row : row + 1, :], spread[row + 1 : row + 2, :])
            rows = slice(8 * k, 8 * k + 8)
            if field == 0:
                depth_out[0, rows, :] = depth[0, rows, :] + add
            else:
                flux_out[0, field - 1, rows, :] = flux[0, field - 1, rows, :] + add


def finish(depth, flux, old, news):
    vmem = pl.BlockSpec(memory_space=pltpu.VMEM)
    return pl.pallas_call(
        finish_kernel,
        in_specs=[vmem] * 7,
        out_specs=[vmem] * 2,
        out_shape=(jax.ShapeDtypeStruct(depth.shape, F32), jax.ShapeDtypeStruct(flux.shape, F32)),
        scratch_shapes=[pltpu.VMEM((4, 3 * C_ROWS, 128), F32), pltpu.VMEM((3 * C_ROWS, COLS), F32)],
        compiler_params=pltpu.CompilerParams(vmem_limit_bytes=VMEM_LIMIT),
    )(depth, flux, old, *news)


def time_route(move):
    route = []
    for source in range(SLICES):
        z, x, core = move(source // 8, (source // 2) % 4, source % 2)
        route.append((source, (z % 2) * 8 + (x % 4) * 2 + core % 2))
    return route


def with_row(values, flip):
    return lax.ppermute(values, "sx", [(i, i ^ flip) for i in range(4)])


def over_x(values, distance):
    return lax.ppermute(values, "tm", time_route(lambda z, x, core: (z, x + distance, core)))


def on_device(
    depth_start, flux_start, elevation, roughness_class, building, manning, radar_rates, tile_index
):
    fields = (depth_start, flux_start, elevation, roughness_class, building)
    first, second, row_a, row_b = pack(*fields)
    first = lax.ppermute(first, "sy", [(0, 1), (1, 0), (2, 3), (3, 2)])
    second = lax.ppermute(second, "sy", [(1, 2), (2, 1)])
    row_a, row_b = with_row(row_a, 1), with_row(row_b, 3)
    size = 6 * HALO
    tops = jnp.concatenate([first[:size], second[:size]], axis=0)
    bottoms = jnp.concatenate([first[size : 2 * size], second[size : 2 * size]], axis=0)
    even_row = lax.axis_index("sx") % 2 == 0
    corner_a = with_row(jnp.where(even_row, bottoms, tops), 1)
    corner_b = with_row(jnp.where(even_row, tops, bottoms), 3)
    *arrays, rain, rates = ready(
        manning, radar_rates, *fields, tile_index, first, second, row_a, row_b
    )
    depth, flux, old, own, *away, ground = fine(manning, corner_a, corner_b, rain, rates, arrays)
    parts = [own] + [over_x(away[d - 1], d) for d in (1, 2, 3)]
    column = jnp.concatenate([part[:FIELDS] for part in parts] + [ground], axis=0)
    mine = jnp.concatenate([column] + [part[FIELDS:] for part in parts], axis=0)
    sibling = time_route(lambda z, x, core: (z, x, core + 1))
    arrays = [mine] + [with_row(column, flip) for flip in (1, 3, 2)]
    twins = []
    for group in ((0, 1), (2,), (3,)):
        joined = jnp.concatenate([arrays[k] for k in group], axis=0) if len(group) > 1 else arrays[group[0]]
        joined = lax.ppermute(joined, "tm", sibling)
        start = 0
        for k in group:
            twins.append(joined[start : start + arrays[k].shape[0]])
            start += arrays[k].shape[0]
    arrays = arrays + twins
    change, rain, ground, early, halfway = first_sweep(arrays)
    halfway = lax.ppermute(halfway, "tm", time_route(lambda z, x, core: (z + 1, x, core)))
    news = second_sweep(change, rain, ground, early, halfway)
    news = [news[0]] + [over_x(news[d], d) for d in (1, 2, 3)]
    return finish(depth, flux, old, news)


def solution(mesh):
    placed = (
        P("tm", "sx", "sy"),
        P("tm", None, "sx", "sy"),
        P("sx", "sy"),
        P("sx", "sy"),
        P("sx", "sy"),
        P(),
        P(),
        P("tm", None, None, None),
    )
    return jax.shard_map(
        on_device,
        mesh=mesh,
        in_specs=placed,
        out_specs=(P("tm", "sx", "sy"), P("tm", None, "sx", "sy")),
        check_vma=False,
    )
```

```python
import math

import jax
import jax.numpy as jnp
from jax import lax
from jax.experimental import pallas as pl
from jax.experimental.pallas import tpu as pltpu
from jax.sharding import PartitionSpec as P

FINE_STEPS = 8
COARSE_STEPS = 2
COARSENING = 4
RAIN_BLOCK = 64
RADAR_TILES = 64
ROUGH_CLASSES = 8
SLICES = 16

GRAVITY = 9.81
DEPTH_FLOOR = 0.05
CELL_SIDE = 2.0
TIME_STEP = 0.25
COARSE_SECONDS = TIME_STEP * FINE_STEPS / COARSE_STEPS
COARSE_SIDE = CELL_SIDE * COARSENING
POWER = -7.0 / 3.0 / math.log(2.0)

COURANT = TIME_STEP / CELL_SIDE
SCALE = COURANT * GRAVITY * TIME_STEP / CELL_SIDE
FLOW_SCALE = SCALE * COURANT
FLOOR = SCALE * DEPTH_FLOOR
FINE_DRAG = GRAVITY * TIME_STEP * SCALE ** (7.0 / 3.0) / FLOW_SCALE
COARSE_DRAG = GRAVITY * COARSE_SECONDS * SCALE ** (7.0 / 3.0) / FLOW_SCALE
CLOSED = 1e30
GROUP = 40

ROWS, COLS = 64, 1024
EDGE = 128
HALO = 8
HIGH, WIDE = ROWS + 2 * HALO, COLS + 2 * EDGE
C_ROWS, C_COLS = ROWS // COARSENING, COLS // COARSENING
C_HIGH, C_WIDE = 32, 384
PART = 3 * C_ROWS // 2
BLOCK = 3 * C_ROWS + 8
F32 = jnp.float32
BF16 = jnp.bfloat16
VMEM_LIMIT = 24 * 1024 * 1024


def face(level, level_next, flux, sill, drag, gate=None):
    raw = jnp.maximum(level, level_next) - sill
    power = jnp.exp2(POWER * jnp.log(jnp.maximum(raw, FLOOR)))
    below = 1.0 + drag * jnp.abs(flux) * power
    inverse = pl.reciprocal(below, approx=True)
    if gate is not None:
        inverse = gate * inverse
    return inverse * (flux - (level_next - level) * jnp.maximum(raw, 0.0))


def split_dot(values, weights, parts=3):
    total = None
    for part in range(parts):
        piece = values.astype(BF16)
        product = jnp.dot(piece, weights, preferred_element_type=F32)
        total = product if total is None else total + product
        if part + 1 < parts:
            values = values - piece.astype(F32)
    return total


def turn(values, shift, axis):
    return pltpu.roll(values, shift % values.shape[axis], axis)


def static_faces(elev, friction, opened, axis, drag):
    sill = jnp.maximum(elev, turn(elev, -1, axis))
    rough = 0.5 * (friction + turn(friction, -1, axis))
    gate = opened * turn(opened, -1, axis)
    return sill, drag * rough * rough, gate


def whole_step(level, flux_x, flux_y, faces_x, faces_y, rain):
    flux_x = face(level, turn(level, -1, 0), flux_x, *faces_x)
    flux_y = face(level, turn(level, -1, 1), flux_y, *faces_y)
    gain = (turn(flux_x, 1, 0) - flux_x) + (turn(flux_y, 1, 1) - flux_y)
    return level + (gain + rain), flux_x, flux_y


def both_sides_step(level, fluxes, faces, rain):
    last_x, next_x, last_y, next_y = fluxes
    fluxes = (
        face(turn(level, 1, 0), level, last_x, *faces[0]),
        face(level, turn(level, -1, 0), next_x, *faces[1]),
        face(turn(level, 1, 1), level, last_y, *faces[2]),
        face(level, turn(level, -1, 1), next_y, *faces[3]),
    )
    gain = (fluxes[0] - fluxes[1]) + (fluxes[2] - fluxes[3])
    return level + (gain + rain), fluxes


def edge_parts(index):
    return (
        (0, HALO, HALO * index),
        (ROWS - HALO, HALO, 6 * HALO + HALO * index),
        (HALO, ROWS - 2 * HALO, 12 * HALO + (ROWS - 2 * HALO) * index),
    )


def pack_kernel(*refs):
    ins, (first, second, row_a, row_b) = refs[:20], refs[20:]
    even = lax.axis_index("sy") % 2 == 0
    even_row = lax.axis_index("sx") % 2 == 0
    index = 0
    for array in range(5):
        left, right, top, bottom = ins[4 * array : 4 * array + 4]
        for lead in (((0,),), ((0, 0), (0, 1)), ((),), ((),), ((),))[array]:
            for row, count, place in edge_parts(index):
                where = lead + (slice(row, row + count), slice(None))
                a, b = left[where].astype(F32), right[where].astype(F32)
                first[place : place + count, :] = jnp.where(even, b, a)
                second[place : place + count, :] = jnp.where(even, a, b)
            here = slice(HALO * index, HALO * index + HALO)
            where = lead + (slice(None), slice(None))
            a, b = top[where].astype(F32), bottom[where].astype(F32)
            row_a[here, :] = jnp.where(even_row, b, a)
            row_b[here, :] = jnp.where(even_row, a, b)
            index += 1


def pack(*fields):
    specs, args = [], []
    for array in fields:
        lead = array.shape[:-2]
        zeros = (0,) * len(lead)
        for shape, place in (
            ((ROWS, EDGE), (0, 0)),
            ((ROWS, EDGE), (0, COLS // EDGE - 1)),
            ((HALO, COLS), (0, 0)),
            ((HALO, COLS), (ROWS // HALO - 1, 0)),
        ):
            specs.append(pl.BlockSpec(lead + shape, lambda i, at=zeros + place: at))
            args.append(array)
    column = jax.ShapeDtypeStruct((6 * ROWS, EDGE), F32)
    row = jax.ShapeDtypeStruct((6 * HALO, COLS), F32)
    return pl.pallas_call(
        pack_kernel,
        grid=(1,),
        in_specs=specs,
        out_specs=[pl.BlockSpec(memory_space=pltpu.VMEM)] * 4,
        out_shape=(column, column, row, row),
    )(*args)


def roughness_of(classes, manning):
    value = jnp.full(classes.shape, manning[0], F32)
    for entry in range(1, ROUGH_CLASSES):
        value = jnp.where(classes == float(entry), manning[entry], value)
    return value


def pool_matrix():
    return jnp.where(
        lax.broadcasted_iota(jnp.int32, (512, 128), 0) // COARSENING
        == lax.broadcasted_iota(jnp.int32, (512, 128), 1),
        1.0 / 16.0,
        0.0,
    ).astype(BF16)


def restrict(sources, take, spans, pooled, coarse):
    pool = pool_matrix()
    high = None
    for part in range(3):
        cols = slice(512 * part, min(512 * part + 512, WIDE))
        values = [take(source, cols) for source in sources]
        high = values[0].shape[0]
        values = jnp.concatenate(values, axis=0)
        pooled[part, 0 : values.shape[0], :] = split_dot(values, pool[0 : values.shape[1], :], 2)
    for slot in range(len(sources)):
        for part in range(3):
            cols = slice(128 * part, 128 * part + 128)
            for target, start, count in spans:
                first = high * slot + start
                total = pooled[part, pl.ds(first, count, stride=4), :]
                for q in range(1, 4):
                    total = total + pooled[part, pl.ds(first + q, count, stride=4), :]
                coarse[slot, target : target + count, cols] = total


def set_faces(k, elev, friction, opened, sill_x, drag_x, sill_y, drag_y):
    rows, after, out = pl.ds(8 + 8 * k, 8), pl.ds(9 + 8 * k, 8), pl.ds(8 * k, 8)
    e, f, o = elev[rows, :], friction[rows, :], opened[rows, :]
    gate = o * opened[after, :]
    sill_x[out, :] = jnp.where(gate > 0.0, jnp.maximum(e, elev[after, :]), CLOSED)
    rough = 0.5 * (f + friction[after, :])
    drag_x[out, :] = FINE_DRAG * rough * rough
    sill, drag_y[out, :], gate = static_faces(e, f, o, 1, FINE_DRAG)
    sill_y[out, :] = jnp.where(gate > 0.0, sill, CLOSED)


def places():
    time_place = lax.axis_index("tm")
    return lax.axis_index("sx"), lax.axis_index("sy"), time_place, (time_place // 2) % 4, time_place % 2


def ready_kernel(
    manning, radar, depth, flux, elevation, roughness, building, tiles, first, second, row_a, row_b,
    level, flow_x, flow_y, elev, friction, opened, sill_x, drag_x, sill_y, drag_y, coarse, rain_s, rates_out,
    index_s, pooled,
):
    row_place, col_place, time_place, x_place, core = places()
    even = col_place % 2 == 0
    odd_row = row_place % 2 == 1
    none = jnp.zeros((HALO, EDGE), F32)

    def fill(target, index, own, scale=1.0):
        target[0:8, :] = jnp.zeros((8, WIDE), F32)
        target[88:96, :] = jnp.zeros((8, WIDE), F32)
        target[16:80, EDGE : EDGE + COLS] = scale * own
        for row, count, place in edge_parts(index):
            rows, a, b = slice(16 + row, 16 + row + count), first[place : place + count], second[place : place + count]
            target[rows, 0:EDGE] = scale * jnp.where(even, b, a)
            target[rows, EDGE + COLS : WIDE] = scale * jnp.where(even, a, b)
        here = slice(index * HALO, index * HALO + HALO)
        for rows, is_first in ((slice(8, 16), odd_row), (slice(80, 88), ~odd_row)):
            target[rows, EDGE : EDGE + COLS] = scale * jnp.where(is_first, row_a[here, :], row_b[here, :])
            target[rows, 0:EDGE] = none
            target[rows, EDGE + COLS : WIDE] = none

    fill(level, 0, depth[0], SCALE)
    fill(flow_x, 1, flux[0, 0], FLOW_SCALE)
    fill(flow_y, 2, flux[0, 1], FLOW_SCALE)
    fill(elev, 3, elevation[...], SCALE)
    fill(friction, 4, roughness[...].astype(F32))
    fill(opened, 5, building[...].astype(F32))

    lane = lax.broadcasted_iota(jnp.int32, (8, WIDE), 1)
    inside = jnp.where(
        ((col_place == 0) & (lane < EDGE)) | ((col_place == 3) & (lane >= EDGE + COLS)), 0.0, 1.0
    )
    for k in range(12):
        here = pl.ds(8 * k, 8)
        friction[here, :] = roughness_of(friction[here, :], manning)
        if k in (0, 11):
            opened[here, :] = jnp.zeros((8, WIDE), F32)
            continue
        free = (1.0 - opened[here, :]) * inside
        if k == 1:
            free = free * jnp.where(row_place == 0, 0.0, 1.0)
        if k == 10:
            free = free * jnp.where(row_place == 3, 0.0, 1.0)
        opened[here, :] = free

    index_s[...] = jnp.full((32, 128), -1, jnp.int32)
    for step in range(FINE_STEPS):
        index_s[4 * step : 4 * step + 4, 0:64] = tiles[0, step]
    index = index_s[...]
    rates = jnp.zeros((32, 128), F32)
    for entry in range(RADAR_TILES):
        rates = jnp.where(index == entry, radar[entry], rates)
    block = lax.broadcasted_iota(jnp.int32, (128, WIDE), 0)
    column = lax.broadcasted_iota(jnp.int32, (128, WIDE), 1) + (COLS * col_place - EDGE)
    rain_s[0:32, :] = (SCALE * TIME_STEP) * split_dot(
        rates, jnp.where((column >> 6) == block, 1.0, 0.0).astype(BF16)
    )
    means = []
    for half in range(COARSE_STEPS):
        part = rates[16 * half : 16 * half + 16, :]
        means.append((0.25 * SCALE * COARSE_SECONDS) * (part[0:4] + part[4:8] + part[8:12] + part[12:16]))
    coarse_rates = jnp.concatenate(means, axis=0)
    rates_out[...] = coarse_rates
    block = lax.broadcasted_iota(jnp.int32, (128, C_WIDE), 0)
    column = lax.broadcasted_iota(jnp.int32, (128, C_WIDE), 1) + (C_COLS * col_place - EDGE // COARSENING)
    padded = jnp.concatenate([coarse_rates, jnp.zeros((8, 128), F32)], axis=0)
    rain_s[32:40, :] = jnp.zeros((8, WIDE), F32)
    rain_s[32:40, 0:C_WIDE] = split_dot(
        padded, jnp.where((column >> 4) == block, 1.0, 0.0).astype(BF16)
    )[0:8]

    coarse[...] = jnp.zeros(coarse.shape, F32)
    sources = (level, flow_x, flow_y, elev, friction, opened)
    restrict(sources, lambda source, cols: source[16:80, cols], ((8, 0, 16),), pooled, coarse)
    for k in range(1, 8):
        set_faces(k, elev, friction, opened, sill_x, drag_x, sill_y, drag_y)
        rows, out = pl.ds(8 + 8 * k, 8), pl.ds(8 * k, 8)
        level[rows, :] = level[rows, :] + elev[rows, :]
        flow_x[rows, :] = jnp.where(sill_x[out, :] < CLOSED, flow_x[rows, :], 0.0)
        flow_y[rows, :] = jnp.where(sill_y[out, :] < CLOSED, flow_y[rows, :], 0.0)


def fine_kernel(*refs):
    manning, corner_a, corner_b, rain_s, rates = refs[:5]
    level, flow_x, flow_y, elev, friction, opened, sill_x, drag_x, sill_y, drag_y, coarse = refs[16:27]
    depth_out, flux_out, old_out, to0, to1, to2, to3, ground_out = refs[27:35]
    pooled, ground_s, windows = refs[35:]
    row_place, col_place, time_place, x_place, core = places()
    even = col_place % 2 == 0
    odd_row = row_place % 2 == 1

    left, right = slice(0, EDGE), slice(EDGE + COLS, WIDE)
    grid_row = (jnp.where(row_place == 0, 0.0, 1.0), jnp.where(row_place == 3, 0.0, 1.0))
    grid_col = (jnp.where(col_place == 0, 0.0, 1.0), jnp.where(col_place == 3, 0.0, 1.0))
    scales = (SCALE, FLOW_SCALE, FLOW_SCALE, SCALE)
    for index, target in enumerate((level, flow_x, flow_y, elev, friction, opened)):
        here = slice(index * HALO, index * HALO + HALO)
        there = slice((6 + index) * HALO, (6 + index) * HALO + HALO)
        for r, (rows, is_first) in enumerate(((slice(8, 16), odd_row), (slice(80, 88), ~odd_row))):
            a = jnp.where(is_first, corner_a[here, :], corner_b[here, :])
            b = jnp.where(is_first, corner_a[there, :], corner_b[there, :])
            for c, (cols, value) in enumerate(((left, jnp.where(even, b, a)), (right, jnp.where(even, a, b)))):
                if index < 4:
                    value = scales[index] * value
                elif index == 4:
                    value = roughness_of(value, manning)
                else:
                    value = (1.0 - value) * (grid_row[r] * grid_col[c])
                target[rows, cols] = value

    sources = (level, flow_x, flow_y, elev, friction, opened)
    take = lambda source, cols: jnp.concatenate([source[8:16, cols], source[80:88, cols]], axis=0)
    restrict(sources, take, ((6, 0, 2), (24, 8, 2)), pooled, coarse)
    for k in (0, 8, 9):
        set_faces(k, elev, friction, opened, sill_x, drag_x, sill_y, drag_y)
    for k in (0, 8, 9):
        rows, out = pl.ds(8 + 8 * k, 8), pl.ds(8 * k, 8)
        level[rows, :] = level[rows, :] + elev[rows, :]
        flow_x[rows, :] = jnp.where(sill_x[out, :] < CLOSED, flow_x[rows, :], 0.0)
        flow_y[rows, :] = jnp.where(sill_y[out, :] < CLOSED, flow_y[rows, :], 0.0)
    row_above = jnp.maximum(row_place - 1, 0)
    row_below = jnp.minimum(row_place + 1, 3)

    sub = lax.broadcasted_iota(jnp.int32, (GROUP, WIDE), 0)

    def fine_step(step, carry):
        rains = [rain_s[pl.ds(4 * step + place, 1), :] for place in (row_above, row_place, row_below)]
        now = level[8 : 8 + GROUP, :]
        up = turn(now, -1, 0)
        after, up_after, west = now, up, now
        for k in range(HIGH // GROUP):
            out = slice(GROUP * k, GROUP * k + GROUP)
            rows = slice(8 + GROUP * k, 8 + GROUP * k + GROUP)
            if k + 1 < HIGH // GROUP:
                after = level[8 + GROUP * k + GROUP : 8 + 2 * GROUP + GROUP * k, :]
                up_after = turn(after, -1, 0)
            north = jnp.where(sub == GROUP - 1, up_after, up)
            qx = face(now, north, flow_x[rows, :], sill_x[out, :], drag_x[out, :])
            qy = face(now, turn(now, -1, 1), flow_y[rows, :], sill_y[out, :], drag_y[out, :])
            flow_x[rows, :] = qx
            flow_y[rows, :] = qy
            down = turn(qx, 1, 0)
            gain = (jnp.where(sub == 0, west, down) - qx) + (turn(qy, 1, 1) - qy)
            rain = rains[1]
            if k == 0:
                rain = jnp.where(sub < HALO, rains[0], rain)
            if k + 1 == HIGH // GROUP:
                rain = jnp.where(sub >= GROUP - HALO, rains[2], rain)
            level[rows, :] = now + (gain + rain)
            now, up, west = after, up_after, down
        return carry

    lax.fori_loop(0, FINE_STEPS, fine_step, 0, unroll=True)

    c_elev, c_friction, c_open = coarse[3], coarse[4], coarse[5]
    faces_x = static_faces(c_elev, c_friction, c_open, 0, COARSE_DRAG)
    faces_y = static_faces(c_elev, c_friction, c_open, 1, COARSE_DRAG)
    state = (coarse[0] + c_elev, coarse[1], coarse[2])
    row = lax.broadcasted_iota(jnp.int32, (C_HIGH, C_WIDE), 0)
    for step in range(COARSE_STEPS):
        parts = [rain_s[pl.ds(32 + 4 * step + place, 1), 0:C_WIDE] for place in (row_above, row_place, row_below)]
        rain = jnp.where(row < 8, parts[0], jnp.where(row < 24, parts[1], parts[2]))
        state = whole_step(*state, faces_x, faces_y, rain)
    old = (state[0] - c_elev, state[1], state[2])

    for k in range(10):
        rows = pl.ds(8 + 8 * k, 8)
        level[rows, :] = level[rows, :] - elev[rows, :]
    own = (slice(16, 80), slice(EDGE, EDGE + COLS))
    depth_out[0] = (1.0 / SCALE) * level[own]
    flux_out[0, 0] = (1.0 / FLOW_SCALE) * flow_x[own]
    flux_out[0, 1] = (1.0 / FLOW_SCALE) * flow_y[own]
    sources = (level, flow_x, flow_y)
    restrict(sources, lambda source, cols: source[16:80, cols], ((8, 0, 16),), pooled, coarse)
    factor = jnp.where(time_place == 0, 0.0, 1.0)
    side = EDGE // COARSENING
    outs = (to0, to1, to2, to3)
    for slot in range(3):
        mine = old[slot][8:24, :]
        old_out[C_ROWS * slot : C_ROWS * slot + C_ROWS, :] = turn(mine, -side, 1)[:, 0:C_COLS]
        value = coarse[slot, 8:24, :] - factor * mine
        fixed = coarse[3 + slot, 8:24, :]
        here = slice(C_ROWS * slot, C_ROWS * slot + C_ROWS)
        for odd, (now, ground_now) in enumerate(((value, fixed), (turn(value, -64, 1), turn(fixed, -64, 1)))):
            for half in range(2):
                cols = slice(128 * half, 128 * half + 128)
                windows[2 * half + odd, here, :] = now[:, cols]
                ground_s[2 * half + odd, here, :] = ground_now[:, cols]
    ground_out[...] = ground_s[x_place, pl.ds(pl.multiple_of(core * PART, PART), PART), :]
    for d, out in enumerate(outs):
        out[0 : 3 * C_ROWS, :] = windows[(x_place + d) % 4]
        out[3 * C_ROWS : BLOCK, :] = rates[...]


def ready(manning, radar, *rest):
    smem = pl.BlockSpec(memory_space=pltpu.SMEM)
    vmem = pl.BlockSpec(memory_space=pltpu.VMEM)
    padded = jax.ShapeDtypeStruct((HIGH + 16, WIDE), F32)
    faces = jax.ShapeDtypeStruct((HIGH, WIDE), F32)
    coarse = jax.ShapeDtypeStruct((6, C_HIGH, C_WIDE), F32)
    rain = jax.ShapeDtypeStruct((40, WIDE), F32)
    rates = jax.ShapeDtypeStruct((8, 128), F32)
    return pl.pallas_call(
        ready_kernel,
        in_specs=[smem, smem] + [vmem] * 10,
        out_specs=[vmem] * 13,
        out_shape=[padded] * 6 + [faces] * 4 + [coarse, rain, rates],
        scratch_shapes=[pltpu.VMEM((32, 128), jnp.int32), pltpu.VMEM((3, 6 * ROWS, 128), F32)],
        cost_estimate=pl.CostEstimate(flops=40_000_000, bytes_accessed=10_000_000, transcendentals=0),
        compiler_params=pltpu.CompilerParams(vmem_limit_bytes=VMEM_LIMIT),
    )(manning, radar, *rest)


def fine(manning, corner_a, corner_b, rain, rates, arrays):
    smem = pl.BlockSpec(memory_space=pltpu.SMEM)
    vmem = pl.BlockSpec(memory_space=pltpu.VMEM)
    message = jax.ShapeDtypeStruct((BLOCK, 128), F32)
    shapes = [jax.ShapeDtypeStruct(array.shape, F32) for array in arrays]
    return pl.pallas_call(
        fine_kernel,
        in_specs=[smem] + [vmem] * 15,
        out_specs=[vmem] * 19,
        out_shape=shapes
        + [
            jax.ShapeDtypeStruct((1, ROWS, COLS), F32),
            jax.ShapeDtypeStruct((1, 2, ROWS, COLS), F32),
            jax.ShapeDtypeStruct((3 * C_ROWS, C_COLS), F32),
            message,
            message,
            message,
            message,
            jax.ShapeDtypeStruct((PART, 128), F32),
        ],
        input_output_aliases={5 + place: place for place in range(11)},
        scratch_shapes=[
            pltpu.VMEM((3, 3 * ROWS, 128), F32),
            pltpu.VMEM((4, 3 * C_ROWS, 128), F32),
            pltpu.VMEM((4, 3 * C_ROWS, 128), F32),
        ],
        compiler_params=pltpu.CompilerParams(vmem_limit_bytes=VMEM_LIMIT),
    )(manning, corner_a, corner_b, rain, rates, *arrays)[11:]


HALF = SLICES // 2
TALL = 4 * C_ROWS
NEAR = 3 * C_ROWS
FIELDS = 3 * C_ROWS


def sweep_faces(ground):
    sill, drag, gate = static_faces(*ground, 0, COARSE_DRAG)
    last = lax.broadcasted_iota(jnp.int32, gate.shape, 0) == gate.shape[0] - 1
    gate = jnp.where(last, 0.0, gate)
    faces_x, faces_y = (sill, drag, gate), static_faces(*ground, 1, COARSE_DRAG)
    moved_x = tuple(turn(part, 1, 0) for part in faces_x)
    moved_y = tuple(turn(part, 1, 1) for part in faces_y)
    return moved_x, faces_x, moved_y, faces_y


def near_start(row_place):
    return pl.multiple_of(C_ROWS * jnp.clip(row_place - 1, 0, 1), C_ROWS)


def sweep_slices(first, state, change, rain, ground, newest, top, high):
    faces = sweep_faces(ground)
    rows = pl.ds(top, high)
    level, flux_x, flux_y = state
    fluxes = (turn(flux_x, 1, 0), flux_x, turn(flux_y, 1, 1), flux_y)

    for moment in range(first, HALF):
        for step in range(COARSE_STEPS):
            wet = jnp.concatenate(
                [
                    jnp.broadcast_to(
                        rain[pl.ds(8 * moment + 4 * step + top // C_ROWS + b, 1), :], (C_ROWS, 128)
                    )
                    for b in range(high // C_ROWS)
                ],
                axis=0,
            )
            level, fluxes = both_sides_step(level, fluxes, faces, wet)
        for field, value in enumerate((level, fluxes[1], fluxes[3])):
            newest[3 * moment + field, 0:high, :] = value
        add, add_x, add_y = (change[3 * moment + field, rows, :] for field in range(3))
        level = level + add
        fluxes = (
            fluxes[0] + turn(add_x, 1, 0), fluxes[1] + add_x, fluxes[2] + turn(add_y, 1, 1), fluxes[3] + add_y
        )
    return level, fluxes[1], fluxes[3]


def first_kernel(*refs):
    ins, (change, rain, ground, newest, halfway), (rates, state_s, all_s, parts_s) = refs[:8], refs[8:13], refs[13:]
    row_place = lax.axis_index("sx")
    col_place = lax.axis_index("sy")
    time_place = lax.axis_index("tm")
    z_place, x_place, core = time_place // 8, (time_place // 2) % 4, time_place % 2

    for other in range(2):
        for e in range(4):
            ref = ins[4 * other + e]
            source = (row_place, row_place + 1 - 2 * (row_place % 2), 3 - row_place, (row_place + 2) % 4)[e]
            start = pl.multiple_of(C_ROWS * source, C_ROWS)
            rows = pl.ds(start, C_ROWS)
            for d in range(4):
                slice_of = ((x_place + 4 - d) % 4) * 2 + (core + other) % 2
                for field in range(3):
                    base = FIELDS * d + C_ROWS * field
                    change[3 * slice_of + field, rows, :] = ref[base : base + C_ROWS, :]
                if e == 0:
                    base = 4 * FIELDS + PART + 8 * d
                    rates[pl.ds(pl.multiple_of(8 * slice_of, 8), 8), :] = ref[base : base + 8, :]
            half = (core + other) % 2
            base = 4 * FIELDS
            parts_s[pl.ds(pl.multiple_of(half * PART, PART), PART), :] = ref[base : base + PART, :]
            if other == 1:
                twin = ins[e]
                parts_s[pl.ds(pl.multiple_of(core * PART, PART), PART), :] = twin[base : base + PART, :]
                for field in range(3):
                    ground[field, rows, :] = parts_s[C_ROWS * field : C_ROWS * field + C_ROWS, :]

    block = lax.broadcasted_iota(jnp.int32, (128, 128), 0)
    column = lax.broadcasted_iota(jnp.int32, (128, 128), 1)
    column = column + (C_COLS * col_place + 64 * x_place - EDGE // COARSENING)
    rain[...] = split_dot(rates[...], jnp.where((column >> 4) == block, 1.0, 0.0).astype(BF16))

    all_s[...] = jnp.zeros(all_s.shape, F32)

    @pl.when(z_place == 0)
    def _():
        fixed = (ground[0], ground[1], ground[2])
        state = (change[0] + ground[0], change[1], change[2])
        state = sweep_slices(1, state, change, rain, fixed, newest, 0, TALL)
        for field in range(3):
            all_s[field] = state[field]

    near = pl.ds(near_start(row_place), NEAR)
    for field in range(3):
        state_s[NEAR * field : NEAR * field + NEAR, :] = all_s[field, near, :]
    lane = lax.broadcasted_iota(jnp.int32, (C_ROWS, 128), 1)
    pieces = [state_s[C_ROWS * k : C_ROWS * k + C_ROWS, :] for k in range(9)]
    for k in range(6):
        guest = turn(pieces[6 + k // 3], 80 - 32 * (k % 3), 1)
        halfway[C_ROWS * k : C_ROWS * k + C_ROWS, :] = jnp.where(lane < 96, turn(pieces[k], -16, 1), guest)
    halfway[6 * C_ROWS : 7 * C_ROWS, :] = turn(pieces[8], -16, 1)


def first_sweep(arrays):
    vmem = pl.BlockSpec(memory_space=pltpu.VMEM)
    field = jax.ShapeDtypeStruct((3 * HALF, TALL, 128), F32)
    return pl.pallas_call(
        first_kernel,
        in_specs=[vmem] * 8,
        out_specs=[vmem] * 5,
        out_shape=(
            field,
            jax.ShapeDtypeStruct((8 * HALF, 128), F32),
            jax.ShapeDtypeStruct((3, TALL, 128), F32),
            field,
            jax.ShapeDtypeStruct((7 * C_ROWS, 128), F32),
        ),
        scratch_shapes=[
            pltpu.VMEM((8 * HALF, 128), F32),
            pltpu.VMEM((3 * NEAR, 128), F32),
            pltpu.VMEM((3, TALL, 128), F32),
            pltpu.VMEM((3 * C_ROWS, 128), F32),
        ],
        compiler_params=pltpu.CompilerParams(vmem_limit_bytes=VMEM_LIMIT),
    )(*arrays)


def second_kernel(change, rain, ground, early, halfway, out0, out1, out2, out3, late, state_s):
    row_place = lax.axis_index("sx")
    time_place = lax.axis_index("tm")
    z_place, x_place, core = time_place // 8, (time_place // 2) % 4, time_place % 2
    top = near_start(row_place)

    @pl.when(z_place == 1)
    def _():
        lane = lax.broadcasted_iota(jnp.int32, (C_ROWS, 128), 1)
        pieces = [halfway[C_ROWS * k : C_ROWS * k + C_ROWS, :] for k in range(7)]
        for k in range(6):
            state_s[C_ROWS * k : C_ROWS * k + C_ROWS, :] = turn(pieces[k], 16, 1)
        for k in range(2):
            a, b, c = (turn(pieces[3 * k + part], 32 * part - 80, 1) for part in range(3))
            value = jnp.where(lane < 48, a, jnp.where(lane < 80, b, c))
            state_s[C_ROWS * (6 + k) : C_ROWS * (7 + k), :] = value
        state_s[8 * C_ROWS : 9 * C_ROWS, :] = turn(pieces[6], 16, 1)
        state = tuple(state_s[NEAR * field : NEAR * field + NEAR, :] for field in range(3))
        fixed = tuple(ground[field, pl.ds(top, NEAR), :] for field in range(3))
        sweep_slices(0, state, change, rain, fixed, late, top, NEAR)

    rows = pl.ds(pl.multiple_of(C_ROWS * row_place, C_ROWS), C_ROWS)
    late_rows = pl.ds(pl.multiple_of(C_ROWS * row_place - top, C_ROWS), C_ROWS)
    for d, out in enumerate((out0, out1, out2, out3)):
        slice_of = ((x_place + d) % 4) * 2 + core
        for field in range(3):
            here = 3 * slice_of + field
            value = jnp.where(z_place == 0, early[here, rows, :], late[here, late_rows, :])
            if field == 0:
                value = value - ground[0, rows, :]
            out[C_ROWS * field : C_ROWS * field + C_ROWS, :] = value


def second_sweep(change, rain, ground, early, halfway):
    vmem = pl.BlockSpec(memory_space=pltpu.VMEM)
    out = jax.ShapeDtypeStruct((FIELDS, 128), F32)
    return pl.pallas_call(
        second_kernel,
        in_specs=[vmem] * 5,
        out_specs=[vmem] * 4,
        out_shape=(out,) * 4,
        scratch_shapes=[pltpu.VMEM((3 * HALF, NEAR, 128), F32), pltpu.VMEM((3 * NEAR, 128), F32)],
        compiler_params=pltpu.CompilerParams(vmem_limit_bytes=VMEM_LIMIT),
    )(change, rain, ground, early, halfway)


def finish_kernel(depth, flux, old, new0, new1, new2, new3, depth_out, flux_out, parts, spread):
    time_place = lax.axis_index("tm")
    x_place = (time_place // 2) % 4
    for d, ref in enumerate((new0, new1, new2, new3)):
        parts[(x_place + 4 - d) % 4] = ref[...]
    lane = lax.broadcasted_iota(jnp.int32, (3 * C_ROWS, 128), 1)
    halves = [jnp.where(lane < 64, turn(parts[b], -32, 1), turn(parts[b + 1], 32, 1)) for b in (0, 2)]
    delta = jnp.concatenate(halves, axis=1) - old[...]
    delta = jnp.where(time_place == 0, 0.0, delta)
    copies = jnp.where(
        lax.broadcasted_iota(jnp.int32, (C_COLS, COLS), 0)
        == lax.broadcasted_iota(jnp.int32, (C_COLS, COLS), 1) // COARSENING,
        1.0,
        0.0,
    ).astype(BF16)
    scale = jnp.where(
        lax.broadcasted_iota(jnp.int32, (3 * C_ROWS, C_COLS), 0) < C_ROWS, 1.0 / SCALE, 1.0 / FLOW_SCALE
    )
    spread[...] = split_dot(scale * delta, copies, 2)
    low = lax.broadcasted_iota(jnp.int32, (8, COLS), 0) < 4
    for field in range(3):
        for k in range(ROWS // 8):
            row = C_ROWS * field + 2 * k
            add = jnp.where(low, spread[row : row + 1, :], spread[row + 1 : row + 2, :])
            rows = slice(8 * k, 8 * k + 8)
            if field == 0:
                depth_out[0, rows, :] = depth[0, rows, :] + add
            else:
                flux_out[0, field - 1, rows, :] = flux[0, field - 1, rows, :] + add


def finish(depth, flux, old, news):
    vmem = pl.BlockSpec(memory_space=pltpu.VMEM)
    return pl.pallas_call(
        finish_kernel,
        in_specs=[vmem] * 7,
        out_specs=[vmem] * 2,
        out_shape=(jax.ShapeDtypeStruct(depth.shape, F32), jax.ShapeDtypeStruct(flux.shape, F32)),
        scratch_shapes=[pltpu.VMEM((4, 3 * C_ROWS, 128), F32), pltpu.VMEM((3 * C_ROWS, COLS), F32)],
        compiler_params=pltpu.CompilerParams(vmem_limit_bytes=VMEM_LIMIT),
    )(depth, flux, old, *news)


def time_route(move):
    route = []
    for source in range(SLICES):
        z, x, core = move(source // 8, (source // 2) % 4, source % 2)
        route.append((source, (z % 2) * 8 + (x % 4) * 2 + core % 2))
    return route


def with_row(values, flip):
    return lax.ppermute(values, "sx", [(i, i ^ flip) for i in range(4)])


def over_x(values, distance):
    return lax.ppermute(values, "tm", time_route(lambda z, x, core: (z, x + distance, core)))


def on_device(
    depth_start, flux_start, elevation, roughness_class, building, manning, radar_rates, tile_index
):
    fields = (depth_start, flux_start, elevation, roughness_class, building)
    first, second, row_a, row_b = pack(*fields)
    first = lax.ppermute(first, "sy", [(0, 1), (1, 0), (2, 3), (3, 2)])
    second = lax.ppermute(second, "sy", [(1, 2), (2, 1)])
    row_a, row_b = with_row(row_a, 1), with_row(row_b, 3)
    size = 6 * HALO
    tops = jnp.concatenate([first[:size], second[:size]], axis=0)
    bottoms = jnp.concatenate([first[size : 2 * size], second[size : 2 * size]], axis=0)
    even_row = lax.axis_index("sx") % 2 == 0
    corner_a = with_row(jnp.where(even_row, bottoms, tops), 1)
    corner_b = with_row(jnp.where(even_row, tops, bottoms), 3)
    *arrays, rain, rates = ready(
        manning, radar_rates, *fields, tile_index, first, second, row_a, row_b
    )
    depth, flux, old, own, *away, ground = fine(manning, corner_a, corner_b, rain, rates, arrays)
    parts = [own] + [over_x(away[d - 1], d) for d in (1, 2, 3)]
    column = jnp.concatenate([part[:FIELDS] for part in parts] + [ground], axis=0)
    mine = jnp.concatenate([column] + [part[FIELDS:] for part in parts], axis=0)
    sibling = time_route(lambda z, x, core: (z, x, core + 1))
    arrays = [mine] + [with_row(column, flip) for flip in (1, 3, 2)]
    arrays = arrays + [lax.ppermute(part, "tm", sibling) for part in arrays]
    change, rain, ground, early, halfway = first_sweep(arrays)
    halfway = lax.ppermute(halfway, "tm", time_route(lambda z, x, core: (z + 1, x, core)))
    news = second_sweep(change, rain, ground, early, halfway)
    news = [news[0]] + [over_x(news[d], d) for d in (1, 2, 3)]
    return finish(depth, flux, old, news)


def solution(mesh):
    placed = (
        P("tm", "sx", "sy"),
        P("tm", None, "sx", "sy"),
        P("sx", "sy"),
        P("sx", "sy"),
        P("sx", "sy"),
        P(),
        P(),
        P("tm", None, None, None),
    )
    return jax.shard_map(
        on_device,
        mesh=mesh,
        in_specs=placed,
        out_specs=(P("tm", "sx", "sy"), P("tm", None, "sx", "sy")),
        check_vma=False,
    )
```
